512 devices in a mesh: row: 32 (over x, y), col: 16 (over z, core).
Axes of the slice: x: 4, y: 8, z: 8, core: 2. Of those that a mesh axis runs over, the one named last changes fastest.
Arguments:
- matrix: float32 [16384, 16384], P('row', 'col'), may hold values from -16 to 16, as said below
Outputs:
- banded: float32 [16384, 16384], P('row', 'col')
- reflectors: float32 [2, 16384, 64], P(None, 'row')
- tfactors: float32 [2, 64, 64], replicated
The draws below stay inside these ranges and needn't reach their ends.
Inputs may be any that keep to these rules, and one draw needn't show every extreme that they name: matrix is exactly symmetric.
All inputs are finite; a program needn't handle non-finite values.
Results may differ from the reference program's by a relative error of at most 0.0003.
Values sent between devices are 32-bit elements; how exact they have to be, the bound alone decides.
No kernel may reach another device: no remote copies, remote signals or barrier semaphores. Data moves between devices by JAX's collectives and lax.ppermute only.
A program may use at most 64 MiB of HBM per device.

```python
import math
import jax
import jax.numpy as jnp
from jax import lax

M = 16384
NB = 64
PANELS = 2


def draw_matrix(key, part):
    key = jax.random.fold_in(key, 11)
    noise_key, scale_key = jax.random.split(key, 2)
    noise_field = jnp.clip(jax.random.normal(noise_key, (M, M), jnp.float32), -6.0, 6.0)
    scale_vector = jnp.exp(jax.random.uniform(scale_key, (M,), jnp.float32, math.log(0.4), math.log(4.0)))
    symmetric = 0.5 * (noise_field + noise_field.T)
    return symmetric * (scale_vector[:, None] * scale_vector[None, :]) * 0.0625


def setup_inputs(seed: int = 0) -> dict:
    streams_of = jax.random.split(jax.random.key(seed), 2)
    matrix = draw_matrix(jax.random.fold_in(streams_of[1], 71), 0)
    return dict(matrix=matrix)


precise = lax.Precision.HIGHEST

def product(left_arr, right_arr):
    return jnp.dot(left_arr, right_arr, precision=precise, preferred_element_type=jnp.float32)

def householder(panel_block, start_row):
    places = jnp.arange(panel_block.shape[0])
    slot_index = jnp.arange(NB)
    reduced = panel_block
    vectors = jnp.zeros_like(panel_block)
    factor = jnp.zeros((NB, NB), panel_block.dtype)
    for column in range(NB):
        pivot_row = start_row + column
        below_part = jnp.where(places >= pivot_row, reduced[:, column], 0.0)
        head_value = reduced[pivot_row, column]
        length = jnp.sqrt(jnp.sum(below_part * below_part))
        new_head = -jnp.where(head_value >= 0, 1.0, -1.0) * length
        scaling = (new_head - head_value) / new_head
        vector = jnp.where(places == pivot_row, 1.0, below_part / (head_value - new_head))
        vectors = vectors.at[:, column].set(vector)
        weights = product(vector, reduced)
        reduced = reduced - scaling * vector[:, None] * weights[None, :]
        correlation = jnp.where(slot_index < column, product(vector, vectors), 0.0)
        new_col = jnp.where(slot_index < column, -scaling * product(factor, correlation), 0.0)
        new_col = jnp.where(slot_index == column, scaling, new_col)
        factor = factor.at[:, column].set(new_col)
    return (vectors, factor)

def reference(matrix):
    current = matrix
    vec_store = []
    fac_store = []
    for panel_index in range(PANELS):
        first_col = panel_index * NB
        start_row = first_col + NB
        vectors, factor = householder(current[:, first_col:first_col + NB], start_row)
        image_all = product(current, vectors)
        core_matrix = product(factor.T, product(product(vectors.T, image_all), factor))
        wide_part = product(image_all, factor) - 0.5 * product(vectors, core_matrix)
        left_cat = jnp.concatenate([vectors, wide_part], axis=1)
        right_cat = jnp.concatenate([wide_part, vectors], axis=1)
        current = current - lax.dot_general(left_cat, right_cat, (((1,), (1,)), ((), ())), precision=precise, preferred_element_type=jnp.float32)
        vec_store.append(vectors)
        fac_store.append(factor)
    return (current, jnp.stack(vec_store), jnp.stack(fac_store))
```

```python
import jax
import jax.numpy as jnp
from jax import lax
from jax.experimental import pallas as pl
from jax.experimental.pallas import tpu as pltpu
from jax.sharding import PartitionSpec as P

NB = 64
precise = lax.Precision.HIGHEST


def nn(a, b):
    return lax.dot_general(
        a, b, (((1,), (0,)), ((), ())), precision=precise, preferred_element_type=jnp.float32
    )


def tn(a, b):
    return lax.dot_general(
        a, b, (((0,), (0,)), ((), ())), precision=precise, preferred_element_type=jnp.float32
    )


def nt(a, b):
    return lax.dot_general(
        a, b, (((1,), (1,)), ((), ())), precision=precise, preferred_element_type=jnp.float32
    )


def places():
    sub = lax.broadcasted_iota(jnp.int32, (NB, 2 * NB), 0)
    lane = lax.broadcasted_iota(jnp.int32, (NB, 2 * NB), 1)
    return sub, lane


def inverse_root(gram):
    sub, lane = places()
    eye = (sub + NB == lane).astype(jnp.float32)
    work = jnp.concatenate([gram, jnp.zeros_like(gram)], axis=1) + eye
    scales = jnp.zeros((NB, 2 * NB), jnp.float32)
    for step in range(NB):
        row = work[step : step + 1, :]
        pivot = row[:, step : step + 1]
        scales = jnp.where(sub == step, pivot, scales)
        if step + 1 < NB:
            scaled = row * (1.0 / pivot)
            column = jnp.where(sub > step, work[:, step : step + 1], 0.0)
            work = work - column * scaled
    return (work * lax.rsqrt(scales))[:, NB:]


def signed_lu(negated_top):
    sub, lane = places()
    eye = (sub + NB == lane).astype(jnp.float32)
    work = jnp.concatenate([negated_top, jnp.zeros_like(negated_top)], axis=1) + eye
    lower = jnp.zeros((NB, 2 * NB), jnp.float32)
    upper = jnp.zeros((NB, 2 * NB), jnp.float32)
    signs = jnp.zeros((1, 2 * NB), jnp.float32)
    lane_row = lax.broadcasted_iota(jnp.int32, (1, 2 * NB), 1)
    for step in range(NB):
        row = work[step : step + 1, :]
        raw = row[:, step : step + 1]
        flip = jnp.where(raw > 0, 1.0, -1.0)
        signs = jnp.where(lane_row == step, flip, signs)
        pivot = raw + flip
        inverse = 1.0 / pivot
        row = jnp.where(lane_row == step, pivot, row)
        upper = jnp.where((sub == step) & (lane >= step), row, upper)
        column = work[:, step : step + 1]
        lower = jnp.where(
            lane == step, jnp.where(sub > step, column * inverse, jnp.where(sub == step, 1.0, 0.0)), lower
        )
        scaled = row * inverse
        work = jnp.where(sub == step, scaled, work - column * scaled)
    return lower[:, :NB], upper[:, :NB], work[:, NB:], signs[:, :NB]


def root_kernel(gram_ref, out_ref):
    out_ref[...] = inverse_root(gram_ref[...])


def panel_kernel(
    first_ref, second_gram_ref, raw_inner_ref, top_ref, next_top_ref, image_top_ref,
    pick_ref, coef_ref, factor_ref, pick_t_ref, coef_t_ref, half_ref, lower_ref, wide_top_ref,
):
    second = inverse_root(second_gram_ref[...])
    root = nn(second, first_ref[...])
    negated_top = -nt(top_ref[...], root)
    lower, upper, inverse, signs = signed_lu(negated_top)
    sub = lax.broadcasted_iota(jnp.int32, (NB, NB), 0)
    lane = lax.broadcasted_iota(jnp.int32, (NB, NB), 1)
    triangle = lane >= sub
    upper_inverse = jnp.where(triangle, nn(inverse, lower), 0.0)
    lower_inverse = nn(upper, inverse)
    factor = jnp.where(triangle, nt(upper * signs, lower_inverse), 0.0)
    sign_square = jnp.where(sub == lane, signs, 0.0)
    pick = nn(sign_square, upper_inverse)
    coef = tn(root, upper_inverse)
    next_top = next_top_ref[...]
    image_top = image_top_ref[...]
    cross = tn(pick, nn(image_top, coef))
    crossed = tn(nn(image_top, coef), pick)
    inner = (
        tn(pick, nn(next_top, pick)) - cross - crossed + tn(coef, nn(raw_inner_ref[...], coef))
    )
    core = tn(factor, nn(inner, factor))
    pick_t = nn(pick, factor)
    coef_t = nn(coef, factor)
    half = 0.5 * core
    pick_ref[...] = pick
    coef_ref[...] = coef
    factor_ref[...] = factor
    pick_t_ref[...] = pick_t
    coef_t_ref[...] = coef_t
    half_ref[...] = half
    lower_ref[...] = lower
    wide_top_ref[...] = nn(next_top, pick_t) - nn(image_top, coef_t) - nn(lower, half)


square = jax.ShapeDtypeStruct((NB, NB), jnp.float32)


def root_of(gram):
    return pl.pallas_call(root_kernel, out_shape=square, name="root")(gram)


def panel_of(*smalls):
    return pl.pallas_call(panel_kernel, out_shape=[square] * 8, name="panel")(*smalls)


def fold(x):
    half = x.shape[1] // 2
    return jnp.concatenate([x[:, :half], x[:, half:]], axis=2)


def unfold(x):
    return jnp.concatenate([x[:, :, :NB], x[:, :, NB:]], axis=1)


def swap(x, axis):
    return lax.all_to_all(x, axis, 0, 0)


def spread(x, axis, size):
    return swap(jnp.broadcast_to(x[None], (size,) + x.shape), axis)


def tall(x):
    return unfold(x).reshape(-1, NB)


def solution(mesh):
    nr = mesh.shape["row"]
    nc = mesh.shape["col"]

    def local(matrix):
        rows_here, cols_here = matrix.shape
        chunk = rows_here // nc
        half = chunk // 2
        my_row = lax.axis_index("row")
        my_col = lax.axis_index("col")
        row_place = (my_row * rows_here + jnp.arange(rows_here))[:, None]
        col_place = (my_col * cols_here + jnp.arange(cols_here))[:, None]
        to_rows = []
        for r in range(nr):
            for c in range(nc):
                first = r * rows_here + c * chunk
                source = (first % cols_here // chunk) * nc + first // cols_here
                to_rows.append((source, r * nc + c))
        to_cols = [(b, a) for a, b in to_rows]

        def pack_small(parts, size):
            flat = jnp.concatenate(parts, axis=1).reshape(size, -1, 2 * NB)
            return flat

        def unpack_small(x, count):
            wide = x.reshape(NB, count * NB)
            return [wide[:, k * NB : (k + 1) * NB] for k in range(count)]

        raw = matrix[:, : 3 * NB].reshape(nc, chunk, 3 * NB)
        raw = jnp.concatenate([raw[:, :, : 2 * NB], fold(raw[:, :, 2 * NB :])], axis=1)
        raw_chunk = swap(raw, "col")[0]
        raw_chunk_c = lax.ppermute(raw_chunk, ("row", "col"), to_cols)
        raw_row = spread(raw_chunk, "col", nc)

        def raw_parts(x):
            pair = x[:, :chunk].reshape(-1, 2 * NB)
            return pair[:, :NB], pair[:, NB:], tall(x[:, chunk:])

        first_r, next_r, last_r = raw_parts(raw_row)

        def in_row_zero(x):
            return jnp.where(my_row == 0, x, 0.0)

        panel_r = jnp.where(row_place >= NB, first_r, 0.0)
        partial_image = fold(tn(matrix, panel_r).reshape(nr, chunk, NB))
        smalls = pack_small(
            [
                tn(panel_r, panel_r),
                tn(next_r, panel_r),
                in_row_zero(first_r[NB : 2 * NB]),
                in_row_zero(next_r[NB : 2 * NB]),
                in_row_zero(last_r[2 * NB : 3 * NB]),
                jnp.zeros((NB, NB), jnp.float32),
            ],
            nr,
        )
        summed = jnp.sum(swap(jnp.concatenate([partial_image, smalls], axis=1), "row"), axis=0)
        image_chunk = summed[:half]
        image_chunk_r = lax.ppermute(image_chunk, ("row", "col"), to_rows)
        gathered = spread(jnp.concatenate([summed, raw_chunk_c], axis=0), "row", nr)
        few = summed.shape[0]
        image_c = tall(gathered[:, :half])
        gram, image_top, top, next_top, last_top, _ = unpack_small(gathered[:, half:few], 6)
        first_c, next_c, last_c = raw_parts(gathered[:, few:])
        panel_c = jnp.where(col_place >= NB, first_c, 0.0)
        root = root_of(gram)
        once_c = nt(panel_c, root)
        both = jnp.concatenate([tn(once_c, once_c), tn(panel_c, image_c)], axis=1)
        got = spread(jnp.concatenate([both, image_chunk_r], axis=0), "col", nc)
        both = jnp.sum(got[:, :NB], axis=0)
        image_r = tall(got[:, NB:])
        pick, coef, factor_one, pick_t, coef_t, half_core, lower, wide_top = panel_of(
            root, both[:, :NB], both[:, NB:], top, next_top, image_top
        )

        def panel_vectors(place, start, panel, following, image):
            here = place - start
            inside = (here >= 0) & (here < NB)
            offset = start % rows_here
            placed = jnp.pad(pick, ((offset, place.shape[0] - offset - NB), (0, 0)))
            vectors = jnp.where(inside, placed, 0.0) - nn(panel, coef)
            wide = nn(following, pick_t) - nn(image, coef_t) - nn(vectors, half_core)
            return vectors, wide

        vec_one_r, wide_one_r = panel_vectors(row_place, NB, panel_r, next_r, image_r)
        vec_one_c, wide_one_c = panel_vectors(col_place, NB, panel_c, next_c, image_c)

        def second_panel(place, following, vectors, wide):
            changed = following - nt(vectors, wide_top) - nt(wide, lower)
            return jnp.where(place >= 2 * NB, changed, 0.0)

        panel_r = second_panel(row_place, next_r, vec_one_r, wide_one_r)
        panel_c = second_panel(col_place, next_c, vec_one_c, wide_one_c)
        partial_image = fold(tn(matrix, panel_r).reshape(nr, chunk, NB))
        place = slice(2 * NB, 3 * NB)
        smalls = pack_small(
            [
                tn(panel_r, panel_r),
                tn(last_r, panel_r),
                tn(vec_one_r, panel_r),
                tn(wide_one_r, panel_r),
                in_row_zero(panel_r[place]),
                in_row_zero(vec_one_r[place]),
                in_row_zero(wide_one_r[place]),
                jnp.zeros((NB, NB), jnp.float32),
            ],
            nr,
        )
        summed = jnp.sum(swap(jnp.concatenate([partial_image, smalls], axis=1), "row"), axis=0)
        image_chunk = summed[:half]
        image_chunk_r = lax.ppermute(image_chunk, ("row", "col"), to_rows)
        gathered = spread(summed, "row", nr)
        image_c = tall(gathered[:, :half])
        gram, image_top, vec_dot, wide_dot, top, vec_top, wide_top, _ = unpack_small(
            gathered[:, half:], 8
        )
        root = root_of(gram)
        once_c = nt(panel_c, root)
        both = jnp.concatenate([tn(once_c, once_c), tn(panel_c, image_c)], axis=1)
        got = spread(jnp.concatenate([both, image_chunk_r], axis=0), "col", nc)
        both = jnp.sum(got[:, :NB], axis=0)
        image_r = tall(got[:, NB:])
        crossed = tn(vec_dot, wide_dot)
        raw_inner = both[:, NB:] - crossed - crossed.T
        image_top = image_top - nn(vec_top, wide_dot) - nn(wide_top, vec_dot)
        crossed = nt(vec_top, wide_top)
        next_top = last_top - crossed - crossed.T
        pick, coef, factor_two, pick_t, coef_t, half_core, lower, _ = panel_of(
            root, both[:, :NB], raw_inner, top, next_top, image_top
        )

        def later(panel, vectors, wide, last, image, place):
            last = last - nt(vectors, wide_top) - nt(wide, vec_top)
            image = image - nn(vectors, wide_dot) - nn(wide, vec_dot)
            return panel_vectors(place, 2 * NB, panel, last, image)

        vec_two_r, wide_two_r = later(panel_r, vec_one_r, wide_one_r, last_r, image_r, row_place)
        vec_two_c, wide_two_c = later(panel_c, vec_one_c, wide_one_c, last_c, image_c, col_place)
        left = jnp.concatenate([vec_one_r, wide_one_r, vec_two_r, wide_two_r], axis=1)
        right = jnp.concatenate([wide_one_c, vec_one_c, wide_two_c, vec_two_c], axis=1)
        banded = matrix - nt(left, right)
        return banded, jnp.stack([vec_one_r, vec_two_r]), jnp.stack([factor_one, factor_two])

    return jax.shard_map(
        local,
        mesh=mesh,
        in_specs=(P("row", "col"),),
        out_specs=(P("row", "col"), P(None, "row", None), P()),
        check_vma=False,
    )
```

```python
import jax
import jax.numpy as jnp
from jax import lax
from jax.experimental import pallas as pl
from jax.experimental.pallas import tpu as pltpu
from jax.sharding import PartitionSpec as P

NB = 64
precise = lax.Precision.HIGHEST


def nn(a, b):
    return lax.dot_general(
        a, b, (((1,), (0,)), ((), ())), precision=precise, preferred_element_type=jnp.float32
    )


def tn(a, b):
    return lax.dot_general(
        a, b, (((0,), (0,)), ((), ())), precision=precise, preferred_element_type=jnp.float32
    )


def nt(a, b):
    return lax.dot_general(
        a, b, (((1,), (1,)), ((), ())), precision=precise, preferred_element_type=jnp.float32
    )


def places():
    sub = lax.broadcasted_iota(jnp.int32, (NB, 2 * NB), 0)
    lane = lax.broadcasted_iota(jnp.int32, (NB, 2 * NB), 1)
    return sub, lane


def inverse_root(gram):
    sub, lane = places()
    eye = (sub + NB == lane).astype(jnp.float32)
    work = jnp.concatenate([gram, jnp.zeros_like(gram)], axis=1) + eye
    scales = jnp.zeros((NB, 2 * NB), jnp.float32)
    for step in range(NB):
        row = work[step : step + 1, :]
        pivot = row[:, step : step + 1]
        scales = jnp.where(sub == step, pivot, scales)
        if step + 1 < NB:
            scaled = row * (1.0 / pivot)
            column = jnp.where(sub > step, work[:, step : step + 1], 0.0)
            work = work - column * scaled
    return (work * lax.rsqrt(scales))[:, NB:]


def signed_lu(negated_top):
    sub, lane = places()
    eye = (sub + NB == lane).astype(jnp.float32)
    work = jnp.concatenate([negated_top, jnp.zeros_like(negated_top)], axis=1) + eye
    lower = jnp.zeros((NB, 2 * NB), jnp.float32)
    upper = jnp.zeros((NB, 2 * NB), jnp.float32)
    signs = jnp.zeros((1, 2 * NB), jnp.float32)
    lane_row = lax.broadcasted_iota(jnp.int32, (1, 2 * NB), 1)
    for step in range(NB):
        row = work[step : step + 1, :]
        raw = row[:, step : step + 1]
        flip = jnp.where(raw > 0, 1.0, -1.0)
        signs = jnp.where(lane_row == step, flip, signs)
        pivot = raw + flip
        inverse = 1.0 / pivot
        row = jnp.where(lane_row == step, pivot, row)
        upper = jnp.where((sub == step) & (lane >= step), row, upper)
        column = work[:, step : step + 1]
        lower = jnp.where(
            lane == step, jnp.where(sub > step, column * inverse, jnp.where(sub == step, 1.0, 0.0)), lower
        )
        scaled = row * inverse
        work = jnp.where(sub == step, scaled, work - column * scaled)
    return lower[:, :NB], upper[:, :NB], work[:, NB:], signs[:, :NB]


def near_root(gram):
    sub = lax.broadcasted_iota(jnp.int32, (NB, NB), 0)
    lane = lax.broadcasted_iota(jnp.int32, (NB, NB), 1)
    eye = (sub == lane).astype(jnp.float32)
    off = gram - eye
    first_order = eye - jnp.where(sub > lane, off, jnp.where(sub == lane, 0.5 * off, 0.0))
    close = jnp.sum(off * off) < 2e-8
    return lax.cond(close, lambda: first_order, lambda: inverse_root(gram))


def root_kernel(gram_ref, out_ref):
    out_ref[...] = inverse_root(gram_ref[...])


def panel_kernel(
    second_gram_ref, raw_inner_ref, top_ref, next_top_ref, image_top_ref,
    pick_ref, coef_ref, factor_ref, pick_t_ref, coef_t_ref, half_ref, lower_ref, wide_top_ref,
):
    root = near_root(second_gram_ref[...])
    negated_top = -nt(top_ref[...], root)
    lower, upper, inverse, signs = signed_lu(negated_top)
    sub = lax.broadcasted_iota(jnp.int32, (NB, NB), 0)
    lane = lax.broadcasted_iota(jnp.int32, (NB, NB), 1)
    triangle = lane >= sub
    upper_inverse = jnp.where(triangle, nn(inverse, lower), 0.0)
    lower_inverse = nn(upper, inverse)
    factor = jnp.where(triangle, nt(upper * signs, lower_inverse), 0.0)
    sign_square = jnp.where(sub == lane, signs, 0.0)
    pick = nn(sign_square, upper_inverse)
    coef = tn(root, upper_inverse)
    next_top = next_top_ref[...]
    image_top = image_top_ref[...]
    cross = tn(pick, nn(image_top, coef))
    crossed = tn(nn(image_top, coef), pick)
    inner = (
        tn(pick, nn(next_top, pick)) - cross - crossed + tn(coef, nn(raw_inner_ref[...], coef))
    )
    core = tn(factor, nn(inner, factor))
    pick_t = nn(pick, factor)
    coef_t = nn(coef, factor)
    half = 0.5 * core
    pick_ref[...] = pick
    coef_ref[...] = coef
    factor_ref[...] = factor
    pick_t_ref[...] = pick_t
    coef_t_ref[...] = coef_t
    half_ref[...] = half
    lower_ref[...] = lower
    wide_top_ref[...] = nn(next_top, pick_t) - nn(image_top, coef_t) - nn(lower, half)


square = jax.ShapeDtypeStruct((NB, NB), jnp.float32)


def root_of(gram):
    return pl.pallas_call(root_kernel, out_shape=square, name="root")(gram)


def panel_of(*smalls):
    return pl.pallas_call(panel_kernel, out_shape=[square] * 8, name="panel")(*smalls)


def fold(x):
    half = x.shape[1] // 2
    return jnp.concatenate([x[:, :half], x[:, half:]], axis=2)


def unfold(x):
    return jnp.concatenate([x[:, :, :NB], x[:, :, NB:]], axis=1)


def swap(x, axis):
    return lax.all_to_all(x, axis, 0, 0)


def spread(x, axis, size):
    return swap(jnp.broadcast_to(x[None], (size,) + x.shape), axis)


def tall(x):
    return unfold(x).reshape(-1, NB)


def solution(mesh):
    nr = mesh.shape["row"]
    nc = mesh.shape["col"]

    def local(matrix):
        rows_here, cols_here = matrix.shape
        chunk = rows_here // nc
        half = chunk // 2
        my_row = lax.axis_index("row")
        my_col = lax.axis_index("col")
        row_place = (my_row * rows_here + jnp.arange(rows_here))[:, None]
        col_place = (my_col * cols_here + jnp.arange(cols_here))[:, None]
        to_rows = []
        for r in range(nr):
            for c in range(nc):
                first = r * rows_here + c * chunk
                source = (first % cols_here // chunk) * nc + first // cols_here
                to_rows.append((source, r * nc + c))
        to_cols = [(b, a) for a, b in to_rows]

        def pack_small(parts, size):
            flat = jnp.concatenate(parts, axis=1).reshape(size, -1, 2 * NB)
            return flat

        def unpack_small(x, count):
            wide = x.reshape(NB, count * NB)
            return [wide[:, k * NB : (k + 1) * NB] for k in range(count)]

        raw = matrix[:, : 3 * NB].reshape(nc, chunk, 3 * NB)
        raw = jnp.concatenate([raw[:, :, : 2 * NB], fold(raw[:, :, 2 * NB :])], axis=1)
        raw_chunk = swap(raw, "col")[0]
        raw_chunk_c = lax.ppermute(raw_chunk, ("row", "col"), to_cols)
        raw_row = spread(raw_chunk, "col", nc)

        def raw_parts(x):
            pair = x[:, :chunk].reshape(-1, 2 * NB)
            return pair[:, :NB], pair[:, NB:], tall(x[:, chunk:])

        first_r, next_r, last_r = raw_parts(raw_row)

        def in_row_zero(x):
            return jnp.where(my_row == 0, x, 0.0)

        def total(x, axis, size):
            return unfold(jnp.sum(spread(fold(x[None])[0], axis, size), axis=0)[None])[0]

        panel_r = jnp.where(row_place >= NB, first_r, 0.0)
        root = root_of(total(tn(panel_r, panel_r), "row", nr))
        once_r = nt(panel_r, root)
        partial_image = fold(tn(matrix, once_r).reshape(nr, chunk, NB))
        smalls = pack_small(
            [
                tn(once_r, once_r),
                tn(next_r, once_r),
                in_row_zero(once_r[NB : 2 * NB]),
                in_row_zero(next_r[NB : 2 * NB]),
                in_row_zero(last_r[2 * NB : 3 * NB]),
                jnp.zeros((NB, NB), jnp.float32),
            ],
            nr,
        )
        summed = jnp.sum(swap(jnp.concatenate([partial_image, smalls], axis=1), "row"), axis=0)
        image_chunk = summed[:half]
        image_chunk_r = lax.ppermute(image_chunk, ("row", "col"), to_rows)
        gathered = spread(jnp.concatenate([summed, raw_chunk_c], axis=0), "row", nr)
        few = summed.shape[0]
        image_c = tall(gathered[:, :half])
        gram, image_top, top, next_top, last_top, _ = unpack_small(gathered[:, half:few], 6)
        first_c, next_c, last_c = raw_parts(gathered[:, few:])
        once_c = nt(jnp.where(col_place >= NB, first_c, 0.0), root)
        inner = fold(tn(once_c, image_c)[None])[0]
        got = spread(jnp.concatenate([inner, image_chunk_r], axis=0), "col", nc)
        inner = unfold(jnp.sum(got[:, : NB // 2], axis=0)[None])[0]
        image_r = tall(got[:, NB // 2 :])
        pick, coef, factor_one, pick_t, coef_t, half_core, lower, wide_top = panel_of(
            gram, inner, top, next_top, image_top
        )

        def panel_vectors(place, start, panel, following, image):
            here = place - start
            inside = (here >= 0) & (here < NB)
            offset = start % rows_here
            placed = jnp.pad(pick, ((offset, place.shape[0] - offset - NB), (0, 0)))
            vectors = jnp.where(inside, placed, 0.0) - nn(panel, coef)
            wide = nn(following, pick_t) - nn(image, coef_t) - nn(vectors, half_core)
            return vectors, wide

        vec_one_r, wide_one_r = panel_vectors(row_place, NB, once_r, next_r, image_r)
        vec_one_c, wide_one_c = panel_vectors(col_place, NB, once_c, next_c, image_c)

        def second_panel(place, following, vectors, wide):
            changed = following - nt(vectors, wide_top) - nt(wide, lower)
            return jnp.where(place >= 2 * NB, changed, 0.0)

        panel_c = second_panel(col_place, next_c, vec_one_c, wide_one_c)
        panel_r = second_panel(row_place, next_r, vec_one_r, wide_one_r)
        root = root_of(total(tn(panel_c, panel_c), "col", nc))
        once_r = nt(panel_r, root)
        once_c = nt(panel_c, root)
        partial_image = fold(tn(matrix, once_r).reshape(nr, chunk, NB))
        place = slice(2 * NB, 3 * NB)
        smalls = pack_small(
            [
                tn(once_r, once_r),
                tn(last_r, once_r),
                tn(vec_one_r, once_r),
                tn(wide_one_r, once_r),
                in_row_zero(once_r[place]),
                in_row_zero(vec_one_r[place]),
                in_row_zero(wide_one_r[place]),
                jnp.zeros((NB, NB), jnp.float32),
            ],
            nr,
        )
        summed = jnp.sum(swap(jnp.concatenate([partial_image, smalls], axis=1), "row"), axis=0)
        image_chunk = summed[:half]
        image_chunk_r = lax.ppermute(image_chunk, ("row", "col"), to_rows)
        gathered = spread(summed, "row", nr)
        image_c = tall(gathered[:, :half])
        gram, image_top, vec_dot, wide_dot, top, vec_top, wide_top, _ = unpack_small(
            gathered[:, half:], 8
        )
        inner = fold(tn(once_c, image_c)[None])[0]
        got = spread(jnp.concatenate([inner, image_chunk_r], axis=0), "col", nc)
        inner = unfold(jnp.sum(got[:, : NB // 2], axis=0)[None])[0]
        image_r = tall(got[:, NB // 2 :])
        crossed = tn(vec_dot, wide_dot)
        inner = inner - crossed - crossed.T
        image_top = image_top - nn(vec_top, wide_dot) - nn(wide_top, vec_dot)
        crossed = nt(vec_top, wide_top)
        next_top = last_top - crossed - crossed.T
        pick, coef, factor_two, pick_t, coef_t, half_core, lower, _ = panel_of(
            gram, inner, top, next_top, image_top
        )

        def later(panel, vectors, wide, last, image, place):
            last = last - nt(vectors, wide_top) - nt(wide, vec_top)
            image = image - nn(vectors, wide_dot) - nn(wide, vec_dot)
            return panel_vectors(place, 2 * NB, panel, last, image)

        vec_two_r, wide_two_r = later(once_r, vec_one_r, wide_one_r, last_r, image_r, row_place)
        vec_two_c, wide_two_c = later(once_c, vec_one_c, wide_one_c, last_c, image_c, col_place)
        left = jnp.concatenate([vec_one_r, wide_one_r, vec_two_r, wide_two_r], axis=1)
        right = jnp.concatenate([wide_one_c, vec_one_c, wide_two_c, vec_two_c], axis=1)
        banded = matrix - nt(left, right)
        return banded, jnp.stack([vec_one_r, vec_two_r]), jnp.stack([factor_one, factor_two])

    return jax.shard_map(
        local,
        mesh=mesh,
        in_specs=(P("row", "col"),),
        out_specs=(P("row", "col"), P(None, "row", None), P()),
        check_vma=False,
    )
```

```python
import functools

import jax
import jax.numpy as jnp
from jax import lax
from jax.experimental import pallas as pl
from jax.experimental.pallas import tpu as pltpu
from jax.sharding import PartitionSpec as P

NB = 64
precise = lax.Precision.HIGHEST


def nn(a, b):
    return lax.dot_general(
        a, b, (((1,), (0,)), ((), ())), precision=precise, preferred_element_type=jnp.float32
    )


def tn(a, b):
    return lax.dot_general(
        a, b, (((0,), (0,)), ((), ())), precision=precise, preferred_element_type=jnp.float32
    )


def nt(a, b):
    return lax.dot_general(
        a, b, (((1,), (1,)), ((), ())), precision=precise, preferred_element_type=jnp.float32
    )


def places():
    sub = lax.broadcasted_iota(jnp.int32, (NB, 2 * NB), 0)
    lane = lax.broadcasted_iota(jnp.int32, (NB, 2 * NB), 1)
    return sub, lane


def inverse_root(gram):
    sub, lane = places()
    eye = (sub + NB == lane).astype(jnp.float32)
    work = jnp.concatenate([gram, jnp.zeros_like(gram)], axis=1) + eye
    scales = jnp.zeros((NB, 2 * NB), jnp.float32)
    for step in range(NB):
        row = work[step : step + 1, :]
        pivot = row[:, step : step + 1]
        scales = jnp.where(sub == step, pivot, scales)
        if step + 1 < NB:
            scaled = row * (1.0 / pivot)
            column = jnp.where(sub > step, work[:, step : step + 1], 0.0)
            work = work - column * scaled
    return (work * lax.rsqrt(scales))[:, NB:]


def signed_lu(negated_top):
    sub, lane = places()
    eye = (sub + NB == lane).astype(jnp.float32)
    work = jnp.concatenate([negated_top, jnp.zeros_like(negated_top)], axis=1) + eye
    lower = jnp.zeros((NB, 2 * NB), jnp.float32)
    upper = jnp.zeros((NB, 2 * NB), jnp.float32)
    signs = jnp.zeros((1, 2 * NB), jnp.float32)
    lane_row = lax.broadcasted_iota(jnp.int32, (1, 2 * NB), 1)
    for step in range(NB):
        row = work[step : step + 1, :]
        raw = row[:, step : step + 1]
        flip = jnp.where(raw > 0, 1.0, -1.0)
        signs = jnp.where(lane_row == step, flip, signs)
        pivot = raw + flip
        inverse = 1.0 / pivot
        row = jnp.where(lane_row == step, pivot, row)
        upper = jnp.where((sub == step) & (lane >= step), row, upper)
        column = work[:, step : step + 1]
        lower = jnp.where(
            lane == step, jnp.where(sub > step, column * inverse, jnp.where(sub == step, 1.0, 0.0)), lower
        )
        scaled = row * inverse
        work = jnp.where(sub == step, scaled, work - column * scaled)
    return lower[:, :NB], upper[:, :NB], work[:, NB:], signs[:, :NB]


def near_root(gram):
    sub = lax.broadcasted_iota(jnp.int32, (NB, NB), 0)
    lane = lax.broadcasted_iota(jnp.int32, (NB, NB), 1)
    eye = (sub == lane).astype(jnp.float32)
    off = gram - eye
    first_order = eye - jnp.where(sub > lane, off, jnp.where(sub == lane, 0.5 * off, 0.0))
    close = jnp.sum(off * off) < 2e-8
    return lax.cond(close, lambda: first_order, lambda: inverse_root(gram))


def fold(x, chunk):
    x = x.reshape(-1, chunk, NB)
    return jnp.concatenate([x[:, : chunk // 2], x[:, chunk // 2 :]], axis=2)


def unfold(x):
    return jnp.concatenate([x[:, :, :NB], x[:, :, NB:]], axis=1).reshape(-1, NB)


def pack_symmetric(g):
    h = NB // 2
    rows = []
    for quadrant in (g[:h, :h], g[:h, h:], g[h:, h:]):
        rows.append(jnp.concatenate([quadrant[k : k + 8] for k in range(0, h, 8)], axis=1))
    return jnp.concatenate(rows, axis=0)


def unpack_symmetric(x):
    h = NB // 2
    first, cross, last = [
        jnp.concatenate([x[q : q + 8, k : k + h] for k in range(0, 4 * h, h)], axis=0)
        for q in (0, 8, 16)
    ]
    upper = jnp.concatenate([first, cross], axis=1)
    return jnp.concatenate([upper, jnp.concatenate([cross.T, last], axis=1)], axis=0)


PACKED = 24


def put_pairs(out_ref, pairs):
    peers, rows = out_ref.shape[:2]
    per = NB // peers
    for q, pair in enumerate(pairs):
        for t in range(per):
            out_ref[:, q * per + t, :] = pair[t * peers : (t + 1) * peers]
    for k in range(len(pairs) * per, rows):
        out_ref[:, k, :] = jnp.zeros((peers, 2 * NB), jnp.float32)


def get_pairs(ref, first, count):
    per = NB // ref.shape[0]
    pairs = []
    for q in range(count):
        slots = [ref[:, first + q * per + t, :] for t in range(per)]
        pair = jnp.concatenate(slots, axis=0)
        pairs += [pair[:, :NB], pair[:, NB:]]
    return pairs


def beside(*parts):
    return jnp.concatenate(parts, axis=1)


def below(x, index, start):
    place = lax.broadcasted_iota(jnp.int32, x.shape, 0)
    return jnp.where((place >= start) | (index > 0), x, 0.0)


def gram_kernel(chunk, index_ref, raw_ref, out_ref):
    pair = raw_ref[:, :chunk, :].reshape(-1, 2 * NB)
    panel = below(pair[:, :NB], index_ref[0], NB)
    packed = pack_symmetric(tn(panel, panel))
    out_ref[...] = jnp.broadcast_to(packed[None], out_ref.shape)


def first_once_kernel(chunk, index_ref, got_ref, raw_ref, root_ref, once_ref, small_ref):
    index = index_ref[0]
    root = inverse_root(unpack_symmetric(jnp.sum(got_ref[...], axis=0)))
    root_ref[...] = root
    pair = raw_ref[:, :chunk, :].reshape(-1, 2 * NB)
    following = pair[:, NB:]
    once = nt(below(pair[:, :NB], index, NB), root)
    once_ref[...] = once
    last = unfold(raw_ref[:, chunk:, :])
    gram = tn(once, once)
    image_top = tn(following, once)

    def top(x, k):
        return jnp.where(index == 0, x[k * NB : (k + 1) * NB], 0.0)

    put_pairs(
        small_ref,
        [
            beside(gram, image_top),
            beside(top(once, 1), top(following, 1)),
            beside(top(last, 2), jnp.zeros((NB, NB), jnp.float32)),
        ],
    )


def second_once_kernel(
    chunk, index_ref, got_ref, raw_ref, panel_ref, vec_ref, wide_ref, root_ref, once_ref, small_ref
):
    index = index_ref[0]
    root = inverse_root(unpack_symmetric(jnp.sum(got_ref[...], axis=0)))
    root_ref[...] = root
    once = nt(panel_ref[...], root)
    once_ref[...] = once
    last = unfold(raw_ref[:, chunk:, :])
    vec = vec_ref[...]
    wide = wide_ref[...]

    def top(x):
        return jnp.where(index == 0, x[2 * NB : 3 * NB], 0.0)

    put_pairs(
        small_ref,
        [
            beside(tn(once, once), tn(last, once)),
            beside(tn(vec, once), tn(wide, once)),
            beside(top(once), top(vec)),
            beside(top(wide), jnp.zeros((NB, NB), jnp.float32)),
        ],
    )


def sum_kernel(got_ref, out_ref, chunk_ref):
    summed = jnp.sum(got_ref[...], axis=0)
    out_ref[...] = jnp.broadcast_to(summed[None], out_ref.shape)
    chunk_ref[...] = summed[: chunk_ref.shape[0]]


def inner_kernel(gathered_ref, once_ref, chunk_ref, out_ref):
    half = chunk_ref.shape[0]
    inner = tn(once_ref[...], unfold(gathered_ref[:, :half, :]))
    block = jnp.concatenate([pack_symmetric(inner), chunk_ref[...]], axis=0)
    out_ref[...] = jnp.broadcast_to(block[None], out_ref.shape)


PICK, COEF, PICK_T, COEF_T, LOWER, FACTOR, INNER, WIDE = range(8)


def factor_small(gram, top, next_top, image_top, small_ref):
    root = near_root(gram)
    lower, upper, inverse, signs = signed_lu(-nt(top, root))
    sub = lax.broadcasted_iota(jnp.int32, (NB, NB), 0)
    lane = lax.broadcasted_iota(jnp.int32, (NB, NB), 1)
    triangle = lane >= sub
    upper_inverse = jnp.where(triangle, nn(inverse, lower), 0.0)
    lower_inverse = nn(upper, inverse)
    factor = jnp.where(triangle, nt(upper * signs, lower_inverse), 0.0)
    pick = nn(jnp.where(sub == lane, signs, 0.0), upper_inverse)
    coef = tn(root, upper_inverse)
    crossed = tn(pick, nn(image_top, coef))
    pick_t = nn(pick, factor)
    coef_t = nn(coef, factor)
    small_ref[PICK] = pick
    small_ref[COEF] = coef
    small_ref[PICK_T] = pick_t
    small_ref[COEF_T] = coef_t
    small_ref[LOWER] = lower
    small_ref[FACTOR] = factor
    small_ref[INNER] = tn(pick, nn(next_top, pick)) - crossed - crossed.T
    small_ref[WIDE] = nn(next_top, pick_t) - nn(image_top, coef_t)
    return pick, coef, pick_t, coef_t


def put_vectors(ref, once, index, start, pick, coef):
    ref[...] = -nn(once, coef)

    @pl.when(index == 0)
    def _():
        ref[start : start + NB, :] += pick


def half_core(small_ref, inner):
    coef = small_ref[COEF]
    factor = small_ref[FACTOR]
    inner = small_ref[INNER] + tn(coef, nn(inner, coef))
    return 0.5 * tn(factor, nn(inner, factor))


def first_factor_kernel(
    chunk, half, row_ref, col_ref, gathered_ref, raw_ref, once_c_ref, once_r_ref,
    small_ref, vec_c_ref, part_c_ref, vec_r_ref,
):
    gram, image_top, top, next_top, _, _ = get_pairs(gathered_ref, half, 3)
    pick, coef, pick_t, coef_t = factor_small(gram, top, next_top, image_top, small_ref)
    put_vectors(vec_c_ref, once_c_ref[...], col_ref[0], NB, pick, coef)
    put_vectors(vec_r_ref, once_r_ref[...], row_ref[0], NB, pick, coef)
    following = raw_ref[:, :chunk, :].reshape(-1, 2 * NB)[:, NB:]
    image = unfold(gathered_ref[:, :half, :])
    part_c_ref[...] = nn(following, pick_t) - nn(image, coef_t)


def second_panel(following, vec, wide, wide_top, lower, index):
    return below(following - nt(vec, wide_top) - nt(wide, lower), index, 2 * NB)


def first_cols_kernel(
    chunk, col_ref, got_ref, small_ref, vec_ref, part_ref, raw_ref,
    wide_ref, panel_ref, half_ref, wide_top_ref, out_ref,
):
    half = half_core(small_ref, unpack_symmetric(jnp.sum(got_ref[:, :PACKED, :], axis=0)))
    lower = small_ref[LOWER]
    wide_top = small_ref[WIDE] - nn(lower, half)
    half_ref[...] = half
    wide_top_ref[...] = wide_top
    vec = vec_ref[...]
    wide = part_ref[...] - nn(vec, half)
    wide_ref[...] = wide
    following = raw_ref[:, :chunk, :].reshape(-1, 2 * NB)[:, NB:]
    panel = second_panel(following, vec, wide, wide_top, lower, col_ref[0])
    panel_ref[...] = panel
    packed = pack_symmetric(tn(panel, panel))
    out_ref[...] = jnp.broadcast_to(packed[None], out_ref.shape)


def first_rows_kernel(
    chunk, row_ref, got_ref, small_ref, vec_ref, raw_ref, half_ref, wide_top_ref,
    wide_ref, panel_ref,
):
    image = unfold(got_ref[:, PACKED:, :])
    following = raw_ref[:, :chunk, :].reshape(-1, 2 * NB)[:, NB:]
    vec = vec_ref[...]
    wide = nn(following, small_ref[PICK_T]) - nn(image, small_ref[COEF_T]) - nn(vec, half_ref[...])
    wide_ref[...] = wide
    panel_ref[...] = second_panel(
        following, vec, wide, wide_top_ref[...], small_ref[LOWER], row_ref[0]
    )


def second_factor_kernel(
    chunk, half, row_ref, col_ref, gathered_ref, old_ref, raw_c_ref, raw_r_ref,
    once_c_ref, once_r_ref, vec_c_ref, wide_c_ref, vec_r_ref, wide_r_ref,
    small_ref, cross_ref, new_c_ref, part_c_ref, new_r_ref, part_r_ref,
):
    gram, image_top, vec_dot, wide_dot, top, vec_top, wide_top, _ = get_pairs(
        gathered_ref, half, 4
    )
    last_top = get_pairs(old_ref, half, 3)[4]
    crossed = tn(vec_dot, wide_dot)
    cross_ref[...] = crossed + crossed.T
    image_top = image_top - nn(vec_top, wide_dot) - nn(wide_top, vec_dot)
    crossed = nt(vec_top, wide_top)
    next_top = last_top - crossed - crossed.T
    pick, coef, pick_t, coef_t = factor_small(gram, top, next_top, image_top, small_ref)
    put_vectors(new_c_ref, once_c_ref[...], col_ref[0], 2 * NB, pick, coef)
    put_vectors(new_r_ref, once_r_ref[...], row_ref[0], 2 * NB, pick, coef)
    vec_dots = nn(wide_dot, coef_t) - tn(wide_top, pick_t)
    wide_dots = nn(vec_dot, coef_t) - tn(vec_top, pick_t)

    def part(raw_ref, vec, wide):
        last = unfold(raw_ref[:, chunk:, :])
        return nn(last, pick_t) + nn(vec, vec_dots) + nn(wide, wide_dots)

    image = unfold(gathered_ref[:, :half, :])
    part_c_ref[...] = part(raw_c_ref, vec_c_ref[...], wide_c_ref[...]) - nn(image, coef_t)
    part_r_ref[...] = part(raw_r_ref, vec_r_ref[...], wide_r_ref[...])


def last_kernel(
    got_ref, small_ref, cross_ref, vec_c_ref, wide_c_ref, vec_r_ref, wide_r_ref,
    new_c_ref, part_c_ref, new_r_ref, part_r_ref, left_ref, right_ref, vectors_ref,
):
    inner = unpack_symmetric(jnp.sum(got_ref[:, :PACKED, :], axis=0)) - cross_ref[...]
    half = half_core(small_ref, inner)
    new_c = new_c_ref[...]
    wide_c = part_c_ref[...] - nn(new_c, half)
    right_ref[...] = beside(wide_c_ref[...], vec_c_ref[...], wide_c, new_c)
    new_r = new_r_ref[...]
    image = unfold(got_ref[:, PACKED:, :])
    wide_r = part_r_ref[...] - nn(image, small_ref[COEF_T]) - nn(new_r, half)
    vec_r = vec_r_ref[...]
    left_ref[...] = beside(vec_r, wide_r_ref[...], new_r, wide_r)
    vectors_ref[0] = vec_r
    vectors_ref[1] = new_r


def call(kernel, name, outs, *args, statics=(), scalars=0, flops=1 << 24):
    in_smem = pl.BlockSpec(memory_space=pltpu.SMEM)
    in_vmem = pl.BlockSpec(memory_space=pltpu.VMEM)
    result = pl.pallas_call(
        functools.partial(kernel, *statics),
        out_shape=[jax.ShapeDtypeStruct(shape, jnp.float32) for shape in outs],
        in_specs=[in_smem if k < scalars else in_vmem for k in range(len(args))],
        out_specs=[in_vmem] * len(outs),
        compiler_params=pltpu.CompilerParams(vmem_limit_bytes=40 << 20),
        cost_estimate=pl.CostEstimate(flops=flops, bytes_accessed=1 << 22, transcendentals=0),
        name=name,
    )(*args)
    return result[0] if len(outs) == 1 else result


def swap(x, axis):
    return lax.all_to_all(x, axis, 0, 0)


def solution(mesh):
    nr = mesh.shape["row"]
    nc = mesh.shape["col"]

    def local(matrix):
        rows_here, cols_here = matrix.shape
        chunk = rows_here // nc
        half = chunk // 2
        few = -(-4 * (NB // nr) // 8) * 8
        my_row = lax.axis_index("row").astype(jnp.int32).reshape(1)
        my_col = lax.axis_index("col").astype(jnp.int32).reshape(1)
        to_rows = []
        for r in range(nr):
            for c in range(nc):
                first = r * rows_here + c * chunk
                source = (first % cols_here // chunk) * nc + first // cols_here
                to_rows.append((source, r * nc + c))
        to_cols = [(b, a) for a, b in to_rows]
        square = (NB, NB)
        tall_r = (rows_here, NB)
        tall_c = (cols_here, NB)

        raw = matrix[:, : 3 * NB].reshape(nc, chunk, 3 * NB)
        raw = jnp.concatenate(
            [raw[:, :, : 2 * NB], fold(matrix[:, 2 * NB : 3 * NB], chunk)], axis=1
        )
        raw_chunk = swap(raw, "col")[0]
        raw_chunk_c = lax.ppermute(raw_chunk, ("row", "col"), to_cols)
        raw_r = swap(jnp.broadcast_to(raw_chunk[None], raw.shape), "col")
        raw_c = lax.all_gather(raw_chunk_c, "row")

        grams = call(
            gram_kernel, "gram", [(nr, PACKED, 2 * NB)], my_row, raw_r, statics=(chunk,), scalars=1
        )
        root, once_r, smalls = call(
            first_once_kernel, "first_once", [square, tall_r, (nr, few, 2 * NB)],
            my_row, swap(grams, "row"), raw_r, statics=(chunk,), scalars=1,
        )

        def image_round(once_r, smalls):
            partial_image = fold(tn(matrix, once_r), chunk)
            got = swap(jnp.concatenate([partial_image, smalls], axis=1), "row")
            blocks, image_chunk = call(
                sum_kernel, "sum_blocks", [got.shape, (half, 2 * NB)], got
            )
            image_chunk_r = lax.ppermute(image_chunk, ("row", "col"), to_rows)
            return swap(blocks, "row"), image_chunk_r

        gathered, image_chunk_r = image_round(once_r, smalls)
        col_place = lax.axis_index("col") * cols_here + jnp.arange(cols_here)
        first_c = raw_c[:, :chunk].reshape(cols_here, 2 * NB)[:, :NB]
        once_c = nt(jnp.where(col_place[:, None] >= NB, first_c, 0.0), root)
        block = (nc, PACKED + half, 2 * NB)
        inners = call(inner_kernel, "inner", [block], gathered, once_c, image_chunk_r)
        got = swap(inners, "col")
        small_one, vec_c, part_c, vec_r = call(
            first_factor_kernel, "first_factor", [(8,) + square, tall_c, tall_c, tall_r],
            my_row, my_col, gathered, raw_c, once_c, once_r,
            statics=(chunk, half), scalars=2,
        )
        wide_c, panel_c, half_one, wide_top, grams = call(
            first_cols_kernel, "first_cols",
            [tall_c, tall_c, square, square, (nc, PACKED, 2 * NB)],
            my_col, got, small_one, vec_c, part_c, raw_c, statics=(chunk,), scalars=1,
        )
        grams = swap(grams, "col")
        wide_r, panel_r = call(
            first_rows_kernel, "first_rows", [tall_r, tall_r],
            my_row, got, small_one, vec_r, raw_r, half_one, wide_top, statics=(chunk,), scalars=1,
        )

        root, once_r, smalls = call(
            second_once_kernel, "second_once", [square, tall_r, (nr, few, 2 * NB)],
            my_row, grams, raw_r, panel_r, vec_r, wide_r, statics=(chunk,), scalars=1,
        )
        old = gathered
        gathered, image_chunk_r = image_round(once_r, smalls)
        once_c = nt(panel_c, root)
        inners = call(inner_kernel, "inner", [block], gathered, once_c, image_chunk_r)
        got = swap(inners, "col")
        small_two, cross, new_c, part_c, new_r, part_r = call(
            second_factor_kernel, "second_factor",
            [(8,) + square, square, tall_c, tall_c, tall_r, tall_r],
            my_row, my_col, gathered, old, raw_c, raw_r, once_c, once_r,
            vec_c, wide_c, vec_r, wide_r, statics=(chunk, half), scalars=2,
        )
        left, right, vectors = call(
            last_kernel, "last",
            [(rows_here, 4 * NB), (cols_here, 4 * NB), (2,) + tall_r],
            got, small_two, cross, vec_c, wide_c, vec_r, wide_r, new_c, part_c, new_r, part_r,
        )
        factors = jnp.stack([small_one[FACTOR], small_two[FACTOR]])
        return matrix - nt(left, right), vectors, factors

    return jax.shard_map(
        local,
        mesh=mesh,
        in_specs=(P("row", "col"),),
        out_specs=(P("row", "col"), P(None, "row", None), P()),
        check_vma=False,
    )
```

```python
import functools

import jax
import jax.numpy as jnp
from jax import lax
from jax.experimental import pallas as pl
from jax.experimental.pallas import tpu as pltpu
from jax.sharding import PartitionSpec as P

NB = 64
precise = lax.Precision.HIGHEST


def nn(a, b):
    return lax.dot_general(
        a, b, (((1,), (0,)), ((), ())), precision=precise, preferred_element_type=jnp.float32
    )


def tn(a, b):
    return lax.dot_general(
        a, b, (((0,), (0,)), ((), ())), precision=precise, preferred_element_type=jnp.float32
    )


def nt(a, b):
    return lax.dot_general(
        a, b, (((1,), (1,)), ((), ())), precision=precise, preferred_element_type=jnp.float32
    )


def places():
    sub = lax.broadcasted_iota(jnp.int32, (NB, 2 * NB), 0)
    lane = lax.broadcasted_iota(jnp.int32, (NB, 2 * NB), 1)
    return sub, lane


def inverse_root(gram):
    sub, lane = places()
    eye = (sub + NB == lane).astype(jnp.float32)
    work = jnp.concatenate([gram, jnp.zeros_like(gram)], axis=1) + eye
    scales = jnp.zeros((NB, 2 * NB), jnp.float32)
    for step in range(NB):
        row = work[step : step + 1, :]
        pivot = row[:, step : step + 1]
        scales = jnp.where(sub == step, pivot, scales)
        if step + 1 < NB:
            scaled = row * (1.0 / pivot)
            column = jnp.where(sub > step, work[:, step : step + 1], 0.0)
            work = work - column * scaled
    return (work * lax.rsqrt(scales))[:, NB:]


def signed_lu(negated_top):
    sub, lane = places()
    eye = (sub + NB == lane).astype(jnp.float32)
    work = jnp.concatenate([negated_top, jnp.zeros_like(negated_top)], axis=1) + eye
    lower = jnp.zeros((NB, 2 * NB), jnp.float32)
    upper = jnp.zeros((NB, 2 * NB), jnp.float32)
    signs = jnp.zeros((1, 2 * NB), jnp.float32)
    lane_row = lax.broadcasted_iota(jnp.int32, (1, 2 * NB), 1)
    for step in range(NB):
        row = work[step : step + 1, :]
        raw = row[:, step : step + 1]
        flip = jnp.where(raw > 0, 1.0, -1.0)
        signs = jnp.where(lane_row == step, flip, signs)
        pivot = raw + flip
        inverse = 1.0 / pivot
        row = jnp.where(lane_row == step, pivot, row)
        upper = jnp.where((sub == step) & (lane >= step), row, upper)
        column = work[:, step : step + 1]
        lower = jnp.where(
            lane == step, jnp.where(sub > step, column * inverse, jnp.where(sub == step, 1.0, 0.0)), lower
        )
        scaled = row * inverse
        work = jnp.where(sub == step, scaled, work - column * scaled)
    return lower[:, :NB], upper[:, :NB], work[:, NB:], signs[:, :NB]


def near_root(gram):
    sub = lax.broadcasted_iota(jnp.int32, (NB, NB), 0)
    lane = lax.broadcasted_iota(jnp.int32, (NB, NB), 1)
    eye = (sub == lane).astype(jnp.float32)
    off = gram - eye
    first_order = eye - jnp.where(sub > lane, off, jnp.where(sub == lane, 0.5 * off, 0.0))
    close = jnp.sum(off * off) < 2e-8
    return lax.cond(close, lambda: first_order, lambda: inverse_root(gram))


def fold(x, chunk):
    x = x.reshape(-1, chunk, NB)
    return jnp.concatenate([x[:, : chunk // 2], x[:, chunk // 2 :]], axis=2)


def unfold(x):
    return jnp.concatenate([x[:, :, :NB], x[:, :, NB:]], axis=1).reshape(-1, NB)


def pack_symmetric(g):
    h = NB // 2
    rows = []
    for quadrant in (g[:h, :h], g[:h, h:], g[h:, h:]):
        rows.append(jnp.concatenate([quadrant[k : k + 8] for k in range(0, h, 8)], axis=1))
    return jnp.concatenate(rows, axis=0)


def unpack_symmetric(x):
    h = NB // 2
    first, cross, last = [
        jnp.concatenate([x[q : q + 8, k : k + h] for k in range(0, 4 * h, h)], axis=0)
        for q in (0, 8, 16)
    ]
    upper = jnp.concatenate([first, cross], axis=1)
    return jnp.concatenate([upper, jnp.concatenate([cross.T, last], axis=1)], axis=0)


PACKED = 24


def put_pairs(out_ref, pairs):
    peers, rows = out_ref.shape[:2]
    per = NB // peers
    for q, pair in enumerate(pairs):
        for t in range(per):
            out_ref[:, q * per + t, :] = pair[t * peers : (t + 1) * peers]
    for k in range(len(pairs) * per, rows):
        out_ref[:, k, :] = jnp.zeros((peers, 2 * NB), jnp.float32)


def get_pairs(ref, first, count):
    per = NB // ref.shape[0]
    pairs = []
    for q in range(count):
        slots = [ref[:, first + q * per + t, :] for t in range(per)]
        pair = jnp.concatenate(slots, axis=0)
        pairs += [pair[:, :NB], pair[:, NB:]]
    return pairs


def beside(*parts):
    return jnp.concatenate(parts, axis=1)


def below(x, index, start):
    place = lax.broadcasted_iota(jnp.int32, x.shape, 0)
    return jnp.where((place >= start) | (index > 0), x, 0.0)


def start_kernel(chunk, index_ref, matrix_ref, raw_ref, out_ref):
    pair = matrix_ref[:, : 2 * NB]
    last = matrix_ref[:, 2 * NB : 3 * NB]
    raw_ref[:, :chunk, :] = pair.reshape(-1, chunk, 2 * NB)
    raw_ref[:, chunk:, :] = fold(last, chunk)
    panel = below(pair[:, :NB], index_ref[0], NB)
    packed = pack_symmetric(tn(panel, panel))
    out_ref[...] = jnp.broadcast_to(packed[None], out_ref.shape)


def relay_kernel(raw_ref, got_ref, out_ref):
    block = jnp.concatenate([raw_ref[...], jnp.sum(got_ref[...], axis=0)], axis=0)
    out_ref[...] = jnp.broadcast_to(block[None], out_ref.shape)


def last_raw(raw_ref, chunk):
    return unfold(raw_ref[:, chunk : chunk + chunk // 2, :])


def first_once_kernel(chunk, index_ref, raw_ref, root_ref, once_ref, small_ref):
    index = index_ref[0]
    root = inverse_root(unpack_symmetric(raw_ref[0, chunk + chunk // 2 :, :]))
    root_ref[...] = root
    pair = raw_ref[:, :chunk, :].reshape(-1, 2 * NB)
    following = pair[:, NB:]
    once = nt(below(pair[:, :NB], index, NB), root)
    once_ref[...] = once
    last = last_raw(raw_ref, chunk)
    gram = tn(once, once)
    image_top = tn(following, once)

    def top(x, k):
        return jnp.where(index == 0, x[k * NB : (k + 1) * NB], 0.0)

    put_pairs(
        small_ref,
        [
            beside(gram, image_top),
            beside(top(once, 1), top(following, 1)),
            beside(top(last, 2), jnp.zeros((NB, NB), jnp.float32)),
        ],
    )


def second_once_kernel(
    chunk, index_ref, got_ref, raw_ref, panel_ref, pair_ref, root_ref, once_ref, small_ref
):
    index = index_ref[0]
    root = inverse_root(unpack_symmetric(jnp.sum(got_ref[...], axis=0)))
    root_ref[...] = root
    once = nt(panel_ref[...], root)
    once_ref[...] = once
    last = last_raw(raw_ref, chunk)
    vec = pair_ref[:, :NB]
    wide = pair_ref[:, NB:]

    def top(x):
        return jnp.where(index == 0, x[2 * NB : 3 * NB], 0.0)

    put_pairs(
        small_ref,
        [
            beside(tn(once, once), tn(last, once)),
            beside(tn(vec, once), tn(wide, once)),
            beside(top(once), top(vec)),
            beside(top(wide), jnp.zeros((NB, NB), jnp.float32)),
        ],
    )


def sum_kernel(got_ref, out_ref, chunk_ref):
    summed = jnp.sum(got_ref[...], axis=0)
    out_ref[...] = jnp.broadcast_to(summed[None], out_ref.shape)
    chunk_ref[...] = summed[: chunk_ref.shape[0]]


def inner_kernel(gathered_ref, once_ref, chunk_ref, out_ref):
    half = chunk_ref.shape[0]
    inner = tn(once_ref[...], unfold(gathered_ref[:, :half, :]))
    block = jnp.concatenate([pack_symmetric(inner), chunk_ref[...]], axis=0)
    out_ref[...] = jnp.broadcast_to(block[None], out_ref.shape)


PICK, COEF, PICK_T, COEF_T, LOWER, FACTOR, INNER, WIDE = range(8)


def factor_small(gram, top, next_top, image_top, small_ref):
    root = near_root(gram)
    lower, upper, inverse, signs = signed_lu(-nt(top, root))
    sub = lax.broadcasted_iota(jnp.int32, (NB, NB), 0)
    lane = lax.broadcasted_iota(jnp.int32, (NB, NB), 1)
    triangle = lane >= sub
    upper_inverse = jnp.where(triangle, nn(inverse, lower), 0.0)
    lower_inverse = nn(upper, inverse)
    factor = jnp.where(triangle, nt(upper * signs, lower_inverse), 0.0)
    pick = nn(jnp.where(sub == lane, signs, 0.0), upper_inverse)
    coef = tn(root, upper_inverse)
    crossed = tn(pick, nn(image_top, coef))
    pick_t = nn(pick, factor)
    coef_t = nn(coef, factor)
    small_ref[PICK] = pick
    small_ref[COEF] = coef
    small_ref[PICK_T] = pick_t
    small_ref[COEF_T] = coef_t
    small_ref[LOWER] = lower
    small_ref[FACTOR] = factor
    small_ref[INNER] = tn(pick, nn(next_top, pick)) - crossed - crossed.T
    small_ref[WIDE] = nn(next_top, pick_t) - nn(image_top, coef_t)
    return pick, coef, pick_t, coef_t


def vectors_of(once, index, start, pick, coef):
    vec = -nn(once, coef)
    top = vec[start : start + NB] + jnp.where(index == 0, pick, 0.0)
    return jnp.concatenate([vec[:start], top, vec[start + NB :]], axis=0)


def half_core(small_ref, inner):
    coef = small_ref[COEF]
    factor = small_ref[FACTOR]
    inner = small_ref[INNER] + tn(coef, nn(inner, coef))
    return 0.5 * tn(factor, nn(inner, factor))


def first_factor_kernel(
    chunk, half, row_ref, col_ref, gathered_ref, raw_ref, once_c_ref, once_r_ref,
    small_ref, state_ref, vec_ref, factor_ref,
):
    gram, image_top, top, next_top, _, _ = get_pairs(gathered_ref, half, 3)
    pick, coef, pick_t, coef_t = factor_small(gram, top, next_top, image_top, small_ref)
    factor_ref[...] = small_ref[FACTOR]
    vec_ref[...] = vectors_of(once_r_ref[...], row_ref[0], NB, pick, coef)
    following = raw_ref[:, :chunk, :].reshape(-1, 2 * NB)[:, NB:]
    image = unfold(gathered_ref[:, :half, :])
    vec = vectors_of(once_c_ref[...], col_ref[0], NB, pick, coef)
    state_ref[...] = beside(vec, nn(following, pick_t) - nn(image, coef_t))


def second_panel(following, vec, wide, wide_top, lower, index):
    return below(following - nt(vec, wide_top) - nt(wide, lower), index, 2 * NB)


def first_cols_kernel(
    chunk, col_ref, got_ref, small_ref, state_ref, raw_ref, pair_ref, panel_ref, tops_ref, out_ref
):
    half = half_core(small_ref, unpack_symmetric(jnp.sum(got_ref[:, :PACKED, :], axis=0)))
    lower = small_ref[LOWER]
    wide_top = small_ref[WIDE] - nn(lower, half)
    tops_ref[0] = half
    tops_ref[1] = wide_top
    vec = state_ref[:, :NB]
    wide = state_ref[:, NB:] - nn(vec, half)
    pair_ref[...] = beside(wide, vec)
    following = raw_ref[:, :chunk, :].reshape(-1, 2 * NB)[:, NB:]
    panel = second_panel(following, vec, wide, wide_top, lower, col_ref[0])
    panel_ref[...] = panel
    packed = pack_symmetric(tn(panel, panel))
    out_ref[...] = jnp.broadcast_to(packed[None], out_ref.shape)


def first_rows_kernel(
    chunk, row_ref, got_ref, small_ref, vec_ref, raw_ref, tops_ref, pair_ref, panel_ref
):
    image = unfold(got_ref[:, PACKED:, :])
    following = raw_ref[:, :chunk, :].reshape(-1, 2 * NB)[:, NB:]
    vec = vec_ref[...]
    wide = nn(following, small_ref[PICK_T]) - nn(image, small_ref[COEF_T]) - nn(vec, tops_ref[0])
    pair_ref[...] = beside(vec, wide)
    panel_ref[...] = second_panel(following, vec, wide, tops_ref[1], small_ref[LOWER], row_ref[0])


def second_factor_kernel(
    chunk, half, row_ref, col_ref, gathered_ref, old_ref, raw_c_ref, raw_r_ref,
    once_c_ref, once_r_ref, pair_c_ref, pair_r_ref, factor_ref,
    small_ref, right_ref, state_ref, vectors_ref, factors_ref,
):
    gram, image_top, vec_dot, wide_dot, top, vec_top, wide_top, _ = get_pairs(
        gathered_ref, half, 4
    )
    last_top = get_pairs(old_ref, half, 3)[4]
    image_top = image_top - nn(vec_top, wide_dot) - nn(wide_top, vec_dot)
    crossed = nt(vec_top, wide_top)
    next_top = last_top - crossed - crossed.T
    pick, coef, pick_t, coef_t = factor_small(gram, top, next_top, image_top, small_ref)
    crossed = tn(nn(vec_dot, coef), nn(wide_dot, coef))
    small_ref[INNER] -= crossed + crossed.T
    factors_ref[0] = factor_ref[...]
    factors_ref[1] = small_ref[FACTOR]
    vec_dots = nn(wide_dot, coef_t) - tn(wide_top, pick_t)
    wide_dots = nn(vec_dot, coef_t) - tn(vec_top, pick_t)
    new = vectors_of(once_r_ref[...], row_ref[0], 2 * NB, pick, coef)
    vec = pair_r_ref[:, :NB]
    vectors_ref[0] = vec
    vectors_ref[1] = new
    part = nn(last_raw(raw_r_ref, chunk), pick_t)
    part += nn(vec, vec_dots) + nn(pair_r_ref[:, NB:], wide_dots)
    state_ref[...] = beside(new, part)
    new = vectors_of(once_c_ref[...], col_ref[0], 2 * NB, pick, coef)
    part = nn(last_raw(raw_c_ref, chunk), pick_t) - nn(unfold(gathered_ref[:, :half, :]), coef_t)
    part += nn(pair_c_ref[:, NB:], vec_dots) + nn(pair_c_ref[:, :NB], wide_dots)
    right_ref[...] = beside(part, new)


def last_kernel(got_ref, small_ref, state_ref, left_ref):
    half = half_core(small_ref, unpack_symmetric(jnp.sum(got_ref[:, :PACKED, :], axis=0)))
    new = state_ref[:, :NB]
    image = unfold(got_ref[:, PACKED:, :])
    wide = state_ref[:, NB:] - nn(image, small_ref[COEF_T]) - nn(new, half + half.T)
    left_ref[...] = beside(new, wide)


def call(kernel, name, outs, *args, statics=(), scalars=0, flops=1 << 24):
    in_smem = pl.BlockSpec(memory_space=pltpu.SMEM)
    in_vmem = pl.BlockSpec(memory_space=pltpu.VMEM)
    result = pl.pallas_call(
        functools.partial(kernel, *statics),
        out_shape=[jax.ShapeDtypeStruct(shape, jnp.float32) for shape in outs],
        in_specs=[in_smem if k < scalars else in_vmem for k in range(len(args))],
        out_specs=[in_vmem] * len(outs),
        compiler_params=pltpu.CompilerParams(vmem_limit_bytes=16 << 20),
        cost_estimate=pl.CostEstimate(flops=flops, bytes_accessed=1 << 22, transcendentals=0),
        name=name,
    )(*args)
    return result[0] if len(outs) == 1 else result


def swap(x, axis):
    return lax.all_to_all(x, axis, 0, 0)


def solution(mesh):
    nr = mesh.shape["row"]
    nc = mesh.shape["col"]

    def local(matrix):
        rows_here, cols_here = matrix.shape
        chunk = rows_here // nc
        half = chunk // 2
        few = -(-4 * (NB // nr) // 8) * 8
        my_row = lax.axis_index("row").astype(jnp.int32).reshape(1)
        my_col = lax.axis_index("col").astype(jnp.int32).reshape(1)
        to_rows = []
        for r in range(nr):
            for c in range(nc):
                first = r * rows_here + c * chunk
                source = (first % cols_here // chunk) * nc + first // cols_here
                to_rows.append((source, r * nc + c))
        to_cols = [(b, a) for a, b in to_rows]
        square = (NB, NB)
        tall_r = (rows_here, NB)
        tall_c = (cols_here, NB)

        raw_rows = chunk + half
        raw, grams = call(
            start_kernel, "start", [(nc, raw_rows, 2 * NB), (nr, PACKED, 2 * NB)],
            my_row, matrix[:, : 4 * NB], statics=(chunk,), scalars=1,
        )
        raw_chunk = swap(raw, "col")[0]
        raw_chunk_c = lax.ppermute(raw_chunk, ("row", "col"), to_cols)
        raw_r = call(
            relay_kernel, "relay", [(nc, raw_rows + PACKED, 2 * NB)], raw_chunk, swap(grams, "row")
        )
        raw_r = swap(raw_r, "col")
        raw_c = swap(jnp.broadcast_to(raw_chunk_c[None], (nr, raw_rows, 2 * NB)), "row")

        root, once_r, smalls = call(
            first_once_kernel, "first_once", [square, tall_r, (nr, few, 2 * NB)],
            my_row, raw_r, statics=(chunk,), scalars=1,
        )

        def image_round(once_r, smalls, ready):
            partial_image = fold(tn(matrix, once_r), chunk)
            got = swap(jnp.concatenate([partial_image, smalls], axis=1), "row")
            got, ready = lax.optimization_barrier((got, ready))
            blocks, image_chunk = call(
                sum_kernel, "sum_blocks", [got.shape, (half, 2 * NB)], got
            )
            image_chunk_r = lax.ppermute(image_chunk, ("row", "col"), to_rows)
            return swap(blocks, "row"), image_chunk_r, ready

        gathered, image_chunk_r, raw_c = image_round(once_r, smalls, raw_c)
        col_place = lax.axis_index("col") * cols_here + jnp.arange(cols_here)
        first_c = raw_c[:, :chunk].reshape(cols_here, 2 * NB)[:, :NB]
        once_c = nt(jnp.where(col_place[:, None] >= NB, first_c, 0.0), root)
        block = (nc, PACKED + half, 2 * NB)
        inners = call(inner_kernel, "inner", [block], gathered, once_c, image_chunk_r)
        got = swap(inners, "col")
        pair_shape_c = (cols_here, 2 * NB)
        pair_shape_r = (rows_here, 2 * NB)
        small_one, state_c, vec_r, factor_one = call(
            first_factor_kernel, "first_factor", [(8,) + square, pair_shape_c, tall_r, square],
            my_row, my_col, gathered, raw_c, once_c, once_r, statics=(chunk, half), scalars=2,
        )
        pair_c, panel_c, tops, grams = call(
            first_cols_kernel, "first_cols",
            [pair_shape_c, tall_c, (2,) + square, (nc, PACKED, 2 * NB)],
            my_col, got, small_one, state_c, raw_c, statics=(chunk,), scalars=1,
        )
        grams = swap(grams, "col")
        pair_r, panel_r = call(
            first_rows_kernel, "first_rows", [pair_shape_r, tall_r],
            my_row, got, small_one, vec_r, raw_r, tops, statics=(chunk,), scalars=1,
        )

        root, once_r, smalls = call(
            second_once_kernel, "second_once", [square, tall_r, (nr, few, 2 * NB)],
            my_row, grams, raw_r, panel_r, pair_r, statics=(chunk,), scalars=1,
        )
        old = gathered
        gathered, image_chunk_r, _ = image_round(once_r, smalls, my_row)
        once_c = nt(panel_c, root)
        current = matrix - nt(pair_r, pair_c)
        inners = call(inner_kernel, "inner", [block], gathered, once_c, image_chunk_r)
        got = swap(inners, "col")
        small_two, right, state_r, vectors, factors = call(
            second_factor_kernel, "second_factor",
            [(8,) + square, pair_shape_c, pair_shape_r, (2,) + tall_r, (2,) + square],
            my_row, my_col, gathered, old, raw_c, raw_r, once_c, once_r, pair_c, pair_r, factor_one,
            statics=(chunk, half), scalars=2,
        )
        left = call(last_kernel, "last", [pair_shape_r], got, small_two, state_r)
        return current - nt(left, right), vectors, factors

    return jax.shard_map(
        local,
        mesh=mesh,
        in_specs=(P("row", "col"),),
        out_specs=(P("row", "col"), P(None, "row", None), P()),
        check_vma=False,
    )
```

```python
import functools

import jax
import jax.numpy as jnp
from jax import lax
from jax.experimental import pallas as pl
from jax.experimental.pallas import tpu as pltpu
from jax.sharding import PartitionSpec as P

NB = 64
precise = lax.Precision.HIGHEST


def nn(a, b):
    return lax.dot_general(
        a, b, (((1,), (0,)), ((), ())), precision=precise, preferred_element_type=jnp.float32
    )


def tn(a, b):
    return lax.dot_general(
        a, b, (((0,), (0,)), ((), ())), precision=precise, preferred_element_type=jnp.float32
    )


def nt(a, b):
    return lax.dot_general(
        a, b, (((1,), (1,)), ((), ())), precision=precise, preferred_element_type=jnp.float32
    )


def places():
    sub = lax.broadcasted_iota(jnp.int32, (NB, 2 * NB), 0)
    lane = lax.broadcasted_iota(jnp.int32, (NB, 2 * NB), 1)
    return sub, lane


def inverse_root(gram):
    sub, lane = places()
    eye = (sub + NB == lane).astype(jnp.float32)
    work = jnp.concatenate([gram, jnp.zeros_like(gram)], axis=1) + eye
    scales = jnp.zeros((NB, 2 * NB), jnp.float32)
    for step in range(NB):
        row = work[step : step + 1, :]
        pivot = row[:, step : step + 1]
        scales = jnp.where(sub == step, pivot, scales)
        if step + 1 < NB:
            scaled = row * (1.0 / pivot)
            column = jnp.where(sub > step, work[:, step : step + 1], 0.0)
            work = work - column * scaled
    return (work * lax.rsqrt(scales))[:, NB:]


def signed_lu(negated_top):
    sub, lane = places()
    eye = (sub + NB == lane).astype(jnp.float32)
    work = jnp.concatenate([negated_top, jnp.zeros_like(negated_top)], axis=1) + eye
    lower = jnp.zeros((NB, 2 * NB), jnp.float32)
    upper = jnp.zeros((NB, 2 * NB), jnp.float32)
    signs = jnp.zeros((1, 2 * NB), jnp.float32)
    lane_row = lax.broadcasted_iota(jnp.int32, (1, 2 * NB), 1)
    for step in range(NB):
        row = work[step : step + 1, :]
        raw = row[:, step : step + 1]
        flip = jnp.where(raw > 0, 1.0, -1.0)
        signs = jnp.where(lane_row == step, flip, signs)
        pivot = raw + flip
        inverse = 1.0 / pivot
        row = jnp.where(lane_row == step, pivot, row)
        upper = jnp.where((sub == step) & (lane >= step), row, upper)
        column = work[:, step : step + 1]
        lower = jnp.where(
            lane == step, jnp.where(sub > step, column * inverse, jnp.where(sub == step, 1.0, 0.0)), lower
        )
        scaled = row * inverse
        work = jnp.where(sub == step, scaled, work - column * scaled)
    return lower[:, :NB], upper[:, :NB], work[:, NB:], signs[:, :NB]


def near_root(gram):
    sub = lax.broadcasted_iota(jnp.int32, (NB, NB), 0)
    lane = lax.broadcasted_iota(jnp.int32, (NB, NB), 1)
    eye = (sub == lane).astype(jnp.float32)
    off = gram - eye
    first_order = eye - jnp.where(sub > lane, off, jnp.where(sub == lane, 0.5 * off, 0.0))
    close = jnp.sum(off * off) < 2e-8
    return lax.cond(close, lambda: first_order, lambda: inverse_root(gram))


def fold(x, chunk):
    x = x.reshape(-1, chunk, NB)
    return jnp.concatenate([x[:, : chunk // 2], x[:, chunk // 2 :]], axis=2)


def unfold(x):
    return jnp.concatenate([x[:, :, :NB], x[:, :, NB:]], axis=1).reshape(-1, NB)


def pack_symmetric(g):
    h = NB // 2
    rows = []
    for quadrant in (g[:h, :h], g[:h, h:], g[h:, h:]):
        rows.append(jnp.concatenate([quadrant[k : k + 8] for k in range(0, h, 8)], axis=1))
    return jnp.concatenate(rows, axis=0)


def unpack_symmetric(x):
    h = NB // 2
    first, cross, last = [
        jnp.concatenate([x[q : q + 8, k : k + h] for k in range(0, 4 * h, h)], axis=0)
        for q in (0, 8, 16)
    ]
    upper = jnp.concatenate([first, cross], axis=1)
    return jnp.concatenate([upper, jnp.concatenate([cross.T, last], axis=1)], axis=0)


PACKED = 24


def put_pairs(out_ref, pairs):
    peers, rows = out_ref.shape[:2]
    per = NB // peers
    for q, pair in enumerate(pairs):
        for t in range(per):
            out_ref[:, q * per + t, :] = pair[t * peers : (t + 1) * peers]
    for k in range(len(pairs) * per, rows):
        out_ref[:, k, :] = jnp.zeros((peers, 2 * NB), jnp.float32)


def get_pairs(ref, first, count):
    per = NB // ref.shape[0]
    pairs = []
    for q in range(count):
        slots = [ref[:, first + q * per + t, :] for t in range(per)]
        pair = jnp.concatenate(slots, axis=0)
        pairs += [pair[:, :NB], pair[:, NB:]]
    return pairs


def beside(*parts):
    return jnp.concatenate(parts, axis=1)


def below(x, index, start):
    place = lax.broadcasted_iota(jnp.int32, x.shape, 0)
    return jnp.where((place >= start) | (index > 0), x, 0.0)


def plain_start_kernel(chunk, matrix_ref, raw_ref):
    raw_ref[:, :chunk, :] = matrix_ref[:, : 2 * NB].reshape(-1, chunk, 2 * NB)
    raw_ref[:, chunk:, :] = fold(matrix_ref[:, 2 * NB : 3 * NB], chunk)


def start_kernel(chunk, index_ref, matrix_ref, raw_ref, out_ref):
    plain_start_kernel(chunk, matrix_ref, raw_ref)
    panel = below(matrix_ref[:, :NB], index_ref[0], NB)
    packed = pack_symmetric(tn(panel, panel))
    out_ref[...] = jnp.broadcast_to(packed[None], out_ref.shape)


def relay_kernel(raw_ref, got_ref, out_ref):
    block = jnp.concatenate([raw_ref[...], jnp.sum(got_ref[...], axis=0)], axis=0)
    out_ref[...] = jnp.broadcast_to(block[None], out_ref.shape)


def last_raw(raw_ref, chunk):
    return unfold(raw_ref[:, chunk : chunk + chunk // 2, :])


def first_pairs(chunk, index, raw_ref, root, once_ref, small_ref):
    pair = raw_ref[:, :chunk, :].reshape(-1, 2 * NB)
    following = pair[:, NB:]
    once = below(pair[:, :NB], index, NB)
    if root is not None:
        once = nt(once, root)
    once_ref[...] = once
    last = last_raw(raw_ref, chunk)
    gram = tn(once, once)
    image_top = tn(following, once)

    def top(x, k):
        return jnp.where(index == 0, x[k * NB : (k + 1) * NB], 0.0)

    put_pairs(
        small_ref,
        [
            beside(gram, image_top),
            beside(top(once, 1), top(following, 1)),
            beside(top(last, 2), jnp.zeros((NB, NB), jnp.float32)),
        ],
    )


def plain_first_kernel(chunk, index_ref, raw_ref, panel_ref, small_ref):
    first_pairs(chunk, index_ref[0], raw_ref, None, panel_ref, small_ref)


def first_once_kernel(chunk, index_ref, raw_ref, root_ref, once_ref, small_ref):
    root = inverse_root(unpack_symmetric(raw_ref[0, chunk + chunk // 2 :, :]))
    root_ref[...] = root
    first_pairs(chunk, index_ref[0], raw_ref, root, once_ref, small_ref)


def second_pairs(index, once, last, vec, wide, small_ref):
    def top(x):
        return jnp.where(index == 0, x[2 * NB : 3 * NB], 0.0)

    put_pairs(
        small_ref,
        [
            beside(tn(once, once), tn(last, once)),
            beside(tn(vec, once), tn(wide, once)),
            beside(top(once), top(vec)),
            beside(top(wide), jnp.zeros((NB, NB), jnp.float32)),
        ],
    )


def second_once_kernel(
    chunk, index_ref, got_ref, raw_ref, panel_ref, pair_ref, root_ref, once_ref, small_ref
):
    root = inverse_root(unpack_symmetric(jnp.sum(got_ref[...], axis=0)))
    root_ref[...] = root
    once = nt(panel_ref[...], root)
    once_ref[...] = once
    last = last_raw(raw_ref, chunk)
    second_pairs(index_ref[0], once, last, pair_ref[:, :NB], pair_ref[:, NB:], small_ref)


def sum_kernel(got_ref, out_ref, chunk_ref):
    summed = jnp.sum(got_ref[...], axis=0)
    out_ref[...] = jnp.broadcast_to(summed[None], out_ref.shape)
    chunk_ref[...] = summed[: chunk_ref.shape[0]]


def inner_kernel(gathered_ref, once_ref, chunk_ref, out_ref):
    half = chunk_ref.shape[0]
    inner = tn(once_ref[...], unfold(gathered_ref[:, :half, :]))
    block = jnp.concatenate([pack_symmetric(inner), chunk_ref[...]], axis=0)
    out_ref[...] = jnp.broadcast_to(block[None], out_ref.shape)


PICK, COEF, PICK_T, COEF_T, LOWER, FACTOR, INNER, WIDE = range(8)


def factor_small(near, gram, top, next_top, image_top, small_ref):
    root = near_root(gram) if near else inverse_root(gram)
    lower, upper, inverse, signs = signed_lu(-nt(top, root))
    sub = lax.broadcasted_iota(jnp.int32, (NB, NB), 0)
    lane = lax.broadcasted_iota(jnp.int32, (NB, NB), 1)
    triangle = lane >= sub
    upper_inverse = jnp.where(triangle, nn(inverse, lower), 0.0)
    lower_inverse = nn(upper, inverse)
    factor = jnp.where(triangle, nt(upper * signs, lower_inverse), 0.0)
    pick = nn(jnp.where(sub == lane, signs, 0.0), upper_inverse)
    coef = tn(root, upper_inverse)
    crossed = tn(pick, nn(image_top, coef))
    pick_t = nn(pick, factor)
    coef_t = nn(coef, factor)
    small_ref[PICK] = pick
    small_ref[COEF] = coef
    small_ref[PICK_T] = pick_t
    small_ref[COEF_T] = coef_t
    small_ref[LOWER] = lower
    small_ref[FACTOR] = factor
    small_ref[INNER] = tn(pick, nn(next_top, pick)) - crossed - crossed.T
    small_ref[WIDE] = nn(next_top, pick_t) - nn(image_top, coef_t)
    sizes = jnp.sum(jnp.where(sub == lane, gram, 0.0), axis=0, keepdims=True)
    fine = jnp.sum(root * root * sizes) < 1.5 * NB
    return pick, coef, pick_t, coef_t, fine


def vectors_of(once, index, start, pick, coef):
    vec = -nn(once, coef)
    top = vec[start : start + NB] + jnp.where(index == 0, pick, 0.0)
    return jnp.concatenate([vec[:start], top, vec[start + NB :]], axis=0)


def half_core(small_ref, inner):
    coef = small_ref[COEF]
    factor = small_ref[FACTOR]
    inner = small_ref[INNER] + tn(coef, nn(inner, coef))
    return 0.5 * tn(factor, nn(inner, factor))


def first_factor_kernel(
    near, chunk, half, row_ref, col_ref, gathered_ref, raw_ref, once_c_ref, once_r_ref,
    small_ref, state_ref, vec_ref, factor_ref, fine_ref,
):
    gram, image_top, top, next_top, _, _ = get_pairs(gathered_ref, half, 3)
    pick, coef, pick_t, coef_t, fine = factor_small(
        near, gram, top, next_top, image_top, small_ref
    )
    fine_ref[0] = jnp.where(fine, 1, 0)
    factor_ref[...] = small_ref[FACTOR]
    vec_ref[...] = vectors_of(once_r_ref[...], row_ref[0], NB, pick, coef)
    following = raw_ref[:, :chunk, :].reshape(-1, 2 * NB)[:, NB:]
    image = unfold(gathered_ref[:, :half, :])
    vec = vectors_of(once_c_ref[...], col_ref[0], NB, pick, coef)
    state_ref[...] = beside(vec, nn(following, pick_t) - nn(image, coef_t))


def second_panel(following, vec, wide, wide_top, lower, index):
    return below(following - nt(vec, wide_top) - nt(wide, lower), index, 2 * NB)


def first_cols(chunk, index, got_ref, small_ref, state_ref, raw_ref, pair_ref, panel_ref, tops_ref):
    half = half_core(small_ref, unpack_symmetric(jnp.sum(got_ref[:, :PACKED, :], axis=0)))
    lower = small_ref[LOWER]
    wide_top = small_ref[WIDE] - nn(lower, half)
    tops_ref[0] = half
    tops_ref[1] = wide_top
    vec = state_ref[:, :NB]
    wide = state_ref[:, NB:] - nn(vec, half)
    pair_ref[...] = beside(wide, vec)
    following = raw_ref[:, :chunk, :].reshape(-1, 2 * NB)[:, NB:]
    panel = second_panel(following, vec, wide, wide_top, lower, index)
    panel_ref[...] = panel
    return panel, vec, wide


def first_cols_kernel(
    chunk, col_ref, got_ref, small_ref, state_ref, raw_ref, pair_ref, panel_ref, tops_ref, out_ref
):
    panel, _, _ = first_cols(
        chunk, col_ref[0], got_ref, small_ref, state_ref, raw_ref, pair_ref, panel_ref, tops_ref
    )
    packed = pack_symmetric(tn(panel, panel))
    out_ref[...] = jnp.broadcast_to(packed[None], out_ref.shape)


def plain_cols_kernel(
    chunk, col_ref, got_ref, small_ref, state_ref, raw_ref, pair_ref, panel_ref, tops_ref, out_ref
):
    panel, vec, wide = first_cols(
        chunk, col_ref[0], got_ref, small_ref, state_ref, raw_ref, pair_ref, panel_ref, tops_ref
    )
    second_pairs(col_ref[0], panel, last_raw(raw_ref, chunk), vec, wide, out_ref)


def first_rows_kernel(
    chunk, row_ref, got_ref, small_ref, vec_ref, raw_ref, tops_ref, pair_ref, panel_ref
):
    image = unfold(got_ref[:, PACKED:, :])
    following = raw_ref[:, :chunk, :].reshape(-1, 2 * NB)[:, NB:]
    vec = vec_ref[...]
    wide = nn(following, small_ref[PICK_T]) - nn(image, small_ref[COEF_T]) - nn(vec, tops_ref[0])
    pair_ref[...] = beside(vec, wide)
    panel_ref[...] = second_panel(following, vec, wide, tops_ref[1], small_ref[LOWER], row_ref[0])


def second_small(near, half, old_half, gathered_ref, old_ref, factor_ref, small_ref, factors_ref):
    gram, image_top, vec_dot, wide_dot, top, vec_top, wide_top, _ = get_pairs(
        gathered_ref, half, 4
    )
    last_top = get_pairs(old_ref, old_half, 3)[4]
    image_top = image_top - nn(vec_top, wide_dot) - nn(wide_top, vec_dot)
    crossed = nt(vec_top, wide_top)
    next_top = last_top - crossed - crossed.T
    pick, coef, pick_t, coef_t, fine = factor_small(
        near, gram, top, next_top, image_top, small_ref
    )
    crossed = tn(nn(vec_dot, coef), nn(wide_dot, coef))
    small_ref[INNER] -= crossed + crossed.T
    factors_ref[0] = factor_ref[...]
    factors_ref[1] = small_ref[FACTOR]
    vec_dots = nn(wide_dot, coef_t) - tn(wide_top, pick_t)
    wide_dots = nn(vec_dot, coef_t) - tn(vec_top, pick_t)
    return pick, coef, pick_t, coef_t, vec_dots, wide_dots, fine


def second_factor_kernel(
    chunk, half, row_ref, col_ref, gathered_ref, old_ref, raw_c_ref, raw_r_ref,
    once_c_ref, once_r_ref, pair_c_ref, pair_r_ref, factor_ref,
    small_ref, right_ref, state_ref, vectors_ref, factors_ref,
):
    pick, coef, pick_t, coef_t, vec_dots, wide_dots, _ = second_small(
        True, half, half, gathered_ref, old_ref, factor_ref, small_ref, factors_ref
    )
    new = vectors_of(once_r_ref[...], row_ref[0], 2 * NB, pick, coef)
    vec = pair_r_ref[:, :NB]
    vectors_ref[0] = vec
    vectors_ref[1] = new
    part = nn(last_raw(raw_r_ref, chunk), pick_t)
    part += nn(vec, vec_dots) + nn(pair_r_ref[:, NB:], wide_dots)
    state_ref[...] = beside(new, part)
    new = vectors_of(once_c_ref[...], col_ref[0], 2 * NB, pick, coef)
    part = nn(last_raw(raw_c_ref, chunk), pick_t) - nn(unfold(gathered_ref[:, :half, :]), coef_t)
    part += nn(pair_c_ref[:, NB:], vec_dots) + nn(pair_c_ref[:, :NB], wide_dots)
    right_ref[...] = beside(part, new)


def plain_second_kernel(
    chunk, half, row_ref, col_ref, gathered_ref, old_ref, raw_c_ref, raw_r_ref,
    panel_c_ref, panel_r_ref, pair_c_ref, pair_r_ref, factor_ref,
    small_ref, state_ref, left_ref, vectors_ref, factors_ref, fine_ref,
):
    pick, coef, pick_t, coef_t, vec_dots, wide_dots, fine = second_small(
        False, half, half, gathered_ref, old_ref, factor_ref, small_ref, factors_ref
    )
    fine_ref[0] = jnp.where(fine, 1, 0)
    new = vectors_of(panel_r_ref[...], row_ref[0], 2 * NB, pick, coef)
    vec = pair_r_ref[:, :NB]
    vectors_ref[0] = vec
    vectors_ref[1] = new
    part = nn(last_raw(raw_r_ref, chunk), pick_t) - nn(unfold(gathered_ref[:, :half, :]), coef_t)
    part += nn(vec, vec_dots) + nn(pair_r_ref[:, NB:], wide_dots)
    left_ref[...] = beside(part, new)
    new = vectors_of(panel_c_ref[...], col_ref[0], 2 * NB, pick, coef)
    part = nn(last_raw(raw_c_ref, chunk), pick_t)
    part += nn(pair_c_ref[:, NB:], vec_dots) + nn(pair_c_ref[:, :NB], wide_dots)
    state_ref[...] = beside(new, part)


def last_kernel(got_ref, small_ref, state_ref, out_ref):
    half = half_core(small_ref, unpack_symmetric(jnp.sum(got_ref[:, :PACKED, :], axis=0)))
    new = state_ref[:, :NB]
    image = unfold(got_ref[:, PACKED:, :])
    wide = state_ref[:, NB:] - nn(image, small_ref[COEF_T]) - nn(new, half + half.T)
    out_ref[...] = beside(new, wide)


def call(kernel, name, outs, *args, statics=(), scalars=0, flag=False):
    in_smem = pl.BlockSpec(memory_space=pltpu.SMEM)
    in_vmem = pl.BlockSpec(memory_space=pltpu.VMEM)
    out_shape = [jax.ShapeDtypeStruct(shape, jnp.float32) for shape in outs]
    out_specs = [in_vmem] * len(outs)
    if flag:
        out_shape.append(jax.ShapeDtypeStruct((1,), jnp.int32))
        out_specs.append(in_smem)
    result = pl.pallas_call(
        functools.partial(kernel, *statics),
        out_shape=out_shape,
        in_specs=[in_smem if k < scalars else in_vmem for k in range(len(args))],
        out_specs=out_specs,
        compiler_params=pltpu.CompilerParams(vmem_limit_bytes=16 << 20),
        cost_estimate=pl.CostEstimate(flops=1 << 24, bytes_accessed=1 << 22, transcendentals=0),
        name=name,
    )(*args)
    return result[0] if len(result) == 1 else result


def swap(x, axis):
    return lax.all_to_all(x, axis, 0, 0)


def solution(mesh):
    nr = mesh.shape["row"]
    nc = mesh.shape["col"]

    def local(matrix):
        rows_here, cols_here = matrix.shape
        chunk = rows_here // nc
        half = chunk // 2
        my_row = lax.axis_index("row").astype(jnp.int32).reshape(1)
        my_col = lax.axis_index("col").astype(jnp.int32).reshape(1)
        col_place = (lax.axis_index("col") * cols_here + jnp.arange(cols_here))[:, None]
        to_rows = []
        for r in range(nr):
            for c in range(nc):
                first = r * rows_here + c * chunk
                source = (first % cols_here // chunk) * nc + first // cols_here
                to_rows.append((source, r * nc + c))
        to_cols = [(b, a) for a, b in to_rows]
        square = (NB, NB)
        tall_r = (rows_here, NB)
        tall_c = (cols_here, NB)
        pair_shape_c = (cols_here, 2 * NB)
        pair_shape_r = (rows_here, 2 * NB)
        raw_rows = chunk + half

        def few(peers):
            return -(-4 * (NB // peers) // 8) * 8

        def image_round(partial_image, smalls, axis, targets, ready):
            mine = jnp.concatenate([fold(partial_image, chunk), smalls], axis=1)
            got, ready = lax.optimization_barrier((swap(mine, axis), ready))
            blocks, image_chunk = call(sum_kernel, "sum_blocks", [got.shape, (half, 2 * NB)], got)
            other = lax.ppermute(image_chunk, ("row", "col"), targets)
            return swap(blocks, axis), other, ready

        def spread_columns(raw_c):
            return swap(jnp.broadcast_to(raw_c[None], (nr, raw_rows, 2 * NB)), "row")

        def first_columns(raw_c):
            first_c = raw_c[:, :chunk].reshape(cols_here, 2 * NB)[:, :NB]
            return jnp.where(col_place >= NB, first_c, 0.0)

        block_r = (nc, PACKED + half, 2 * NB)
        block_c = (nr, PACKED + half, 2 * NB)

        def plain():
            raw = call(
                plain_start_kernel, "plain_start", [(nc, raw_rows, 2 * NB)],
                matrix[:, : 4 * NB], statics=(chunk,),
            )
            raw_chunk = swap(raw, "col")[0]
            raw_chunk_c = lax.ppermute(raw_chunk, ("row", "col"), to_cols)
            raw_r = swap(jnp.broadcast_to(raw_chunk[None], raw.shape), "col")
            raw_c = spread_columns(raw_chunk_c)
            first_r, smalls = call(
                plain_first_kernel, "plain_first", [tall_r, (nr, few(nr), 2 * NB)],
                my_row, raw_r, statics=(chunk,), scalars=1,
            )
            gathered, image_chunk, raw_c = image_round(
                tn(matrix, first_r), smalls, "row", to_rows, raw_c
            )
            first_c = first_columns(raw_c)
            inners = call(inner_kernel, "inner", [block_r], gathered, first_c, image_chunk)
            got = swap(inners, "col")
            small_one, state_c, vec_r, factor_one, fine_one = call(
                first_factor_kernel, "plain_factor", [(8,) + square, pair_shape_c, tall_r, square],
                my_row, my_col, gathered, raw_c, first_c, first_r,
                statics=(False, chunk, half), scalars=2, flag=True,
            )
            pair_c, panel_c, tops, smalls = call(
                plain_cols_kernel, "plain_cols",
                [pair_shape_c, tall_c, (2,) + square, (nc, few(nc), 2 * NB)],
                my_col, got, small_one, state_c, raw_c, statics=(chunk,), scalars=1,
            )
            pair_r, panel_r = call(
                first_rows_kernel, "first_rows", [pair_shape_r, tall_r],
                my_row, got, small_one, vec_r, raw_r, tops, statics=(chunk,), scalars=1,
            )
            old = gathered
            gathered, image_chunk, _ = image_round(
                nn(matrix, panel_c), smalls, "col", to_cols, my_row
            )
            current = matrix - nt(pair_r, pair_c)
            gathered, current = lax.optimization_barrier((gathered, current))
            inners = call(inner_kernel, "inner", [block_c], gathered, panel_r, image_chunk)
            got = swap(inners, "row")
            small_two, state_c, left, vectors, factors, fine_two = call(
                plain_second_kernel, "plain_second",
                [(8,) + square, pair_shape_c, pair_shape_r, (2,) + tall_r, (2,) + square],
                my_row, my_col, gathered, old, raw_c, raw_r, panel_c, panel_r,
                pair_c, pair_r, factor_one, statics=(chunk, half), scalars=2, flag=True,
            )
            right = call(last_kernel, "last", [pair_shape_c], got, small_two, state_c)
            return (current, left, right, vectors, factors), (fine_one + fine_two)[0] == 2

        def careful():
            raw, grams = call(
                start_kernel, "start", [(nc, raw_rows, 2 * NB), (nr, PACKED, 2 * NB)],
                my_row, matrix[:, : 4 * NB], statics=(chunk,), scalars=1,
            )
            raw_chunk = swap(raw, "col")[0]
            raw_chunk_c = lax.ppermute(raw_chunk, ("row", "col"), to_cols)
            raw_r = call(
                relay_kernel, "relay", [(nc, raw_rows + PACKED, 2 * NB)], raw_chunk, swap(grams, "row")
            )
            raw_r = swap(raw_r, "col")
            raw_c = spread_columns(raw_chunk_c)

            root, once_r, smalls = call(
                first_once_kernel, "first_once", [square, tall_r, (nr, few(nr), 2 * NB)],
                my_row, raw_r, statics=(chunk,), scalars=1,
            )

            gathered, image_chunk_r, raw_c = image_round(
                tn(matrix, once_r), smalls, "row", to_rows, raw_c
            )
            once_c = nt(first_columns(raw_c), root)
            inners = call(inner_kernel, "inner", [block_r], gathered, once_c, image_chunk_r)
            got = swap(inners, "col")
            small_one, state_c, vec_r, factor_one, _ = call(
                first_factor_kernel, "first_factor", [(8,) + square, pair_shape_c, tall_r, square],
                my_row, my_col, gathered, raw_c, once_c, once_r,
                statics=(True, chunk, half), scalars=2, flag=True,
            )
            pair_c, panel_c, tops, grams = call(
                first_cols_kernel, "first_cols",
                [pair_shape_c, tall_c, (2,) + square, (nc, PACKED, 2 * NB)],
                my_col, got, small_one, state_c, raw_c, statics=(chunk,), scalars=1,
            )
            grams = swap(grams, "col")
            pair_r, panel_r = call(
                first_rows_kernel, "first_rows", [pair_shape_r, tall_r],
                my_row, got, small_one, vec_r, raw_r, tops, statics=(chunk,), scalars=1,
            )

            root, once_r, smalls = call(
                second_once_kernel, "second_once", [square, tall_r, (nr, few(nr), 2 * NB)],
                my_row, grams, raw_r, panel_r, pair_r, statics=(chunk,), scalars=1,
            )
            old = gathered
            gathered, image_chunk_r, _ = image_round(
                tn(matrix, once_r), smalls, "row", to_rows, my_row
            )
            once_c = nt(panel_c, root)
            current = matrix - nt(pair_r, pair_c)
            inners = call(inner_kernel, "inner", [block_r], gathered, once_c, image_chunk_r)
            got = swap(inners, "col")
            small_two, right, state_r, vectors, factors = call(
                second_factor_kernel, "second_factor",
                [(8,) + square, pair_shape_c, pair_shape_r, (2,) + tall_r, (2,) + square],
                my_row, my_col, gathered, old, raw_c, raw_r, once_c, once_r, pair_c, pair_r, factor_one,
                statics=(chunk, half), scalars=2,
            )
            left = call(last_kernel, "last", [pair_shape_r], got, small_two, state_r)
            return current - nt(left, right), vectors, factors

        ready, fine = plain()

        def finish(current, left, right, vectors, factors):
            return current - nt(left, right), vectors, factors

        return lax.cond(fine, finish, lambda *_: careful(), *ready)

    return jax.shard_map(
        local,
        mesh=mesh,
        in_specs=(P("row", "col"),),
        out_specs=(P("row", "col"), P(None, "row", None), P()),
        check_vma=False,
    )
```

```python
import functools

import jax
import jax.numpy as jnp
from jax import lax
from jax.experimental import pallas as pl
from jax.experimental.pallas import tpu as pltpu
from jax.sharding import PartitionSpec as P

NB = 64
precise = lax.Precision.HIGHEST


def nn(a, b):
    return lax.dot_general(
        a, b, (((1,), (0,)), ((), ())), precision=precise, preferred_element_type=jnp.float32
    )


def tn(a, b):
    return lax.dot_general(
        a, b, (((0,), (0,)), ((), ())), precision=precise, preferred_element_type=jnp.float32
    )


def nt(a, b):
    return lax.dot_general(
        a, b, (((1,), (1,)), ((), ())), precision=precise, preferred_element_type=jnp.float32
    )


def places():
    sub = lax.broadcasted_iota(jnp.int32, (NB, 2 * NB), 0)
    lane = lax.broadcasted_iota(jnp.int32, (NB, 2 * NB), 1)
    return sub, lane


def inverse_root(gram):
    sub, lane = places()
    eye = (sub + NB == lane).astype(jnp.float32)
    work = jnp.concatenate([gram, jnp.zeros_like(gram)], axis=1) + eye
    scales = jnp.zeros((NB, 2 * NB), jnp.float32)
    for step in range(0, NB, 2):
        first = work[step : step + 1]
        second = work[step + 1 : step + 2]
        left = jnp.broadcast_to(work[:, step : step + 1], work.shape)
        right = jnp.broadcast_to(work[:, step + 1 : step + 2], work.shape)
        a, b = left[step : step + 1], right[step : step + 1]
        c, d = left[step + 1 : step + 2], right[step + 1 : step + 2]
        inverse = 1.0 / a
        det = a * d - b * c
        last = a * (1.0 / det)
        second = second - (c * inverse) * first
        scales = jnp.where(sub == step, a, jnp.where(sub == step + 1, det * inverse, scales))
        second_scaled = second * last
        first_scaled = first * inverse - (b * inverse) * second_scaled
        change = left * first_scaled + right * second_scaled
        work = jnp.where(sub > step + 1, work - change, jnp.where(sub == step + 1, second, work))
    return (work * lax.rsqrt(scales))[:, NB:]


def signed_lu(negated_top):
    sub, lane = places()
    eye = (sub + NB == lane).astype(jnp.float32)
    work = jnp.concatenate([negated_top, jnp.zeros_like(negated_top)], axis=1) + eye
    lower = jnp.zeros((NB, 2 * NB), jnp.float32)
    upper = jnp.zeros((NB, 2 * NB), jnp.float32)
    signs = jnp.zeros((1, 2 * NB), jnp.float32)
    lane_row = lax.broadcasted_iota(jnp.int32, (1, 2 * NB), 1)
    for step in range(0, NB, 2):
        left = jnp.broadcast_to(work[:, step : step + 1], work.shape)
        right = jnp.broadcast_to(work[:, step + 1 : step + 2], work.shape)
        raw, b = left[step : step + 1], right[step : step + 1]
        c, d = left[step + 1 : step + 2], right[step + 1 : step + 2]
        flip = jnp.where(raw > 0, 1.0, -1.0)
        a = raw + flip
        raw_det = a * d - b * c
        flip_last = jnp.where(raw_det * flip > 0, 1.0, -1.0)
        det = raw_det + flip_last * a
        inverse = 1.0 / a
        last = a * (1.0 / det)
        signs = jnp.where(lane_row == step, flip, jnp.where(lane_row == step + 1, flip_last, signs))
        first = jnp.where(lane_row == step, a, work[step : step + 1])
        second = work[step + 1 : step + 2] - (c * inverse) * first
        second = jnp.where(lane_row == step + 1, det * inverse, second)
        upper = jnp.where(
            (sub == step) & (lane >= step), first,
            jnp.where((sub == step + 1) & (lane > step), second, upper),
        )
        second_scaled = second * last
        second_scaled = jnp.where(lane_row == step, 0.0, second_scaled)
        ratio = b * inverse
        first_scaled = first * inverse - ratio * second_scaled
        below_first = jnp.where(sub > step, left * inverse, jnp.where(sub == step, 1.0, 0.0))
        below_last = (right - left * ratio) * last
        below_last = jnp.where(sub > step + 1, below_last, jnp.where(sub == step + 1, 1.0, 0.0))
        lower = jnp.where(lane == step, below_first, jnp.where(lane == step + 1, below_last, lower))
        change = left * first_scaled + right * second_scaled
        work = jnp.where(
            sub == step, first_scaled, jnp.where(sub == step + 1, second_scaled, work - change)
        )
    return lower[:, :NB], upper[:, :NB], work[:, NB:], signs[:, :NB]


def near_root(gram):
    sub = lax.broadcasted_iota(jnp.int32, (NB, NB), 0)
    lane = lax.broadcasted_iota(jnp.int32, (NB, NB), 1)
    eye = (sub == lane).astype(jnp.float32)
    off = gram - eye
    first_order = eye - jnp.where(sub > lane, off, jnp.where(sub == lane, 0.5 * off, 0.0))
    close = jnp.sum(off * off) < 2e-8
    return lax.cond(close, lambda: first_order, lambda: inverse_root(gram))


def fold(x, chunk):
    x = x.reshape(-1, chunk, NB)
    return jnp.concatenate([x[:, : chunk // 2], x[:, chunk // 2 :]], axis=2)


def unfold(x):
    return jnp.concatenate([x[:, :, :NB], x[:, :, NB:]], axis=1).reshape(-1, NB)


def pack_symmetric(g):
    h = NB // 2
    rows = []
    for quadrant in (g[:h, :h], g[:h, h:], g[h:, h:]):
        rows.append(jnp.concatenate([quadrant[k : k + 8] for k in range(0, h, 8)], axis=1))
    return jnp.concatenate(rows, axis=0)


def unpack_symmetric(x):
    h = NB // 2
    first, cross, last = [
        jnp.concatenate([x[q : q + 8, k : k + h] for k in range(0, 4 * h, h)], axis=0)
        for q in (0, 8, 16)
    ]
    upper = jnp.concatenate([first, cross], axis=1)
    return jnp.concatenate([upper, jnp.concatenate([cross.T, last], axis=1)], axis=0)


PACKED = 24


def put_pairs(out_ref, pairs, first=0):
    peers, rows = out_ref.shape[:2]
    per = NB // peers
    for q, pair in enumerate(pairs):
        for t in range(per):
            out_ref[:, first + q * per + t, :] = pair[t * peers : (t + 1) * peers]
    for k in range(first + len(pairs) * per, rows):
        out_ref[:, k, :] = jnp.zeros((peers, 2 * NB), jnp.float32)


def get_pairs(ref, first, count):
    per = NB // ref.shape[0]
    pairs = []
    for q in range(count):
        slots = [ref[:, first + q * per + t, :] for t in range(per)]
        pair = jnp.concatenate(slots, axis=0)
        pairs += [pair[:, :NB], pair[:, NB:]]
    return pairs


def beside(*parts):
    return jnp.concatenate(parts, axis=1)


def below(x, index, start):
    place = lax.broadcasted_iota(jnp.int32, x.shape, 0)
    return jnp.where((place >= start) | (index > 0), x, 0.0)


def plain_start_kernel(chunk, matrix_ref, raw_ref):
    raw_ref[:, :chunk, :] = matrix_ref[:, : 2 * NB].reshape(-1, chunk, 2 * NB)
    raw_ref[:, chunk:, :] = fold(matrix_ref[:, 2 * NB : 3 * NB], chunk)


def start_kernel(chunk, index_ref, matrix_ref, raw_ref, out_ref):
    plain_start_kernel(chunk, matrix_ref, raw_ref)
    panel = below(matrix_ref[:, :NB], index_ref[0], NB)
    packed = pack_symmetric(tn(panel, panel))
    out_ref[...] = jnp.broadcast_to(packed[None], out_ref.shape)


def relay_kernel(raw_ref, got_ref, out_ref):
    block = jnp.concatenate([raw_ref[...], jnp.sum(got_ref[...], axis=0)], axis=0)
    out_ref[...] = jnp.broadcast_to(block[None], out_ref.shape)


def pair_raw(raw_ref, chunk, at=0):
    return raw_ref[:, at : at + chunk, :].reshape(-1, 2 * NB)


def last_raw(raw_ref, chunk, at=0):
    return unfold(raw_ref[:, at + chunk : at + chunk + chunk // 2, :])


def first_pairs(chunk, index, raw_ref, root, once_ref, small_ref):
    pair = pair_raw(raw_ref, chunk)
    following = pair[:, NB:]
    once = below(pair[:, :NB], index, NB)
    if root is not None:
        once = nt(once, root)
    once_ref[...] = once
    last = last_raw(raw_ref, chunk)
    gram = tn(once, once)
    image_top = tn(following, once)

    def top(x, k):
        return jnp.where(index == 0, x[k * NB : (k + 1) * NB], 0.0)

    put_pairs(
        small_ref,
        [
            beside(gram, image_top),
            beside(top(once, 1), top(following, 1)),
            beside(top(last, 2), jnp.zeros((NB, NB), jnp.float32)),
        ],
    )


def plain_first_kernel(chunk, index_ref, raw_ref, panel_ref, small_ref):
    first_pairs(chunk, index_ref[0], raw_ref, None, panel_ref, small_ref)


def first_once_kernel(chunk, index_ref, raw_ref, root_ref, once_ref, small_ref):
    root = inverse_root(unpack_symmetric(raw_ref[0, chunk + chunk // 2 :, :]))
    root_ref[...] = root
    first_pairs(chunk, index_ref[0], raw_ref, root, once_ref, small_ref)


def second_pairs(index, once, last, vec, wide, small_ref, first=0):
    def top(x):
        return jnp.where(index == 0, x[2 * NB : 3 * NB], 0.0)

    put_pairs(
        small_ref,
        [
            beside(tn(once, once), tn(last, once)),
            beside(tn(vec, once), tn(wide, once)),
            beside(top(once), top(vec)),
            beside(top(wide), jnp.zeros((NB, NB), jnp.float32)),
        ],
        first,
    )


def second_once_kernel(
    chunk, index_ref, got_ref, raw_ref, panel_ref, pair_ref, root_ref, once_ref, small_ref
):
    root = inverse_root(unpack_symmetric(jnp.sum(got_ref[...], axis=0)))
    root_ref[...] = root
    once = nt(panel_ref[...], root)
    once_ref[...] = once
    last = last_raw(raw_ref, chunk)
    second_pairs(index_ref[0], once, last, pair_ref[:, :NB], pair_ref[:, NB:], small_ref)


def sum_kernel(got_ref, out_ref, chunk_ref):
    summed = jnp.sum(got_ref[...], axis=0)
    out_ref[...] = jnp.broadcast_to(summed[None], out_ref.shape)
    chunk_ref[...] = summed[: chunk_ref.shape[0]]


def sum_with_kernel(got_ref, raw_ref, out_ref, chunk_ref):
    summed = jnp.sum(got_ref[...], axis=0)
    block = jnp.concatenate([summed, raw_ref[...]], axis=0)
    out_ref[...] = jnp.broadcast_to(block[None], out_ref.shape)
    chunk_ref[...] = summed[: chunk_ref.shape[0]]


def inner_kernel(gathered_ref, once_ref, chunk_ref, out_ref):
    half = chunk_ref.shape[0]
    inner = tn(once_ref[...], unfold(gathered_ref[:, :half, :]))
    block = jnp.concatenate([pack_symmetric(inner), chunk_ref[...]], axis=0)
    out_ref[...] = jnp.broadcast_to(block[None], out_ref.shape)


def plain_inner_kernel(chunk, at, col_ref, gathered_ref, chunk_ref, out_ref):
    half = chunk_ref.shape[0]
    panel = below(pair_raw(gathered_ref, chunk, at)[:, :NB], col_ref[0], NB)
    inner = tn(panel, unfold(gathered_ref[:, :half, :]))
    block = jnp.concatenate([pack_symmetric(inner), chunk_ref[...]], axis=0)
    out_ref[...] = jnp.broadcast_to(block[None], out_ref.shape)


PICK, COEF, PICK_T, COEF_T, LOWER, FACTOR, INNER, WIDE = range(8)


def factor_small(near, gram, top, next_top, image_top, small_ref):
    root = near_root(gram) if near else inverse_root(gram)
    lower, upper, inverse, signs = signed_lu(-nt(top, root))
    sub = lax.broadcasted_iota(jnp.int32, (NB, NB), 0)
    lane = lax.broadcasted_iota(jnp.int32, (NB, NB), 1)
    triangle = lane >= sub
    upper_inverse = jnp.where(triangle, nn(inverse, lower), 0.0)
    lower_inverse = nn(upper, inverse)
    factor = jnp.where(triangle, nt(upper * signs, lower_inverse), 0.0)
    pick = nn(jnp.where(sub == lane, signs, 0.0), upper_inverse)
    coef = tn(root, upper_inverse)
    crossed = tn(pick, nn(image_top, coef))
    pick_t = nn(pick, factor)
    coef_t = nn(coef, factor)
    small_ref[PICK] = pick
    small_ref[COEF] = coef
    small_ref[PICK_T] = pick_t
    small_ref[COEF_T] = coef_t
    small_ref[LOWER] = lower
    small_ref[FACTOR] = factor
    small_ref[INNER] = tn(pick, nn(next_top, pick)) - crossed - crossed.T
    small_ref[WIDE] = nn(next_top, pick_t) - nn(image_top, coef_t)
    sizes = jnp.sum(jnp.where(sub == lane, gram, 0.0), axis=0, keepdims=True)
    fine = jnp.sum(root * root * sizes) < 1.5 * NB
    return pick, coef, pick_t, coef_t, fine


def vectors_of(once, index, start, pick, coef):
    vec = -nn(once, coef)
    top = vec[start : start + NB] + jnp.where(index == 0, pick, 0.0)
    return jnp.concatenate([vec[:start], top, vec[start + NB :]], axis=0)


def half_core(small_ref, inner):
    coef = small_ref[COEF]
    factor = small_ref[FACTOR]
    inner = small_ref[INNER] + tn(coef, nn(inner, coef))
    return 0.5 * tn(factor, nn(inner, factor))


def first_factor(near, chunk, half, at, row, col, gathered_ref, once_c, once_r, outs):
    small_ref, state_ref, vec_ref, factor_ref, fine_ref = outs
    gram, image_top, top, next_top, _, _ = get_pairs(gathered_ref, half, 3)
    pick, coef, pick_t, coef_t, fine = factor_small(
        near, gram, top, next_top, image_top, small_ref
    )
    fine_ref[0] = jnp.where(fine, 1, 0)
    factor_ref[...] = small_ref[FACTOR]
    vec_ref[...] = vectors_of(once_r, row, NB, pick, coef)
    following = pair_raw(gathered_ref, chunk, at)[:, NB:]
    image = unfold(gathered_ref[:, :half, :])
    vec = vectors_of(once_c, col, NB, pick, coef)
    state_ref[...] = beside(vec, nn(following, pick_t) - nn(image, coef_t))


def first_factor_kernel(
    chunk, half, at, row_ref, col_ref, gathered_ref, once_c_ref, once_r_ref, *outs
):
    first_factor(
        True, chunk, half, at, row_ref[0], col_ref[0], gathered_ref,
        once_c_ref[...], once_r_ref[...], outs,
    )


def plain_factor_kernel(chunk, half, at, row_ref, col_ref, gathered_ref, panel_r_ref, *outs):
    panel = below(pair_raw(gathered_ref, chunk, at)[:, :NB], col_ref[0], NB)
    first_factor(
        False, chunk, half, at, row_ref[0], col_ref[0], gathered_ref, panel, panel_r_ref[...], outs
    )


def second_panel(following, vec, wide, wide_top, lower, index):
    return below(following - nt(vec, wide_top) - nt(wide, lower), index, 2 * NB)


def first_cols(
    chunk, at, index, got_ref, small_ref, state_ref, raw_ref, pair_ref, panel_ref, tops_ref
):
    half = half_core(small_ref, unpack_symmetric(jnp.sum(got_ref[:, :PACKED, :], axis=0)))
    lower = small_ref[LOWER]
    wide_top = small_ref[WIDE] - nn(lower, half)
    tops_ref[0] = half
    tops_ref[1] = wide_top
    vec = state_ref[:, :NB]
    wide = state_ref[:, NB:] - nn(vec, half)
    pair_ref[...] = beside(wide, vec)
    following = pair_raw(raw_ref, chunk, at)[:, NB:]
    panel = second_panel(following, vec, wide, wide_top, lower, index)
    panel_ref[...] = panel
    return panel, vec, wide


def first_cols_kernel(
    chunk, at, col_ref, got_ref, small_ref, state_ref, raw_ref,
    pair_ref, panel_ref, tops_ref, out_ref,
):
    panel, _, _ = first_cols(
        chunk, at, col_ref[0], got_ref, small_ref, state_ref, raw_ref,
        pair_ref, panel_ref, tops_ref,
    )
    packed = pack_symmetric(tn(panel, panel))
    out_ref[...] = jnp.broadcast_to(packed[None], out_ref.shape)


def plain_cols_kernel(
    chunk, at, col_ref, got_ref, small_ref, state_ref, raw_ref, matrix_ref,
    pair_ref, panel_ref, tops_ref, out_ref,
):
    panel, vec, wide = first_cols(
        chunk, at, col_ref[0], got_ref, small_ref, state_ref, raw_ref,
        pair_ref, panel_ref, tops_ref,
    )
    half = chunk // 2
    out_ref[:, :half, :] = fold(nn(matrix_ref[...], panel), chunk)
    last = last_raw(raw_ref, chunk, at)
    second_pairs(col_ref[0], panel, last, vec, wide, out_ref, half)


def first_rows_kernel(
    chunk, row_ref, got_ref, small_ref, vec_ref, raw_ref, tops_ref, pair_ref, panel_ref
):
    image = unfold(got_ref[:, PACKED:, :])
    following = pair_raw(raw_ref, chunk)[:, NB:]
    vec = vec_ref[...]
    wide = nn(following, small_ref[PICK_T]) - nn(image, small_ref[COEF_T]) - nn(vec, tops_ref[0])
    pair_ref[...] = beside(vec, wide)
    panel_ref[...] = second_panel(following, vec, wide, tops_ref[1], small_ref[LOWER], row_ref[0])


def second_small(near, half, old_half, gathered_ref, old_ref, factor_ref, small_ref, factors_ref):
    gram, image_top, vec_dot, wide_dot, top, vec_top, wide_top, _ = get_pairs(
        gathered_ref, half, 4
    )
    last_top = get_pairs(old_ref, old_half, 3)[4]
    image_top = image_top - nn(vec_top, wide_dot) - nn(wide_top, vec_dot)
    crossed = nt(vec_top, wide_top)
    next_top = last_top - crossed - crossed.T
    pick, coef, pick_t, coef_t, fine = factor_small(
        near, gram, top, next_top, image_top, small_ref
    )
    crossed = tn(nn(vec_dot, coef), nn(wide_dot, coef))
    small_ref[INNER] -= crossed + crossed.T
    factors_ref[0] = factor_ref[...]
    factors_ref[1] = small_ref[FACTOR]
    vec_dots = nn(wide_dot, coef_t) - tn(wide_top, pick_t)
    wide_dots = nn(vec_dot, coef_t) - tn(vec_top, pick_t)
    return pick, coef, pick_t, coef_t, vec_dots, wide_dots, fine


def second_factor_kernel(
    chunk, half, at, row_ref, col_ref, gathered_ref, old_ref, raw_r_ref,
    once_c_ref, once_r_ref, pair_c_ref, pair_r_ref, factor_ref,
    small_ref, right_ref, state_ref, vectors_ref, factors_ref,
):
    pick, coef, pick_t, coef_t, vec_dots, wide_dots, _ = second_small(
        True, half, half, gathered_ref, old_ref, factor_ref, small_ref, factors_ref
    )
    new = vectors_of(once_r_ref[...], row_ref[0], 2 * NB, pick, coef)
    vec = pair_r_ref[:, :NB]
    vectors_ref[0] = vec.T
    vectors_ref[1] = new.T
    part = nn(last_raw(raw_r_ref, chunk), pick_t)
    part += nn(vec, vec_dots) + nn(pair_r_ref[:, NB:], wide_dots)
    state_ref[...] = beside(new, part)
    new = vectors_of(once_c_ref[...], col_ref[0], 2 * NB, pick, coef)
    part = nn(last_raw(old_ref, chunk, at), pick_t) - nn(unfold(gathered_ref[:, :half, :]), coef_t)
    part += nn(pair_c_ref[:, NB:], vec_dots) + nn(pair_c_ref[:, :NB], wide_dots)
    right_ref[...] = beside(part, new)


def plain_second_kernel(
    chunk, half, at, row_ref, col_ref, gathered_ref, old_ref, raw_r_ref,
    panel_c_ref, panel_r_ref, pair_c_ref, pair_r_ref, factor_ref,
    small_ref, state_ref, left_ref, vectors_ref, factors_ref, fine_ref,
):
    pick, coef, pick_t, coef_t, vec_dots, wide_dots, fine = second_small(
        False, half, half, gathered_ref, old_ref, factor_ref, small_ref, factors_ref
    )
    fine_ref[0] = jnp.where(fine, 1, 0)
    new = vectors_of(panel_r_ref[...], row_ref[0], 2 * NB, pick, coef)
    vec = pair_r_ref[:, :NB]
    vectors_ref[0] = vec.T
    vectors_ref[1] = new.T
    part = nn(last_raw(raw_r_ref, chunk), pick_t) - nn(unfold(gathered_ref[:, :half, :]), coef_t)
    part += nn(vec, vec_dots) + nn(pair_r_ref[:, NB:], wide_dots)
    left_ref[...] = beside(part, new)
    new = vectors_of(panel_c_ref[...], col_ref[0], 2 * NB, pick, coef)
    part = nn(last_raw(old_ref, chunk, at), pick_t)
    part += nn(pair_c_ref[:, NB:], vec_dots) + nn(pair_c_ref[:, :NB], wide_dots)
    state_ref[...] = beside(new, part)


def last_kernel(got_ref, small_ref, state_ref, out_ref):
    half = half_core(small_ref, unpack_symmetric(jnp.sum(got_ref[:, :PACKED, :], axis=0)))
    new = state_ref[:, :NB]
    image = unfold(got_ref[:, PACKED:, :])
    wide = state_ref[:, NB:] - nn(image, small_ref[COEF_T]) - nn(new, half + half.T)
    out_ref[...] = beside(new, wide)


def call(kernel, name, outs, *args, statics=(), scalars=0, flag=False):
    in_smem = pl.BlockSpec(memory_space=pltpu.SMEM)
    in_vmem = pl.BlockSpec(memory_space=pltpu.VMEM)
    out_shape = [jax.ShapeDtypeStruct(shape, jnp.float32) for shape in outs]
    out_specs = [in_vmem] * len(outs)
    if flag:
        out_shape.append(jax.ShapeDtypeStruct((1,), jnp.int32))
        out_specs.append(in_smem)
    result = pl.pallas_call(
        functools.partial(kernel, *statics),
        out_shape=out_shape,
        in_specs=[in_smem if k < scalars else in_vmem for k in range(len(args))],
        out_specs=out_specs,
        compiler_params=pltpu.CompilerParams(vmem_limit_bytes=16 << 20),
        cost_estimate=pl.CostEstimate(flops=1 << 24, bytes_accessed=1 << 22, transcendentals=0),
        name=name,
    )(*args)
    return result[0] if len(result) == 1 else result


def swap(x, axis):
    return lax.all_to_all(x, axis, 0, 0)


def solution(mesh):
    nr = mesh.shape["row"]
    nc = mesh.shape["col"]

    def local(matrix):
        rows_here, cols_here = matrix.shape
        chunk = rows_here // nc
        half = chunk // 2
        my_row = lax.axis_index("row").astype(jnp.int32).reshape(1)
        my_col = lax.axis_index("col").astype(jnp.int32).reshape(1)
        col_place = (lax.axis_index("col") * cols_here + jnp.arange(cols_here))[:, None]
        to_rows = []
        for r in range(nr):
            for c in range(nc):
                first = r * rows_here + c * chunk
                source = (first % cols_here // chunk) * nc + first // cols_here
                to_rows.append((source, r * nc + c))
        to_cols = [(b, a) for a, b in to_rows]
        square = (NB, NB)
        tall_r = (rows_here, NB)
        tall_c = (cols_here, NB)
        pair_shape_c = (cols_here, 2 * NB)
        pair_shape_r = (rows_here, 2 * NB)
        raw_rows = chunk + half

        def few(peers):
            return -(-4 * (NB // peers) // 8) * 8

        def image_round(mine, axis, targets, extra=()):
            got = swap(mine, axis)
            rows = got.shape[1] + sum(x.shape[0] for x in extra)
            blocks, image_chunk = call(
                sum_with_kernel if extra else sum_kernel, "sum_blocks",
                [(got.shape[0], rows, 2 * NB), (half, 2 * NB)], got, *extra,
            )
            return swap(blocks, axis), lax.ppermute(image_chunk, ("row", "col"), targets)

        def image_blocks(once_r, smalls):
            return jnp.concatenate([fold(tn(matrix, once_r), chunk), smalls], axis=1)

        at = half + few(nr)

        block_r = (nc, PACKED + half, 2 * NB)
        block_c = (nr, PACKED + half, 2 * NB)

        def plain():
            raw = call(
                plain_start_kernel, "plain_start", [(nc, raw_rows, 2 * NB)],
                matrix[:, : 4 * NB], statics=(chunk,),
            )
            raw_chunk = swap(raw, "col")[0]
            raw_chunk_c = lax.ppermute(raw_chunk, ("row", "col"), to_cols)
            raw_r = swap(jnp.broadcast_to(raw_chunk[None], raw.shape), "col")
            first_r, smalls = call(
                plain_first_kernel, "plain_first", [tall_r, (nr, few(nr), 2 * NB)],
                my_row, raw_r, statics=(chunk,), scalars=1,
            )
            gathered, image_chunk = image_round(
                image_blocks(first_r, smalls), "row", to_rows, (raw_chunk_c,)
            )
            inners = call(
                plain_inner_kernel, "plain_inner", [block_r],
                my_col, gathered, image_chunk, statics=(chunk, at), scalars=1,
            )
            got = swap(inners, "col")
            small_one, state_c, vec_r, factor_one, fine_one = call(
                plain_factor_kernel, "plain_factor", [(8,) + square, pair_shape_c, tall_r, square],
                my_row, my_col, gathered, first_r, statics=(chunk, half, at), scalars=2, flag=True,
            )
            pair_c, panel_c, tops, blocks = call(
                plain_cols_kernel, "plain_cols",
                [pair_shape_c, tall_c, (2,) + square, (nc, half + few(nc), 2 * NB)],
                my_col, got, small_one, state_c, gathered, matrix, statics=(chunk, at), scalars=1,
            )
            pair_r, panel_r = call(
                first_rows_kernel, "first_rows", [pair_shape_r, tall_r],
                my_row, got, small_one, vec_r, raw_r, tops, statics=(chunk,), scalars=1,
            )
            old = gathered
            gathered, image_chunk = image_round(blocks, "col", to_cols)
            current = matrix - nt(pair_r, pair_c)
            gathered, current = lax.optimization_barrier((gathered, current))
            inners = call(inner_kernel, "inner", [block_c], gathered, panel_r, image_chunk)
            got = swap(inners, "row")
            small_two, state_c, left, vectors, factors, fine_two = call(
                plain_second_kernel, "plain_second",
                [(8,) + square, pair_shape_c, pair_shape_r, (2, NB, rows_here), (2,) + square],
                my_row, my_col, gathered, old, raw_r, panel_c, panel_r,
                pair_c, pair_r, factor_one, statics=(chunk, half, at), scalars=2, flag=True,
            )
            right = call(last_kernel, "last", [pair_shape_c], got, small_two, state_c)
            return (current, left, right, vectors, factors), (fine_one + fine_two)[0] == 2

        def careful():
            raw, grams = call(
                start_kernel, "start", [(nc, raw_rows, 2 * NB), (nr, PACKED, 2 * NB)],
                my_row, matrix[:, : 4 * NB], statics=(chunk,), scalars=1,
            )
            raw_chunk = swap(raw, "col")[0]
            raw_chunk_c = lax.ppermute(raw_chunk, ("row", "col"), to_cols)
            raw_r = call(
                relay_kernel, "relay", [(nc, raw_rows + PACKED, 2 * NB)], raw_chunk, swap(grams, "row")
            )
            raw_r = swap(raw_r, "col")

            root, once_r, smalls = call(
                first_once_kernel, "first_once", [square, tall_r, (nr, few(nr), 2 * NB)],
                my_row, raw_r, statics=(chunk,), scalars=1,
            )

            gathered, image_chunk_r = image_round(
                image_blocks(once_r, smalls), "row", to_rows, (raw_chunk_c,)
            )
            first_c = gathered[:, at : at + chunk, :NB].reshape(tall_c)
            once_c = nt(jnp.where(col_place >= NB, first_c, 0.0), root)
            inners = call(inner_kernel, "inner", [block_r], gathered, once_c, image_chunk_r)
            got = swap(inners, "col")
            small_one, state_c, vec_r, factor_one, _ = call(
                first_factor_kernel, "first_factor", [(8,) + square, pair_shape_c, tall_r, square],
                my_row, my_col, gathered, once_c, once_r,
                statics=(chunk, half, at), scalars=2, flag=True,
            )
            pair_c, panel_c, tops, grams = call(
                first_cols_kernel, "first_cols",
                [pair_shape_c, tall_c, (2,) + square, (nc, PACKED, 2 * NB)],
                my_col, got, small_one, state_c, gathered, statics=(chunk, at), scalars=1,
            )
            grams = swap(grams, "col")
            pair_r, panel_r = call(
                first_rows_kernel, "first_rows", [pair_shape_r, tall_r],
                my_row, got, small_one, vec_r, raw_r, tops, statics=(chunk,), scalars=1,
            )

            root, once_r, smalls = call(
                second_once_kernel, "second_once", [square, tall_r, (nr, few(nr), 2 * NB)],
                my_row, grams, raw_r, panel_r, pair_r, statics=(chunk,), scalars=1,
            )
            old = gathered
            gathered, image_chunk_r = image_round(image_blocks(once_r, smalls), "row", to_rows)
            once_c = nt(panel_c, root)
            current = matrix - nt(pair_r, pair_c)
            inners = call(inner_kernel, "inner", [block_r], gathered, once_c, image_chunk_r)
            got = swap(inners, "col")
            small_two, right, state_r, vectors, factors = call(
                second_factor_kernel, "second_factor",
                [(8,) + square, pair_shape_c, pair_shape_r, (2, NB, rows_here), (2,) + square],
                my_row, my_col, gathered, old, raw_r, once_c, once_r, pair_c, pair_r, factor_one,
                statics=(chunk, half, at), scalars=2,
            )
            left = call(last_kernel, "last", [pair_shape_r], got, small_two, state_r)
            return current - nt(left, right), vectors, factors

        ready, fine = plain()

        def finish(current, left, right, vectors, factors):
            return current - nt(left, right), vectors, factors

        banded, vectors, factors = lax.cond(fine, finish, lambda *_: careful(), *ready)
        return banded, vectors.transpose(0, 2, 1), factors

    return jax.shard_map(
        local,
        mesh=mesh,
        in_specs=(P("row", "col"),),
        out_specs=(P("row", "col"), P(None, "row", None), P()),
        check_vma=False,
    )
```

```python
import functools

import jax
import jax.numpy as jnp
from jax import lax
from jax.experimental import pallas as pl
from jax.experimental.pallas import tpu as pltpu
from jax.sharding import PartitionSpec as P

NB = 64
precise = lax.Precision.HIGHEST


def nn(a, b):
    return lax.dot_general(
        a, b, (((1,), (0,)), ((), ())), precision=precise, preferred_element_type=jnp.float32
    )


def tn(a, b):
    return lax.dot_general(
        a, b, (((0,), (0,)), ((), ())), precision=precise, preferred_element_type=jnp.float32
    )


def nt(a, b):
    return lax.dot_general(
        a, b, (((1,), (1,)), ((), ())), precision=precise, preferred_element_type=jnp.float32
    )


def places():
    sub = lax.broadcasted_iota(jnp.int32, (NB, 2 * NB), 0)
    lane = lax.broadcasted_iota(jnp.int32, (NB, 2 * NB), 1)
    return sub, lane


def inverse_root(gram):
    sub, lane = places()
    eye = (sub + NB == lane).astype(jnp.float32)
    work = jnp.concatenate([gram, jnp.zeros_like(gram)], axis=1) + eye
    scales = jnp.zeros((NB, 2 * NB), jnp.float32)
    for step in range(0, NB, 2):
        first = work[step : step + 1]
        second = work[step + 1 : step + 2]
        left = jnp.broadcast_to(work[:, step : step + 1], work.shape)
        right = jnp.broadcast_to(work[:, step + 1 : step + 2], work.shape)
        a, b = left[step : step + 1], right[step : step + 1]
        c, d = left[step + 1 : step + 2], right[step + 1 : step + 2]
        inverse = 1.0 / a
        det = a * d - b * c
        last = a * (1.0 / det)
        second = second - (c * inverse) * first
        scales = jnp.where(sub == step, a, jnp.where(sub == step + 1, det * inverse, scales))
        second_scaled = second * last
        first_scaled = first * inverse - (b * inverse) * second_scaled
        change = left * first_scaled + right * second_scaled
        work = jnp.where(sub > step + 1, work - change, jnp.where(sub == step + 1, second, work))
    return (work * lax.rsqrt(scales))[:, NB:]


def signed_lu(negated_top):
    sub, lane = places()
    eye = (sub + NB == lane).astype(jnp.float32)
    work = jnp.concatenate([negated_top, jnp.zeros_like(negated_top)], axis=1) + eye
    lower = jnp.zeros((NB, 2 * NB), jnp.float32)
    upper = jnp.zeros((NB, 2 * NB), jnp.float32)
    signs = jnp.zeros((1, 2 * NB), jnp.float32)
    lane_row = lax.broadcasted_iota(jnp.int32, (1, 2 * NB), 1)
    for step in range(0, NB, 2):
        left = jnp.broadcast_to(work[:, step : step + 1], work.shape)
        right = jnp.broadcast_to(work[:, step + 1 : step + 2], work.shape)
        raw, b = left[step : step + 1], right[step : step + 1]
        c, d = left[step + 1 : step + 2], right[step + 1 : step + 2]
        flip = jnp.where(raw > 0, 1.0, -1.0)
        a = raw + flip
        raw_det = a * d - b * c
        flip_last = jnp.where(raw_det * flip > 0, 1.0, -1.0)
        det = raw_det + flip_last * a
        inverse = 1.0 / a
        last = a * (1.0 / det)
        signs = jnp.where(lane_row == step, flip, jnp.where(lane_row == step + 1, flip_last, signs))
        first = jnp.where(lane_row == step, a, work[step : step + 1])
        second = work[step + 1 : step + 2] - (c * inverse) * first
        second = jnp.where(lane_row == step + 1, det * inverse, second)
        upper = jnp.where(
            (sub == step) & (lane >= step), first,
            jnp.where((sub == step + 1) & (lane > step), second, upper),
        )
        second_scaled = second * last
        second_scaled = jnp.where(lane_row == step, 0.0, second_scaled)
        ratio = b * inverse
        first_scaled = first * inverse - ratio * second_scaled
        below_first = jnp.where(sub > step, left * inverse, jnp.where(sub == step, 1.0, 0.0))
        below_last = (right - left * ratio) * last
        below_last = jnp.where(sub > step + 1, below_last, jnp.where(sub == step + 1, 1.0, 0.0))
        lower = jnp.where(lane == step, below_first, jnp.where(lane == step + 1, below_last, lower))
        change = left * first_scaled + right * second_scaled
        work = jnp.where(
            sub == step, first_scaled, jnp.where(sub == step + 1, second_scaled, work - change)
        )
    return lower[:, :NB], upper[:, :NB], work[:, NB:], signs[:, :NB]


def near_root(gram):
    sub = lax.broadcasted_iota(jnp.int32, (NB, NB), 0)
    lane = lax.broadcasted_iota(jnp.int32, (NB, NB), 1)
    eye = (sub == lane).astype(jnp.float32)
    off = gram - eye
    first_order = eye - jnp.where(sub > lane, off, jnp.where(sub == lane, 0.5 * off, 0.0))
    close = jnp.sum(off * off) < 2e-8
    return lax.cond(close, lambda: first_order, lambda: inverse_root(gram))


def fold(x, chunk):
    x = x.reshape(-1, chunk, NB)
    return jnp.concatenate([x[:, : chunk // 2], x[:, chunk // 2 :]], axis=2)


def unfold(x):
    return jnp.concatenate([x[:, :, :NB], x[:, :, NB:]], axis=1).reshape(-1, NB)


def pack_symmetric(g):
    h = NB // 2
    rows = []
    for quadrant in (g[:h, :h], g[:h, h:], g[h:, h:]):
        rows.append(jnp.concatenate([quadrant[k : k + 8] for k in range(0, h, 8)], axis=1))
    return jnp.concatenate(rows, axis=0)


def unpack_symmetric(x):
    h = NB // 2
    first, cross, last = [
        jnp.concatenate([x[q : q + 8, k : k + h] for k in range(0, 4 * h, h)], axis=0)
        for q in (0, 8, 16)
    ]
    upper = jnp.concatenate([first, cross], axis=1)
    return jnp.concatenate([upper, jnp.concatenate([cross.T, last], axis=1)], axis=0)


PACKED = 24


def put_pairs(out_ref, pairs, first=0):
    peers, rows = out_ref.shape[:2]
    per = NB // peers
    for q, pair in enumerate(pairs):
        for t in range(per):
            out_ref[:, first + q * per + t, :] = pair[t * peers : (t + 1) * peers]
    for k in range(first + len(pairs) * per, rows):
        out_ref[:, k, :] = jnp.zeros((peers, 2 * NB), jnp.float32)


def get_pairs(ref, first, count):
    per = NB // ref.shape[0]
    pairs = []
    for q in range(count):
        slots = [ref[:, first + q * per + t, :] for t in range(per)]
        pair = jnp.concatenate(slots, axis=0)
        pairs += [pair[:, :NB], pair[:, NB:]]
    return pairs


def beside(*parts):
    return jnp.concatenate(parts, axis=1)


def below(x, index, start):
    place = lax.broadcasted_iota(jnp.int32, x.shape, 0)
    return jnp.where((place >= start) | (index > 0), x, 0.0)


def plain_start_kernel(chunk, matrix_ref, raw_ref):
    raw_ref[:, :chunk, :] = matrix_ref[:, : 2 * NB].reshape(-1, chunk, 2 * NB)
    raw_ref[:, chunk:, :] = fold(matrix_ref[:, 2 * NB : 3 * NB], chunk)


def start_kernel(chunk, index_ref, matrix_ref, raw_ref, out_ref):
    plain_start_kernel(chunk, matrix_ref, raw_ref)
    panel = below(matrix_ref[:, :NB], index_ref[0], NB)
    packed = pack_symmetric(tn(panel, panel))
    out_ref[...] = jnp.broadcast_to(packed[None], out_ref.shape)


def relay_kernel(raw_ref, got_ref, out_ref):
    block = jnp.concatenate([raw_ref[...], jnp.sum(got_ref[...], axis=0)], axis=0)
    out_ref[...] = jnp.broadcast_to(block[None], out_ref.shape)


def pair_raw(raw_ref, chunk, at=0):
    return raw_ref[:, at : at + chunk, :].reshape(-1, 2 * NB)


def last_raw(raw_ref, chunk, at=0):
    return unfold(raw_ref[:, at + chunk : at + chunk + chunk // 2, :])


def first_pairs(chunk, index, raw_ref, root, once_ref, small_ref):
    pair = pair_raw(raw_ref, chunk)
    following = pair[:, NB:]
    once = below(pair[:, :NB], index, NB)
    if root is not None:
        once = nt(once, root)
    once_ref[...] = once
    last = last_raw(raw_ref, chunk)
    gram = tn(once, once)
    image_top = tn(following, once)

    def top(x, k):
        return jnp.where(index == 0, x[k * NB : (k + 1) * NB], 0.0)

    put_pairs(
        small_ref,
        [
            beside(gram, image_top),
            beside(top(once, 1), top(following, 1)),
            beside(top(last, 2), jnp.zeros((NB, NB), jnp.float32)),
        ],
    )


def plain_first_kernel(chunk, index_ref, raw_ref, panel_ref, small_ref):
    first_pairs(chunk, index_ref[0], raw_ref, None, panel_ref, small_ref)


def first_once_kernel(chunk, index_ref, raw_ref, root_ref, once_ref, small_ref):
    root = inverse_root(unpack_symmetric(raw_ref[0, chunk + chunk // 2 :, :]))
    root_ref[...] = root
    first_pairs(chunk, index_ref[0], raw_ref, root, once_ref, small_ref)


def second_pairs(index, once, last, vec, wide, small_ref, first=0):
    def top(x):
        return jnp.where(index == 0, x[2 * NB : 3 * NB], 0.0)

    put_pairs(
        small_ref,
        [
            beside(tn(once, once), tn(last, once)),
            beside(tn(vec, once), tn(wide, once)),
            beside(top(once), top(vec)),
            beside(top(wide), jnp.zeros((NB, NB), jnp.float32)),
        ],
        first,
    )


def second_once_kernel(
    chunk, index_ref, got_ref, raw_ref, panel_ref, pair_ref, root_ref, once_ref, small_ref
):
    root = inverse_root(unpack_symmetric(jnp.sum(got_ref[...], axis=0)))
    root_ref[...] = root
    once = nt(panel_ref[...], root)
    once_ref[...] = once
    last = last_raw(raw_ref, chunk)
    second_pairs(index_ref[0], once, last, pair_ref[:, :NB], pair_ref[:, NB:], small_ref)


def sum_kernel(got_ref, out_ref, chunk_ref):
    summed = jnp.sum(got_ref[...], axis=0)
    out_ref[...] = jnp.broadcast_to(summed[None], out_ref.shape)
    chunk_ref[...] = summed[: chunk_ref.shape[0]]


def sum_with_kernel(got_ref, raw_ref, out_ref, chunk_ref):
    summed = jnp.sum(got_ref[...], axis=0)
    block = jnp.concatenate([summed, raw_ref[...]], axis=0)
    out_ref[...] = jnp.broadcast_to(block[None], out_ref.shape)
    chunk_ref[...] = summed[: chunk_ref.shape[0]]


def inner_kernel(gathered_ref, once_ref, chunk_ref, out_ref):
    half = chunk_ref.shape[0]
    inner = tn(once_ref[...], unfold(gathered_ref[:, :half, :]))
    block = jnp.concatenate([pack_symmetric(inner), chunk_ref[...]], axis=0)
    out_ref[...] = jnp.broadcast_to(block[None], out_ref.shape)


def plain_inner_kernel(chunk, at, col_ref, gathered_ref, chunk_ref, out_ref):
    half = chunk_ref.shape[0]
    panel = below(pair_raw(gathered_ref, chunk, at)[:, :NB], col_ref[0], NB)
    inner = tn(panel, unfold(gathered_ref[:, :half, :]))
    block = jnp.concatenate([pack_symmetric(inner), chunk_ref[...]], axis=0)
    out_ref[...] = jnp.broadcast_to(block[None], out_ref.shape)


PICK, COEF, PICK_T, COEF_T, LOWER, FACTOR, INNER, WIDE = range(8)


def factor_small(near, gram, top, next_top, image_top, small_ref):
    root = near_root(gram) if near else inverse_root(gram)
    lower, upper, inverse, signs = signed_lu(-nt(top, root))
    sub = lax.broadcasted_iota(jnp.int32, (NB, NB), 0)
    lane = lax.broadcasted_iota(jnp.int32, (NB, NB), 1)
    triangle = lane >= sub
    upper_inverse = jnp.where(triangle, nn(inverse, lower), 0.0)
    lower_inverse = nn(upper, inverse)
    factor = jnp.where(triangle, nt(upper * signs, lower_inverse), 0.0)
    pick = nn(jnp.where(sub == lane, signs, 0.0), upper_inverse)
    coef = tn(root, upper_inverse)
    crossed = tn(pick, nn(image_top, coef))
    pick_t = nn(pick, factor)
    coef_t = nn(coef, factor)
    small_ref[PICK] = pick
    small_ref[COEF] = coef
    small_ref[PICK_T] = pick_t
    small_ref[COEF_T] = coef_t
    small_ref[LOWER] = lower
    small_ref[FACTOR] = factor
    small_ref[INNER] = tn(pick, nn(next_top, pick)) - crossed - crossed.T
    small_ref[WIDE] = nn(next_top, pick_t) - nn(image_top, coef_t)
    sizes = jnp.sum(jnp.where(sub == lane, gram, 0.0), axis=0, keepdims=True)
    fine = jnp.sum(root * root * sizes) < 1.5 * NB
    return pick, coef, pick_t, coef_t, fine


def vectors_of(once, index, start, pick, coef):
    vec = -nn(once, coef)
    top = vec[start : start + NB] + jnp.where(index == 0, pick, 0.0)
    return jnp.concatenate([vec[:start], top, vec[start + NB :]], axis=0)


def half_core(small_ref, inner):
    coef = small_ref[COEF]
    factor = small_ref[FACTOR]
    inner = small_ref[INNER] + tn(coef, nn(inner, coef))
    return 0.5 * tn(factor, nn(inner, factor))


def first_factor(near, chunk, half, at, row, col, gathered_ref, once_c, once_r, outs):
    small_ref, state_ref, vec_ref, factor_ref, fine_ref = outs
    gram, image_top, top, next_top, _, _ = get_pairs(gathered_ref, half, 3)
    pick, coef, pick_t, coef_t, fine = factor_small(
        near, gram, top, next_top, image_top, small_ref
    )
    fine_ref[0] = jnp.where(fine, 1, 0)
    factor_ref[...] = small_ref[FACTOR]
    vec_ref[...] = vectors_of(once_r, row, NB, pick, coef)
    following = pair_raw(gathered_ref, chunk, at)[:, NB:]
    image = unfold(gathered_ref[:, :half, :])
    vec = vectors_of(once_c, col, NB, pick, coef)
    state_ref[...] = beside(vec, nn(following, pick_t) - nn(image, coef_t))


def first_factor_kernel(
    chunk, half, at, row_ref, col_ref, gathered_ref, once_c_ref, once_r_ref, *outs
):
    first_factor(
        True, chunk, half, at, row_ref[0], col_ref[0], gathered_ref,
        once_c_ref[...], once_r_ref[...], outs,
    )


def plain_factor_kernel(chunk, half, at, row_ref, col_ref, gathered_ref, panel_r_ref, *outs):
    panel = below(pair_raw(gathered_ref, chunk, at)[:, :NB], col_ref[0], NB)
    first_factor(
        False, chunk, half, at, row_ref[0], col_ref[0], gathered_ref, panel, panel_r_ref[...], outs
    )


def second_panel(following, vec, wide, wide_top, lower, index):
    return below(following - nt(vec, wide_top) - nt(wide, lower), index, 2 * NB)


def first_cols(
    chunk, at, index, got_ref, small_ref, state_ref, raw_ref, pair_ref, panel_ref, tops_ref
):
    half = half_core(small_ref, unpack_symmetric(jnp.sum(got_ref[:, :PACKED, :], axis=0)))
    lower = small_ref[LOWER]
    wide_top = small_ref[WIDE] - nn(lower, half)
    tops_ref[0] = half
    tops_ref[1] = wide_top
    vec = state_ref[:, :NB]
    wide = state_ref[:, NB:] - nn(vec, half)
    pair_ref[...] = beside(wide, vec)
    following = pair_raw(raw_ref, chunk, at)[:, NB:]
    panel = second_panel(following, vec, wide, wide_top, lower, index)
    panel_ref[...] = panel
    return panel, vec, wide


def first_cols_kernel(
    chunk, at, col_ref, got_ref, small_ref, state_ref, raw_ref,
    pair_ref, panel_ref, tops_ref, out_ref,
):
    panel, _, _ = first_cols(
        chunk, at, col_ref[0], got_ref, small_ref, state_ref, raw_ref,
        pair_ref, panel_ref, tops_ref,
    )
    packed = pack_symmetric(tn(panel, panel))
    out_ref[...] = jnp.broadcast_to(packed[None], out_ref.shape)


def plain_cols_kernel(
    chunk, at, col_ref, got_ref, small_ref, state_ref, raw_ref, matrix_ref,
    pair_ref, panel_ref, tops_ref, out_ref,
):
    panel, vec, wide = first_cols(
        chunk, at, col_ref[0], got_ref, small_ref, state_ref, raw_ref,
        pair_ref, panel_ref, tops_ref,
    )
    half = chunk // 2
    out_ref[:, :half, :] = fold(nn(matrix_ref[...], panel), chunk)
    last = last_raw(raw_ref, chunk, at)
    second_pairs(col_ref[0], panel, last, vec, wide, out_ref, half)


def first_rows_kernel(
    chunk, row_ref, got_ref, small_ref, vec_ref, raw_ref, tops_ref, pair_ref, panel_ref
):
    image = unfold(got_ref[:, PACKED:, :])
    following = pair_raw(raw_ref, chunk)[:, NB:]
    vec = vec_ref[...]
    wide = nn(following, small_ref[PICK_T]) - nn(image, small_ref[COEF_T]) - nn(vec, tops_ref[0])
    pair_ref[...] = beside(vec, wide)
    panel_ref[...] = second_panel(following, vec, wide, tops_ref[1], small_ref[LOWER], row_ref[0])


def second_small(near, half, old_half, gathered_ref, old_ref, factor_ref, small_ref, factors_ref):
    gram, image_top, vec_dot, wide_dot, top, vec_top, wide_top, _ = get_pairs(
        gathered_ref, half, 4
    )
    last_top = get_pairs(old_ref, old_half, 3)[4]
    image_top = image_top - nn(vec_top, wide_dot) - nn(wide_top, vec_dot)
    crossed = nt(vec_top, wide_top)
    next_top = last_top - crossed - crossed.T
    pick, coef, pick_t, coef_t, fine = factor_small(
        near, gram, top, next_top, image_top, small_ref
    )
    crossed = tn(nn(vec_dot, coef), nn(wide_dot, coef))
    small_ref[INNER] -= crossed + crossed.T
    factors_ref[0] = factor_ref[...]
    factors_ref[1] = small_ref[FACTOR]
    vec_dots = nn(wide_dot, coef_t) - tn(wide_top, pick_t)
    wide_dots = nn(vec_dot, coef_t) - tn(vec_top, pick_t)
    return pick, coef, pick_t, coef_t, vec_dots, wide_dots, fine


def second_factor_kernel(
    chunk, half, at, row_ref, col_ref, gathered_ref, old_ref, raw_r_ref,
    once_c_ref, once_r_ref, pair_c_ref, pair_r_ref, factor_ref,
    small_ref, right_ref, state_ref, vectors_ref, factors_ref,
):
    pick, coef, pick_t, coef_t, vec_dots, wide_dots, _ = second_small(
        True, half, half, gathered_ref, old_ref, factor_ref, small_ref, factors_ref
    )
    new = vectors_of(once_r_ref[...], row_ref[0], 2 * NB, pick, coef)
    vec = pair_r_ref[:, :NB]
    vectors_ref[0] = vec.T
    vectors_ref[1] = new.T
    part = nn(last_raw(raw_r_ref, chunk), pick_t)
    part += nn(vec, vec_dots) + nn(pair_r_ref[:, NB:], wide_dots)
    state_ref[...] = beside(new, part)
    new = vectors_of(once_c_ref[...], col_ref[0], 2 * NB, pick, coef)
    part = nn(last_raw(old_ref, chunk, at), pick_t) - nn(unfold(gathered_ref[:, :half, :]), coef_t)
    part += nn(pair_c_ref[:, NB:], vec_dots) + nn(pair_c_ref[:, :NB], wide_dots)
    right_ref[...] = beside(part, new)


def plain_second_kernel(
    chunk, half, at, row_ref, col_ref, gathered_ref, old_ref, raw_r_ref,
    panel_c_ref, panel_r_ref, pair_c_ref, pair_r_ref, factor_ref,
    small_ref, state_ref, left_ref, vectors_ref, factors_ref, fine_ref,
):
    pick, coef, pick_t, coef_t, vec_dots, wide_dots, fine = second_small(
        False, half, half, gathered_ref, old_ref, factor_ref, small_ref, factors_ref
    )
    fine_ref[0] = jnp.where(fine, 1, 0)
    new = vectors_of(panel_r_ref[...], row_ref[0], 2 * NB, pick, coef)
    vec = pair_r_ref[:, :NB]
    vectors_ref[0] = vec.T
    vectors_ref[1] = new.T
    part = nn(last_raw(raw_r_ref, chunk), pick_t) - nn(unfold(gathered_ref[:, :half, :]), coef_t)
    part += nn(vec, vec_dots) + nn(pair_r_ref[:, NB:], wide_dots)
    left_ref[...] = beside(part, new)
    new = vectors_of(panel_c_ref[...], col_ref[0], 2 * NB, pick, coef)
    part = nn(last_raw(old_ref, chunk, at), pick_t)
    part += nn(pair_c_ref[:, NB:], vec_dots) + nn(pair_c_ref[:, :NB], wide_dots)
    state_ref[...] = beside(new, part)


def last_kernel(got_ref, small_ref, state_ref, out_ref):
    half = half_core(small_ref, unpack_symmetric(jnp.sum(got_ref[:, :PACKED, :], axis=0)))
    new = state_ref[:, :NB]
    image = unfold(got_ref[:, PACKED:, :])
    wide = state_ref[:, NB:] - nn(image, small_ref[COEF_T]) - nn(new, half + half.T)
    out_ref[...] = beside(new, wide)


class FarIn:
    def __init__(self, ref, buffer, semaphore):
        self.buffer = buffer
        self.copy = pltpu.make_async_copy(ref, buffer, semaphore)
        self.copy.start()
        self.here = False

    def __getitem__(self, index):
        if not self.here:
            self.copy.wait()
            self.here = True
        return self.buffer[index]


class FarOut:
    def __init__(self, ref, buffer, semaphore):
        self.buffer = buffer
        self.copy = pltpu.make_async_copy(buffer, ref, semaphore)

    def __setitem__(self, index, value):
        self.buffer[index] = value
        self.copy.start()


def call(kernel, name, outs, *args, statics=(), scalars=0, flag=False, far_in=(), far_out=()):
    in_smem = pl.BlockSpec(memory_space=pltpu.SMEM)
    in_vmem = pl.BlockSpec(memory_space=pltpu.VMEM)
    in_hbm = pl.BlockSpec(memory_space=pltpu.HBM)
    in_specs = [in_smem if k < scalars else in_vmem for k in range(len(args))]
    out_shape = [jax.ShapeDtypeStruct(shape, jnp.float32) for shape in outs]
    out_specs = [in_vmem] * len(outs)
    if flag:
        out_shape.append(jax.ShapeDtypeStruct((1,), jnp.int32))
        out_specs.append(in_smem)
    buffers = []
    for k in far_in:
        in_specs[k] = in_hbm
        buffers.append(pltpu.VMEM(args[k].shape, jnp.float32))
    for k in far_out:
        out_specs[k] = in_hbm
        buffers.append(pltpu.VMEM(outs[k], jnp.float32))
    far = [*far_in, *[len(args) + k for k in far_out]]

    def body(*refs):
        refs = list(refs)
        if far:
            *refs, semaphores = refs
            held = refs[len(refs) - len(far) :]
            refs = refs[: len(refs) - len(far)]
            for slot, k in enumerate(far):
                kind = FarIn if k < len(args) else FarOut
                refs[k] = kind(refs[k], held[slot], semaphores.at[slot])
        kernel(*statics, *refs)
        for k in far:
            if k >= len(args):
                refs[k].copy.wait()

    result = pl.pallas_call(
        body,
        out_shape=out_shape,
        in_specs=in_specs,
        out_specs=out_specs,
        scratch_shapes=[*buffers, pltpu.SemaphoreType.DMA((len(far),))] if far else [],
        compiler_params=pltpu.CompilerParams(vmem_limit_bytes=16 << 20),
        cost_estimate=pl.CostEstimate(flops=1 << 24, bytes_accessed=1 << 22, transcendentals=0),
        name=name,
    )(*args)
    return result[0] if len(result) == 1 else result


def swap(x, axis):
    return lax.all_to_all(x, axis, 0, 0)


def solution(mesh):
    nr = mesh.shape["row"]
    nc = mesh.shape["col"]

    def local(matrix):
        rows_here, cols_here = matrix.shape
        chunk = rows_here // nc
        half = chunk // 2
        my_row = lax.axis_index("row").astype(jnp.int32).reshape(1)
        my_col = lax.axis_index("col").astype(jnp.int32).reshape(1)
        col_place = (lax.axis_index("col") * cols_here + jnp.arange(cols_here))[:, None]
        to_rows = []
        for r in range(nr):
            for c in range(nc):
                first = r * rows_here + c * chunk
                source = (first % cols_here // chunk) * nc + first // cols_here
                to_rows.append((source, r * nc + c))
        to_cols = [(b, a) for a, b in to_rows]
        square = (NB, NB)
        tall_r = (rows_here, NB)
        tall_c = (cols_here, NB)
        pair_shape_c = (cols_here, 2 * NB)
        pair_shape_r = (rows_here, 2 * NB)
        raw_rows = chunk + half

        def few(peers):
            return -(-4 * (NB // peers) // 8) * 8

        def image_round(mine, axis, targets, extra=(), beside=()):
            got, *beside = lax.optimization_barrier((swap(mine, axis), *beside))
            rows = got.shape[1] + sum(x.shape[0] for x in extra)
            blocks, image_chunk = call(
                sum_with_kernel if extra else sum_kernel, "sum_blocks",
                [(got.shape[0], rows, 2 * NB), (half, 2 * NB)], got, *extra,
            )
            return swap(blocks, axis), lax.ppermute(image_chunk, ("row", "col"), targets), *beside

        def image_blocks(once_r, smalls):
            return jnp.concatenate([fold(tn(matrix, once_r), chunk), smalls], axis=1)

        at = half + few(nr)

        block_r = (nc, PACKED + half, 2 * NB)
        block_c = (nr, PACKED + half, 2 * NB)

        def plain():
            raw = pl.pallas_call(
                functools.partial(plain_start_kernel, chunk),
                grid=(1,),
                in_specs=[pl.BlockSpec((rows_here, 4 * NB), lambda _: (0, 0))],
                out_specs=pl.BlockSpec((nc, raw_rows, 2 * NB), lambda _: (0, 0, 0)),
                out_shape=jax.ShapeDtypeStruct((nc, raw_rows, 2 * NB), jnp.float32),
                name="plain_start",
            )(matrix)
            raw_chunk = swap(raw, "col")[0]
            raw_chunk_c = lax.ppermute(raw_chunk, ("row", "col"), to_cols)
            raw_r = swap(jnp.broadcast_to(raw_chunk[None], raw.shape), "col")
            first_r, smalls = call(
                plain_first_kernel, "plain_first", [tall_r, (nr, few(nr), 2 * NB)],
                my_row, raw_r, statics=(chunk,), scalars=1,
            )
            gathered, image_chunk = image_round(
                image_blocks(first_r, smalls), "row", to_rows, (raw_chunk_c,)
            )
            inners = call(
                plain_inner_kernel, "plain_inner", [block_r],
                my_col, gathered, image_chunk, statics=(chunk, at), scalars=1,
            )
            got = swap(inners, "col")
            small_one, state_c, vec_r, factor_one, fine_one = call(
                plain_factor_kernel, "plain_factor", [(8,) + square, pair_shape_c, tall_r, square],
                my_row, my_col, gathered, first_r, statics=(chunk, half, at), scalars=2, flag=True,
                far_out=(1, 2, 3),
            )
            pair_c, panel_c, tops, blocks = call(
                plain_cols_kernel, "plain_cols",
                [pair_shape_c, tall_c, (2,) + square, (nc, half + few(nc), 2 * NB)],
                my_col, got, small_one, state_c, gathered, matrix, statics=(chunk, at), scalars=1,
                far_in=(3,), far_out=(1,),
            )
            pair_r, panel_r = call(
                first_rows_kernel, "first_rows", [pair_shape_r, tall_r],
                my_row, got, small_one, vec_r, raw_r, tops, statics=(chunk,), scalars=1,
                far_in=(3,), far_out=(1,),
            )
            current = matrix - nt(pair_r, pair_c)
            old = gathered
            gathered, image_chunk, current, pair_r, panel_r = image_round(
                blocks, "col", to_cols, beside=(current, pair_r, panel_r)
            )
            inners = call(
                inner_kernel, "inner", [block_c], gathered, panel_r, image_chunk, far_in=(1,)
            )
            got = swap(inners, "row")
            small_two, state_c, left, vectors, factors, fine_two = call(
                plain_second_kernel, "plain_second",
                [(8,) + square, pair_shape_c, pair_shape_r, (2, NB, rows_here), (2,) + square],
                my_row, my_col, gathered, old, raw_r, panel_c, panel_r,
                pair_c, pair_r, factor_one, statics=(chunk, half, at), scalars=2, flag=True,
                far_in=(5, 6, 9), far_out=(1,),
            )
            right = call(
                last_kernel, "last", [pair_shape_c], got, small_two, state_c, far_in=(2,)
            )
            return (current, left, right, vectors, factors), (fine_one + fine_two)[0] == 2

        def careful():
            raw, grams = call(
                start_kernel, "start", [(nc, raw_rows, 2 * NB), (nr, PACKED, 2 * NB)],
                my_row, matrix[:, : 4 * NB], statics=(chunk,), scalars=1,
            )
            raw_chunk = swap(raw, "col")[0]
            raw_chunk_c = lax.ppermute(raw_chunk, ("row", "col"), to_cols)
            raw_r = call(
                relay_kernel, "relay", [(nc, raw_rows + PACKED, 2 * NB)], raw_chunk, swap(grams, "row")
            )
            raw_r = swap(raw_r, "col")

            root, once_r, smalls = call(
                first_once_kernel, "first_once", [square, tall_r, (nr, few(nr), 2 * NB)],
                my_row, raw_r, statics=(chunk,), scalars=1,
            )

            gathered, image_chunk_r = image_round(
                image_blocks(once_r, smalls), "row", to_rows, (raw_chunk_c,)
            )
            first_c = gathered[:, at : at + chunk, :NB].reshape(tall_c)
            once_c = nt(jnp.where(col_place >= NB, first_c, 0.0), root)
            inners = call(inner_kernel, "inner", [block_r], gathered, once_c, image_chunk_r)
            got = swap(inners, "col")
            small_one, state_c, vec_r, factor_one, _ = call(
                first_factor_kernel, "first_factor", [(8,) + square, pair_shape_c, tall_r, square],
                my_row, my_col, gathered, once_c, once_r,
                statics=(chunk, half, at), scalars=2, flag=True,
            )
            pair_c, panel_c, tops, grams = call(
                first_cols_kernel, "first_cols",
                [pair_shape_c, tall_c, (2,) + square, (nc, PACKED, 2 * NB)],
                my_col, got, small_one, state_c, gathered, statics=(chunk, at), scalars=1,
            )
            grams = swap(grams, "col")
            pair_r, panel_r = call(
                first_rows_kernel, "first_rows", [pair_shape_r, tall_r],
                my_row, got, small_one, vec_r, raw_r, tops, statics=(chunk,), scalars=1,
            )

            root, once_r, smalls = call(
                second_once_kernel, "second_once", [square, tall_r, (nr, few(nr), 2 * NB)],
                my_row, grams, raw_r, panel_r, pair_r, statics=(chunk,), scalars=1,
            )
            old = gathered
            gathered, image_chunk_r = image_round(image_blocks(once_r, smalls), "row", to_rows)
            once_c = nt(panel_c, root)
            current = matrix - nt(pair_r, pair_c)
            inners = call(inner_kernel, "inner", [block_r], gathered, once_c, image_chunk_r)
            got = swap(inners, "col")
            small_two, right, state_r, vectors, factors = call(
                second_factor_kernel, "second_factor",
                [(8,) + square, pair_shape_c, pair_shape_r, (2, NB, rows_here), (2,) + square],
                my_row, my_col, gathered, old, raw_r, once_c, once_r, pair_c, pair_r, factor_one,
                statics=(chunk, half, at), scalars=2,
            )
            left = call(last_kernel, "last", [pair_shape_r], got, small_two, state_r)
            return current - nt(left, right), vectors, factors

        ready, fine = plain()

        def finish(current, left, right, vectors, factors):
            return current - nt(left, right), vectors, factors

        banded, vectors, factors = lax.cond(fine, finish, lambda *_: careful(), *ready)
        return banded, vectors.transpose(0, 2, 1), factors

    return jax.shard_map(
        local,
        mesh=mesh,
        in_specs=(P("row", "col"),),
        out_specs=(P("row", "col"), P(None, "row", None), P()),
        check_vma=False,
    )
```

```python
import functools

import jax
import jax.numpy as jnp
from jax import lax
from jax.experimental import pallas as pl
from jax.experimental.pallas import tpu as pltpu
from jax.sharding import PartitionSpec as P

NB = 64
precise = lax.Precision.HIGHEST


def nn(a, b):
    return lax.dot_general(
        a, b, (((1,), (0,)), ((), ())), precision=precise, preferred_element_type=jnp.float32
    )


def tn(a, b):
    return lax.dot_general(
        a, b, (((0,), (0,)), ((), ())), precision=precise, preferred_element_type=jnp.float32
    )


def nt(a, b):
    return lax.dot_general(
        a, b, (((1,), (1,)), ((), ())), precision=precise, preferred_element_type=jnp.float32
    )


def places():
    sub = lax.broadcasted_iota(jnp.int32, (NB, 2 * NB), 0)
    lane = lax.broadcasted_iota(jnp.int32, (NB, 2 * NB), 1)
    return sub, lane


def inverse_root(gram):
    sub, lane = places()
    eye = (sub + NB == lane).astype(jnp.float32)
    work = jnp.concatenate([gram, jnp.zeros_like(gram)], axis=1) + eye
    scales = jnp.zeros((NB, 2 * NB), jnp.float32)
    for step in range(0, NB, 2):
        first = work[step : step + 1]
        second = work[step + 1 : step + 2]
        left = jnp.broadcast_to(work[:, step : step + 1], work.shape)
        right = jnp.broadcast_to(work[:, step + 1 : step + 2], work.shape)
        a, b = left[step : step + 1], right[step : step + 1]
        c, d = left[step + 1 : step + 2], right[step + 1 : step + 2]
        inverse = 1.0 / a
        det = a * d - b * c
        last = a * (1.0 / det)
        second = second - (c * inverse) * first
        scales = jnp.where(sub == step, a, jnp.where(sub == step + 1, det * inverse, scales))
        second_scaled = second * last
        first_scaled = first * inverse - (b * inverse) * second_scaled
        change = left * first_scaled + right * second_scaled
        work = jnp.where(sub > step + 1, work - change, jnp.where(sub == step + 1, second, work))
    return (work * lax.rsqrt(scales))[:, NB:]


def signed_lu(negated_top):
    sub, lane = places()
    eye = (sub + NB == lane).astype(jnp.float32)
    work = jnp.concatenate([negated_top, jnp.zeros_like(negated_top)], axis=1) + eye
    lower = jnp.zeros((NB, 2 * NB), jnp.float32)
    upper = jnp.zeros((NB, 2 * NB), jnp.float32)
    signs = jnp.zeros((1, 2 * NB), jnp.float32)
    lane_row = lax.broadcasted_iota(jnp.int32, (1, 2 * NB), 1)
    for step in range(0, NB, 2):
        left = jnp.broadcast_to(work[:, step : step + 1], work.shape)
        right = jnp.broadcast_to(work[:, step + 1 : step + 2], work.shape)
        raw, b = left[step : step + 1], right[step : step + 1]
        c, d = left[step + 1 : step + 2], right[step + 1 : step + 2]
        flip = jnp.where(raw > 0, 1.0, -1.0)
        a = raw + flip
        raw_det = a * d - b * c
        flip_last = jnp.where(raw_det * flip > 0, 1.0, -1.0)
        det = raw_det + flip_last * a
        inverse = 1.0 / a
        last = a * (1.0 / det)
        signs = jnp.where(lane_row == step, flip, jnp.where(lane_row == step + 1, flip_last, signs))
        first = jnp.where(lane_row == step, a, work[step : step + 1])
        second = work[step + 1 : step + 2] - (c * inverse) * first
        second = jnp.where(lane_row == step + 1, det * inverse, second)
        upper = jnp.where(
            (sub == step) & (lane >= step), first,
            jnp.where((sub == step + 1) & (lane > step), second, upper),
        )
        second_scaled = second * last
        second_scaled = jnp.where(lane_row == step, 0.0, second_scaled)
        ratio = b * inverse
        first_scaled = first * inverse - ratio * second_scaled
        below_first = jnp.where(sub > step, left * inverse, jnp.where(sub == step, 1.0, 0.0))
        below_last = (right - left * ratio) * last
        below_last = jnp.where(sub > step + 1, below_last, jnp.where(sub == step + 1, 1.0, 0.0))
        lower = jnp.where(lane == step, below_first, jnp.where(lane == step + 1, below_last, lower))
        change = left * first_scaled + right * second_scaled
        work = jnp.where(
            sub == step, first_scaled, jnp.where(sub == step + 1, second_scaled, work - change)
        )
    return lower[:, :NB], upper[:, :NB], work[:, NB:], signs[:, :NB]


def near_root(gram):
    sub = lax.broadcasted_iota(jnp.int32, (NB, NB), 0)
    lane = lax.broadcasted_iota(jnp.int32, (NB, NB), 1)
    eye = (sub == lane).astype(jnp.float32)
    off = gram - eye
    first_order = eye - jnp.where(sub > lane, off, jnp.where(sub == lane, 0.5 * off, 0.0))
    close = jnp.sum(off * off) < 2e-8
    return lax.cond(close, lambda: first_order, lambda: inverse_root(gram))


def fold(x, chunk):
    x = x.reshape(-1, chunk, NB)
    return jnp.concatenate([x[:, : chunk // 2], x[:, chunk // 2 :]], axis=2)


def unfold(x):
    return jnp.concatenate([x[:, :, :NB], x[:, :, NB:]], axis=1).reshape(-1, NB)


def pack_symmetric(g):
    h = NB // 2
    rows = []
    for quadrant in (g[:h, :h], g[:h, h:], g[h:, h:]):
        rows.append(jnp.concatenate([quadrant[k : k + 8] for k in range(0, h, 8)], axis=1))
    return jnp.concatenate(rows, axis=0)


def unpack_symmetric(x):
    h = NB // 2
    first, cross, last = [
        jnp.concatenate([x[q : q + 8, k : k + h] for k in range(0, 4 * h, h)], axis=0)
        for q in (0, 8, 16)
    ]
    upper = jnp.concatenate([first, cross], axis=1)
    return jnp.concatenate([upper, jnp.concatenate([cross.T, last], axis=1)], axis=0)


PACKED = 24


def put_pairs(out_ref, pairs, first=0):
    peers, rows = out_ref.shape[:2]
    per = NB // peers
    for q, pair in enumerate(pairs):
        for t in range(per):
            out_ref[:, first + q * per + t, :] = pair[t * peers : (t + 1) * peers]
    for k in range(first + len(pairs) * per, rows):
        out_ref[:, k, :] = jnp.zeros((peers, 2 * NB), jnp.float32)


def get_pairs(ref, first, count):
    per = NB // ref.shape[0]
    pairs = []
    for q in range(count):
        slots = [ref[:, first + q * per + t, :] for t in range(per)]
        pair = jnp.concatenate(slots, axis=0)
        pairs += [pair[:, :NB], pair[:, NB:]]
    return pairs


def beside(*parts):
    return jnp.concatenate(parts, axis=1)


def below(x, index, start):
    place = lax.broadcasted_iota(jnp.int32, x.shape, 0)
    return jnp.where((place >= start) | (index > 0), x, 0.0)


def plain_start_kernel(chunk, matrix_ref, raw_ref):
    raw_ref[:, :chunk, :] = matrix_ref[:, : 2 * NB].reshape(-1, chunk, 2 * NB)
    raw_ref[:, chunk:, :] = fold(matrix_ref[:, 2 * NB : 3 * NB], chunk)


def start_kernel(chunk, index_ref, matrix_ref, raw_ref, out_ref):
    plain_start_kernel(chunk, matrix_ref, raw_ref)
    panel = below(matrix_ref[:, :NB], index_ref[0], NB)
    packed = pack_symmetric(tn(panel, panel))
    out_ref[...] = jnp.broadcast_to(packed[None], out_ref.shape)


def relay_kernel(raw_ref, got_ref, out_ref):
    block = jnp.concatenate([raw_ref[...], jnp.sum(got_ref[...], axis=0)], axis=0)
    out_ref[...] = jnp.broadcast_to(block[None], out_ref.shape)


def pair_raw(raw_ref, chunk, at=0):
    return raw_ref[:, at : at + chunk, :].reshape(-1, 2 * NB)


def last_raw(raw_ref, chunk, at=0):
    return unfold(raw_ref[:, at + chunk : at + chunk + chunk // 2, :])


def first_pairs(chunk, index, raw_ref, root, once_ref, small_ref):
    pair = pair_raw(raw_ref, chunk)
    following = pair[:, NB:]
    once = below(pair[:, :NB], index, NB)
    if root is not None:
        once = nt(once, root)
    once_ref[...] = once
    last = last_raw(raw_ref, chunk)
    gram = tn(once, once)
    image_top = tn(following, once)

    def top(x, k):
        return jnp.where(index == 0, x[k * NB : (k + 1) * NB], 0.0)

    put_pairs(
        small_ref,
        [
            beside(gram, image_top),
            beside(top(once, 1), top(following, 1)),
            beside(top(last, 2), jnp.zeros((NB, NB), jnp.float32)),
        ],
    )


def plain_first_kernel(chunk, index_ref, raw_ref, panel_ref, small_ref):
    first_pairs(chunk, index_ref[0], raw_ref, None, panel_ref, small_ref)


def first_once_kernel(chunk, index_ref, raw_ref, root_ref, once_ref, small_ref):
    root = inverse_root(unpack_symmetric(raw_ref[0, chunk + chunk // 2 :, :]))
    root_ref[...] = root
    first_pairs(chunk, index_ref[0], raw_ref, root, once_ref, small_ref)


def second_pairs(index, once, last, vec, wide, small_ref, first=0):
    def top(x):
        return jnp.where(index == 0, x[2 * NB : 3 * NB], 0.0)

    put_pairs(
        small_ref,
        [
            beside(tn(once, once), tn(last, once)),
            beside(tn(vec, once), tn(wide, once)),
            beside(top(once), top(vec)),
            beside(top(wide), jnp.zeros((NB, NB), jnp.float32)),
        ],
        first,
    )


def second_once_kernel(
    chunk, index_ref, got_ref, raw_ref, panel_ref, pair_ref, root_ref, once_ref, small_ref
):
    root = inverse_root(unpack_symmetric(jnp.sum(got_ref[...], axis=0)))
    root_ref[...] = root
    once = nt(panel_ref[...], root)
    once_ref[...] = once
    last = last_raw(raw_ref, chunk)
    second_pairs(index_ref[0], once, last, pair_ref[:, :NB], pair_ref[:, NB:], small_ref)


def sum_kernel(got_ref, out_ref, chunk_ref):
    summed = jnp.sum(got_ref[...], axis=0)
    out_ref[...] = jnp.broadcast_to(summed[None], out_ref.shape)
    chunk_ref[...] = summed[: chunk_ref.shape[0]]


def sum_with_kernel(got_ref, raw_ref, out_ref, chunk_ref):
    summed = jnp.sum(got_ref[...], axis=0)
    block = jnp.concatenate([summed, raw_ref[...]], axis=0)
    out_ref[...] = jnp.broadcast_to(block[None], out_ref.shape)
    chunk_ref[...] = summed[: chunk_ref.shape[0]]


def inner_kernel(gathered_ref, once_ref, chunk_ref, out_ref):
    half = chunk_ref.shape[0]
    inner = tn(once_ref[...], unfold(gathered_ref[:, :half, :]))
    block = jnp.concatenate([pack_symmetric(inner), chunk_ref[...]], axis=0)
    out_ref[...] = jnp.broadcast_to(block[None], out_ref.shape)


def plain_inner_kernel(chunk, at, col_ref, gathered_ref, chunk_ref, out_ref):
    half = chunk_ref.shape[0]
    panel = below(pair_raw(gathered_ref, chunk, at)[:, :NB], col_ref[0], NB)
    inner = tn(panel, unfold(gathered_ref[:, :half, :]))
    block = jnp.concatenate([pack_symmetric(inner), chunk_ref[...]], axis=0)
    out_ref[...] = jnp.broadcast_to(block[None], out_ref.shape)


PICK, COEF, PICK_T, COEF_T, LOWER, FACTOR, INNER, WIDE = range(8)


def factor_small(near, gram, top, next_top, image_top, small_ref):
    root = near_root(gram) if near else inverse_root(gram)
    lower, upper, inverse, signs = signed_lu(-nt(top, root))
    sub = lax.broadcasted_iota(jnp.int32, (NB, NB), 0)
    lane = lax.broadcasted_iota(jnp.int32, (NB, NB), 1)
    triangle = lane >= sub
    upper_inverse = jnp.where(triangle, nn(inverse, lower), 0.0)
    lower_inverse = nn(upper, inverse)
    factor = jnp.where(triangle, nt(upper * signs, lower_inverse), 0.0)
    pick = nn(jnp.where(sub == lane, signs, 0.0), upper_inverse)
    coef = tn(root, upper_inverse)
    crossed = tn(pick, nn(image_top, coef))
    pick_t = nn(pick, factor)
    coef_t = nn(coef, factor)
    small_ref[PICK] = pick
    small_ref[COEF] = coef
    small_ref[PICK_T] = pick_t
    small_ref[COEF_T] = coef_t
    small_ref[LOWER] = lower
    small_ref[FACTOR] = factor
    small_ref[INNER] = tn(pick, nn(next_top, pick)) - crossed - crossed.T
    small_ref[WIDE] = nn(next_top, pick_t) - nn(image_top, coef_t)
    sizes = jnp.sum(jnp.where(sub == lane, gram, 0.0), axis=0, keepdims=True)
    fine = jnp.sum(root * root * sizes) < 1.5 * NB
    return pick, coef, pick_t, coef_t, fine


def vectors_of(once, index, start, pick, coef):
    vec = -nn(once, coef)
    top = vec[start : start + NB] + jnp.where(index == 0, pick, 0.0)
    return jnp.concatenate([vec[:start], top, vec[start + NB :]], axis=0)


def half_core(coef, factor, known, got):
    inner = known + tn(coef, nn(got, coef))
    return 0.5 * tn(factor, nn(inner, factor))


def first_factor(near, chunk, half, at, col, gathered_ref, once_c, outs):
    small_ref, state_ref, fine_ref = outs
    gram, image_top, top, next_top, _, _ = get_pairs(gathered_ref, half, 3)
    pick, coef, pick_t, coef_t, fine = factor_small(
        near, gram, top, next_top, image_top, small_ref
    )
    fine_ref[0] = jnp.where(fine, 1, 0)
    following = pair_raw(gathered_ref, chunk, at)[:, NB:]
    image = unfold(gathered_ref[:, :half, :])
    vec = vectors_of(once_c, col, NB, pick, coef)
    state_ref[...] = beside(vec, nn(following, pick_t) - nn(image, coef_t))


def first_factor_kernel(chunk, half, at, col_ref, gathered_ref, once_c_ref, *outs):
    first_factor(True, chunk, half, at, col_ref[0], gathered_ref, once_c_ref[...], outs)


def plain_factor_kernel(chunk, half, at, col_ref, gathered_ref, *outs):
    panel = below(pair_raw(gathered_ref, chunk, at)[:, :NB], col_ref[0], NB)
    first_factor(False, chunk, half, at, col_ref[0], gathered_ref, panel, outs)


def second_panel(following, vec, wide, wide_top, lower, index):
    return below(following - nt(vec, wide_top) - nt(wide, lower), index, 2 * NB)


def first_cols(
    chunk, at, index, got_ref, small_ref, state_ref, raw_ref, pair_ref, panel_ref, tops_ref
):
    got = unpack_symmetric(jnp.sum(got_ref[:, :PACKED, :], axis=0))
    half = half_core(small_ref[COEF], small_ref[FACTOR], small_ref[INNER], got)
    lower = small_ref[LOWER]
    wide_top = small_ref[WIDE] - nn(lower, half)
    tops_ref[0] = half
    tops_ref[1] = wide_top
    vec = state_ref[:, :NB]
    wide = state_ref[:, NB:] - nn(vec, half)
    pair_ref[...] = beside(wide, vec)
    following = pair_raw(raw_ref, chunk, at)[:, NB:]
    panel = second_panel(following, vec, wide, wide_top, lower, index)
    spare = jnp.zeros((panel.shape[0] - NB, NB), jnp.float32)
    panel_ref[...] = beside(panel, jnp.concatenate([small_ref[FACTOR], spare], axis=0))
    return panel, vec, wide


def first_cols_kernel(
    chunk, at, col_ref, got_ref, small_ref, state_ref, raw_ref,
    pair_ref, panel_ref, tops_ref, out_ref,
):
    panel, _, _ = first_cols(
        chunk, at, col_ref[0], got_ref, small_ref, state_ref, raw_ref,
        pair_ref, panel_ref, tops_ref,
    )
    packed = pack_symmetric(tn(panel, panel))
    out_ref[...] = jnp.broadcast_to(packed[None], out_ref.shape)


def plain_cols_kernel(
    chunk, at, col_ref, got_ref, small_ref, state_ref, raw_ref, matrix_ref,
    pair_ref, panel_ref, tops_ref, out_ref,
):
    panel, vec, wide = first_cols(
        chunk, at, col_ref[0], got_ref, small_ref, state_ref, raw_ref,
        pair_ref, panel_ref, tops_ref,
    )
    half = chunk // 2
    out_ref[:, :half, :] = fold(nn(matrix_ref[...], panel), chunk)
    last = last_raw(raw_ref, chunk, at)
    second_pairs(col_ref[0], panel, last, vec, wide, out_ref, half)


def first_rows_kernel(
    chunk, row_ref, got_ref, small_ref, once_ref, raw_ref, tops_ref, pair_ref, panel_ref
):
    image = unfold(got_ref[:, PACKED:, :])
    following = pair_raw(raw_ref, chunk)[:, NB:]
    vec = vectors_of(once_ref[...], row_ref[0], NB, small_ref[PICK], small_ref[COEF])
    wide = nn(following, small_ref[PICK_T]) - nn(image, small_ref[COEF_T]) - nn(vec, tops_ref[0])
    pair_ref[...] = beside(vec, wide)
    panel_ref[...] = second_panel(following, vec, wide, tops_ref[1], small_ref[LOWER], row_ref[0])


def second_small(near, half, gathered_ref, old_ref, panel_ref, small_ref, factors_ref):
    gram, image_top, vec_dot, wide_dot, top, vec_top, wide_top, _ = get_pairs(
        gathered_ref, half, 4
    )
    last_top = get_pairs(old_ref, half, 3)[4]
    image_top = image_top - nn(vec_top, wide_dot) - nn(wide_top, vec_dot)
    crossed = nt(vec_top, wide_top)
    next_top = last_top - crossed - crossed.T
    pick, coef, pick_t, coef_t, fine = factor_small(
        near, gram, top, next_top, image_top, small_ref
    )
    crossed = tn(nn(vec_dot, coef), nn(wide_dot, coef))
    small_ref[INNER] -= crossed + crossed.T
    factors_ref[0] = panel_ref[:NB, NB:]
    factors_ref[1] = small_ref[FACTOR]
    vec_dots = nn(wide_dot, coef_t) - tn(wide_top, pick_t)
    wide_dots = nn(vec_dot, coef_t) - tn(vec_top, pick_t)
    return pick, coef, pick_t, coef_t, vec_dots, wide_dots, fine


def second_factor_kernel(
    chunk, half, at, row_ref, col_ref, gathered_ref, old_ref, raw_r_ref,
    panel_c_ref, once_c_ref, once_r_ref, pair_c_ref, pair_r_ref,
    right_ref, state_ref, vectors_ref, factors_ref, small_ref,
):
    pick, coef, pick_t, coef_t, vec_dots, wide_dots, _ = second_small(
        True, half, gathered_ref, old_ref, panel_c_ref, small_ref, factors_ref
    )
    new = vectors_of(once_r_ref[...], row_ref[0], 2 * NB, pick, coef)
    vec = pair_r_ref[:, :NB]
    vectors_ref[0] = vec.T
    vectors_ref[1] = new.T
    part = nn(last_raw(raw_r_ref, chunk), pick_t)
    part += nn(vec, vec_dots) + nn(pair_r_ref[:, NB:], wide_dots)
    state_ref[...] = with_smalls(beside(new, part), small_ref)
    new = vectors_of(once_c_ref[...], col_ref[0], 2 * NB, pick, coef)
    part = nn(last_raw(old_ref, chunk, at), pick_t) - nn(unfold(gathered_ref[:, :half, :]), coef_t)
    part += nn(pair_c_ref[:, NB:], vec_dots) + nn(pair_c_ref[:, :NB], wide_dots)
    right_ref[...] = beside(part, new)


def plain_second_kernel(
    chunk, half, at, row_ref, col_ref, gathered_ref, old_ref, raw_r_ref,
    panel_c_ref, panel_r_ref, pair_c_ref, pair_r_ref,
    state_ref, left_ref, vectors_ref, factors_ref, fine_ref, small_ref,
):
    pick, coef, pick_t, coef_t, vec_dots, wide_dots, fine = second_small(
        False, half, gathered_ref, old_ref, panel_c_ref, small_ref, factors_ref
    )
    fine_ref[0] = jnp.where(fine, 1, 0)
    new = vectors_of(panel_r_ref[...], row_ref[0], 2 * NB, pick, coef)
    vec = pair_r_ref[:, :NB]
    vectors_ref[0] = vec.T
    vectors_ref[1] = new.T
    part = nn(last_raw(raw_r_ref, chunk), pick_t) - nn(unfold(gathered_ref[:, :half, :]), coef_t)
    part += nn(vec, vec_dots) + nn(pair_r_ref[:, NB:], wide_dots)
    left_ref[...] = beside(part, new)
    new = vectors_of(panel_c_ref[:, :NB], col_ref[0], 2 * NB, pick, coef)
    part = nn(last_raw(old_ref, chunk, at), pick_t)
    part += nn(pair_c_ref[:, NB:], vec_dots) + nn(pair_c_ref[:, :NB], wide_dots)
    state_ref[...] = with_smalls(beside(new, part), small_ref)


def with_smalls(state, small_ref):
    upper = beside(small_ref[COEF], small_ref[FACTOR])
    lower = beside(small_ref[INNER], small_ref[COEF_T])
    return jnp.concatenate([state, upper, lower], axis=0)


def last_kernel(got_ref, state_ref, out_ref):
    tall = out_ref.shape[0]
    coef, factor = state_ref[tall : tall + NB, :NB], state_ref[tall : tall + NB, NB:]
    inner, coef_t = state_ref[tall + NB :, :NB], state_ref[tall + NB :, NB:]
    got = unpack_symmetric(jnp.sum(got_ref[:, :PACKED, :], axis=0))
    half = half_core(coef, factor, inner, got)
    new = state_ref[:tall, :NB]
    image = unfold(got_ref[:, PACKED:, :])
    wide = state_ref[:tall, NB:] - nn(image, coef_t) - nn(new, half + half.T)
    out_ref[...] = beside(new, wide)


def call(kernel, name, outs, *args, statics=(), scalars=0, flag=False, small=False):
    in_smem = pl.BlockSpec(memory_space=pltpu.SMEM)
    in_vmem = pl.BlockSpec(memory_space=pltpu.VMEM)
    out_shape = [jax.ShapeDtypeStruct(shape, jnp.float32) for shape in outs]
    out_specs = [in_vmem] * len(outs)
    if flag:
        out_shape.append(jax.ShapeDtypeStruct((1,), jnp.int32))
        out_specs.append(in_smem)
    result = pl.pallas_call(
        functools.partial(kernel, *statics),
        out_shape=out_shape,
        in_specs=[in_smem if k < scalars else in_vmem for k in range(len(args))],
        out_specs=out_specs,
        compiler_params=pltpu.CompilerParams(vmem_limit_bytes=16 << 20),
        scratch_shapes=[pltpu.VMEM((8, NB, NB), jnp.float32)] if small else [],
        cost_estimate=pl.CostEstimate(flops=1 << 24, bytes_accessed=1 << 22, transcendentals=0),
        name=name,
    )(*args)
    return result[0] if len(result) == 1 else result


def swap(x, axis):
    return lax.all_to_all(x, axis, 0, 0)


def solution(mesh):
    nr = mesh.shape["row"]
    nc = mesh.shape["col"]

    def local(matrix):
        rows_here, cols_here = matrix.shape
        chunk = rows_here // nc
        half = chunk // 2
        my_row = lax.axis_index("row").astype(jnp.int32).reshape(1)
        my_col = lax.axis_index("col").astype(jnp.int32).reshape(1)
        col_place = (lax.axis_index("col") * cols_here + jnp.arange(cols_here))[:, None]
        to_rows = []
        for r in range(nr):
            for c in range(nc):
                first = r * rows_here + c * chunk
                source = (first % cols_here // chunk) * nc + first // cols_here
                to_rows.append((source, r * nc + c))
        to_cols = [(b, a) for a, b in to_rows]
        square = (NB, NB)
        tall_r = (rows_here, NB)
        tall_c = (cols_here, NB)
        pair_shape_c = (cols_here, 2 * NB)
        pair_shape_r = (rows_here, 2 * NB)
        raw_rows = chunk + half

        def few(peers):
            return -(-4 * (NB // peers) // 8) * 8

        def image_round(mine, axis, targets, extra=(), beside=()):
            got, *beside = lax.optimization_barrier((swap(mine, axis), *beside))
            rows = got.shape[1] + sum(x.shape[0] for x in extra)
            blocks, image_chunk = call(
                sum_with_kernel if extra else sum_kernel, "sum_blocks",
                [(got.shape[0], rows, 2 * NB), (half, 2 * NB)], got, *extra,
            )
            return swap(blocks, axis), lax.ppermute(image_chunk, ("row", "col"), targets), *beside

        def image_blocks(once_r, smalls):
            return jnp.concatenate([fold(tn(matrix, once_r), chunk), smalls], axis=1)

        at = half + few(nr)

        block_r = (nc, PACKED + half, 2 * NB)
        block_c = (nr, PACKED + half, 2 * NB)

        def plain():
            raw = pl.pallas_call(
                functools.partial(plain_start_kernel, chunk),
                grid=(1,),
                in_specs=[pl.BlockSpec((rows_here, 4 * NB), lambda _: (0, 0))],
                out_specs=pl.BlockSpec((nc, raw_rows, 2 * NB), lambda _: (0, 0, 0)),
                out_shape=jax.ShapeDtypeStruct((nc, raw_rows, 2 * NB), jnp.float32),
                name="plain_start",
            )(matrix)
            raw_chunk = swap(raw, "col")[0]
            raw_chunk_c = lax.ppermute(raw_chunk, ("row", "col"), to_cols)
            raw_r = swap(jnp.broadcast_to(raw_chunk[None], raw.shape), "col")
            first_r, smalls = call(
                plain_first_kernel, "plain_first", [tall_r, (nr, few(nr), 2 * NB)],
                my_row, raw_r, statics=(chunk,), scalars=1,
            )
            gathered, image_chunk = image_round(
                image_blocks(first_r, smalls), "row", to_rows, (raw_chunk_c,)
            )
            inners = call(
                plain_inner_kernel, "plain_inner", [block_r],
                my_col, gathered, image_chunk, statics=(chunk, at), scalars=1,
            )
            got = swap(inners, "col")
            small_one, state_c, fine_one = call(
                plain_factor_kernel, "plain_factor", [(8,) + square, pair_shape_c],
                my_col, gathered, statics=(chunk, half, at), scalars=1, flag=True,
            )
            pair_c, panel_c, tops, blocks = call(
                plain_cols_kernel, "plain_cols",
                [pair_shape_c, pair_shape_c, (2,) + square, (nc, half + few(nc), 2 * NB)],
                my_col, got, small_one, state_c, gathered, matrix, statics=(chunk, at), scalars=1,
            )
            pair_r, panel_r = call(
                first_rows_kernel, "first_rows", [pair_shape_r, tall_r],
                my_row, got, small_one, first_r, raw_r, tops, statics=(chunk,), scalars=1,
            )
            current = matrix - nt(pair_r, pair_c)
            old = gathered
            gathered, image_chunk, current, pair_r, panel_r = image_round(
                blocks, "col", to_cols, beside=(current, pair_r, panel_r)
            )
            inners = call(
                inner_kernel, "inner", [block_c], gathered, panel_r, image_chunk
            )
            got = swap(inners, "row")
            state_c, left, vectors, factors, fine_two = call(
                plain_second_kernel, "plain_second",
                [
                    (cols_here + 2 * NB, 2 * NB), pair_shape_r, (2, NB, rows_here), (2,) + square
                ],
                my_row, my_col, gathered, old, raw_r, panel_c, panel_r,
                pair_c, pair_r, statics=(chunk, half, at), scalars=2, flag=True,
                small=True,
            )
            right = call(
                last_kernel, "last", [pair_shape_c], got, state_c
            )
            return (current, left, right, vectors, factors), (fine_one + fine_two)[0] == 2

        def careful():
            raw, grams = call(
                start_kernel, "start", [(nc, raw_rows, 2 * NB), (nr, PACKED, 2 * NB)],
                my_row, matrix[:, : 4 * NB], statics=(chunk,), scalars=1,
            )
            raw_chunk = swap(raw, "col")[0]
            raw_chunk_c = lax.ppermute(raw_chunk, ("row", "col"), to_cols)
            raw_r = call(
                relay_kernel, "relay", [(nc, raw_rows + PACKED, 2 * NB)], raw_chunk, swap(grams, "row")
            )
            raw_r = swap(raw_r, "col")

            root, once_r, smalls = call(
                first_once_kernel, "first_once", [square, tall_r, (nr, few(nr), 2 * NB)],
                my_row, raw_r, statics=(chunk,), scalars=1,
            )

            gathered, image_chunk_r = image_round(
                image_blocks(once_r, smalls), "row", to_rows, (raw_chunk_c,)
            )
            first_c = gathered[:, at : at + chunk, :NB].reshape(tall_c)
            once_c = nt(jnp.where(col_place >= NB, first_c, 0.0), root)
            inners = call(inner_kernel, "inner", [block_r], gathered, once_c, image_chunk_r)
            got = swap(inners, "col")
            small_one, state_c, _ = call(
                first_factor_kernel, "first_factor", [(8,) + square, pair_shape_c],
                my_col, gathered, once_c, statics=(chunk, half, at), scalars=1, flag=True,
            )
            pair_c, panel_c, tops, grams = call(
                first_cols_kernel, "first_cols",
                [pair_shape_c, pair_shape_c, (2,) + square, (nc, PACKED, 2 * NB)],
                my_col, got, small_one, state_c, gathered, statics=(chunk, at), scalars=1,
            )
            grams = swap(grams, "col")
            pair_r, panel_r = call(
                first_rows_kernel, "first_rows", [pair_shape_r, tall_r],
                my_row, got, small_one, once_r, raw_r, tops, statics=(chunk,), scalars=1,
            )

            root, once_r, smalls = call(
                second_once_kernel, "second_once", [square, tall_r, (nr, few(nr), 2 * NB)],
                my_row, grams, raw_r, panel_r, pair_r, statics=(chunk,), scalars=1,
            )
            old = gathered
            gathered, image_chunk_r = image_round(image_blocks(once_r, smalls), "row", to_rows)
            once_c = nt(panel_c[:, :NB], root)
            current = matrix - nt(pair_r, pair_c)
            inners = call(inner_kernel, "inner", [block_r], gathered, once_c, image_chunk_r)
            got = swap(inners, "col")
            right, state_r, vectors, factors = call(
                second_factor_kernel, "second_factor",
                [
                    pair_shape_c, (rows_here + 2 * NB, 2 * NB), (2, NB, rows_here), (2,) + square
                ],
                my_row, my_col, gathered, old, raw_r, panel_c, once_c, once_r, pair_c, pair_r,
                statics=(chunk, half, at), scalars=2, small=True,
            )
            left = call(last_kernel, "last", [pair_shape_r], got, state_r)
            return current - nt(left, right), vectors, factors

        ready, fine = plain()

        def finish(current, left, right, vectors, factors):
            return current - nt(left, right), vectors, factors

        banded, vectors, factors = lax.cond(fine, finish, lambda *_: careful(), *ready)
        return banded, vectors.transpose(0, 2, 1), factors

    return jax.shard_map(
        local,
        mesh=mesh,
        in_specs=(P("row", "col"),),
        out_specs=(P("row", "col"), P(None, "row", None), P()),
        check_vma=False,
    )
```

```python
import functools

import jax
import jax.numpy as jnp
from jax import lax
from jax.experimental import pallas as pl
from jax.experimental.pallas import tpu as pltpu
from jax.sharding import PartitionSpec as P

NB = 64
precise = lax.Precision.HIGHEST


def nn(a, b):
    return lax.dot_general(
        a, b, (((1,), (0,)), ((), ())), precision=precise, preferred_element_type=jnp.float32
    )


def tn(a, b):
    return lax.dot_general(
        a, b, (((0,), (0,)), ((), ())), precision=precise, preferred_element_type=jnp.float32
    )


def nt(a, b):
    return lax.dot_general(
        a, b, (((1,), (1,)), ((), ())), precision=precise, preferred_element_type=jnp.float32
    )


def places():
    sub = lax.broadcasted_iota(jnp.int32, (NB, 2 * NB), 0)
    lane = lax.broadcasted_iota(jnp.int32, (NB, 2 * NB), 1)
    return sub, lane


def inverse_root(gram):
    sub, lane = places()
    eye = (sub + NB == lane).astype(jnp.float32)
    work = jnp.concatenate([gram, jnp.zeros_like(gram)], axis=1) + eye
    scales = jnp.zeros((NB, 2 * NB), jnp.float32)
    for step in range(0, NB, 2):
        first = work[step : step + 1]
        second = work[step + 1 : step + 2]
        left = jnp.broadcast_to(work[:, step : step + 1], work.shape)
        right = jnp.broadcast_to(work[:, step + 1 : step + 2], work.shape)
        a, b = left[step : step + 1], right[step : step + 1]
        c, d = left[step + 1 : step + 2], right[step + 1 : step + 2]
        inverse = 1.0 / a
        det = a * d - b * c
        last = a * (1.0 / det)
        second = second - (c * inverse) * first
        scales = jnp.where(sub == step, a, jnp.where(sub == step + 1, det * inverse, scales))
        second_scaled = second * last
        first_scaled = first * inverse - (b * inverse) * second_scaled
        change = left * first_scaled + right * second_scaled
        work = jnp.where(sub > step + 1, work - change, jnp.where(sub == step + 1, second, work))
    return (work * lax.rsqrt(scales))[:, NB:]


def signed_lu(negated_top):
    sub, lane = places()
    eye = (sub + NB == lane).astype(jnp.float32)
    work = jnp.concatenate([negated_top, jnp.zeros_like(negated_top)], axis=1) + eye
    lower = jnp.zeros((NB, 2 * NB), jnp.float32)
    upper = jnp.zeros((NB, 2 * NB), jnp.float32)
    signs = jnp.zeros((1, 2 * NB), jnp.float32)
    lane_row = lax.broadcasted_iota(jnp.int32, (1, 2 * NB), 1)
    for step in range(0, NB, 2):
        left = jnp.broadcast_to(work[:, step : step + 1], work.shape)
        right = jnp.broadcast_to(work[:, step + 1 : step + 2], work.shape)
        raw, b = left[step : step + 1], right[step : step + 1]
        c, d = left[step + 1 : step + 2], right[step + 1 : step + 2]
        flip = jnp.where(raw > 0, 1.0, -1.0)
        a = raw + flip
        raw_det = a * d - b * c
        flip_last = jnp.where(raw_det * flip > 0, 1.0, -1.0)
        det = raw_det + flip_last * a
        inverse = 1.0 / a
        last = a * (1.0 / det)
        signs = jnp.where(lane_row == step, flip, jnp.where(lane_row == step + 1, flip_last, signs))
        first = jnp.where(lane_row == step, a, work[step : step + 1])
        second = work[step + 1 : step + 2] - (c * inverse) * first
        second = jnp.where(lane_row == step + 1, det * inverse, second)
        upper = jnp.where(
            (sub == step) & (lane >= step), first,
            jnp.where((sub == step + 1) & (lane > step), second, upper),
        )
        second_scaled = second * last
        second_scaled = jnp.where(lane_row == step, 0.0, second_scaled)
        ratio = b * inverse
        first_scaled = first * inverse - ratio * second_scaled
        below_first = jnp.where(sub > step, left * inverse, jnp.where(sub == step, 1.0, 0.0))
        below_last = (right - left * ratio) * last
        below_last = jnp.where(sub > step + 1, below_last, jnp.where(sub == step + 1, 1.0, 0.0))
        lower = jnp.where(lane == step, below_first, jnp.where(lane == step + 1, below_last, lower))
        change = left * first_scaled + right * second_scaled
        work = jnp.where(
            sub == step, first_scaled, jnp.where(sub == step + 1, second_scaled, work - change)
        )
    return lower[:, :NB], upper[:, :NB], work[:, NB:], signs[:, :NB]


def near_root(gram):
    sub = lax.broadcasted_iota(jnp.int32, (NB, NB), 0)
    lane = lax.broadcasted_iota(jnp.int32, (NB, NB), 1)
    eye = (sub == lane).astype(jnp.float32)
    off = gram - eye
    first_order = eye - jnp.where(sub > lane, off, jnp.where(sub == lane, 0.5 * off, 0.0))
    close = jnp.sum(off * off) < 2e-8
    return lax.cond(close, lambda: first_order, lambda: inverse_root(gram))


def fold(x, chunk):
    x = x.reshape(-1, chunk, NB)
    return jnp.concatenate([x[:, : chunk // 2], x[:, chunk // 2 :]], axis=2)


def unfold(x):
    return jnp.concatenate([x[:, :, :NB], x[:, :, NB:]], axis=1).reshape(-1, NB)


def pack_symmetric(g):
    h = NB // 2
    rows = []
    for quadrant in (g[:h, :h], g[:h, h:], g[h:, h:]):
        rows.append(jnp.concatenate([quadrant[k : k + 8] for k in range(0, h, 8)], axis=1))
    return jnp.concatenate(rows, axis=0)


def unpack_symmetric(x):
    h = NB // 2
    first, cross, last = [
        jnp.concatenate([x[q : q + 8, k : k + h] for k in range(0, 4 * h, h)], axis=0)
        for q in (0, 8, 16)
    ]
    upper = jnp.concatenate([first, cross], axis=1)
    return jnp.concatenate([upper, jnp.concatenate([cross.T, last], axis=1)], axis=0)


PACKED = 24


def put_pairs(out_ref, pairs, first=0):
    peers, rows = out_ref.shape[:2]
    per = NB // peers
    for q, pair in enumerate(pairs):
        for t in range(per):
            out_ref[:, first + q * per + t, :] = pair[t * peers : (t + 1) * peers]
    for k in range(first + len(pairs) * per, rows):
        out_ref[:, k, :] = jnp.zeros((peers, 2 * NB), jnp.float32)


def get_pairs(ref, first, count):
    per = NB // ref.shape[0]
    pairs = []
    for q in range(count):
        slots = [ref[:, first + q * per + t, :] for t in range(per)]
        pair = jnp.concatenate(slots, axis=0)
        pairs += [pair[:, :NB], pair[:, NB:]]
    return pairs


def beside(*parts):
    return jnp.concatenate(parts, axis=1)


def below(x, index, start):
    place = lax.broadcasted_iota(jnp.int32, x.shape, 0)
    return jnp.where((place >= start) | (index > 0), x, 0.0)


def plain_start_kernel(chunk, matrix_ref, raw_ref):
    raw_ref[:, :chunk, :] = matrix_ref[:, : 2 * NB].reshape(-1, chunk, 2 * NB)
    raw_ref[:, chunk:, :] = fold(matrix_ref[:, 2 * NB : 3 * NB], chunk)


def start_kernel(chunk, index_ref, matrix_ref, raw_ref, out_ref):
    plain_start_kernel(chunk, matrix_ref, raw_ref)
    panel = below(matrix_ref[:, :NB], index_ref[0], NB)
    packed = pack_symmetric(tn(panel, panel))
    out_ref[...] = jnp.broadcast_to(packed[None], out_ref.shape)


def relay_kernel(raw_ref, got_ref, out_ref):
    block = jnp.concatenate([raw_ref[...], jnp.sum(got_ref[...], axis=0)], axis=0)
    out_ref[...] = jnp.broadcast_to(block[None], out_ref.shape)


def pair_raw(raw_ref, chunk, at=0):
    return raw_ref[:, at : at + chunk, :].reshape(-1, 2 * NB)


def last_raw(raw_ref, chunk, at=0):
    return unfold(raw_ref[:, at + chunk : at + chunk + chunk // 2, :])


def first_pairs(chunk, index, raw_ref, root, once_ref, small_ref):
    pair = pair_raw(raw_ref, chunk)
    following = pair[:, NB:]
    once = below(pair[:, :NB], index, NB)
    if root is not None:
        once = nt(once, root)
    once_ref[...] = once
    last = last_raw(raw_ref, chunk)
    gram = tn(once, once)
    image_top = tn(following, once)

    def top(x, k):
        return jnp.where(index == 0, x[k * NB : (k + 1) * NB], 0.0)

    put_pairs(
        small_ref,
        [
            beside(gram, image_top),
            beside(top(once, 1), top(following, 1)),
            beside(top(last, 2), jnp.zeros((NB, NB), jnp.float32)),
        ],
    )


def plain_first_kernel(chunk, index_ref, raw_ref, panel_ref, small_ref):
    first_pairs(chunk, index_ref[0], raw_ref, None, panel_ref, small_ref)


def first_once_kernel(chunk, index_ref, raw_ref, root_ref, once_ref, small_ref):
    root = inverse_root(unpack_symmetric(raw_ref[0, chunk + chunk // 2 :, :]))
    root_ref[...] = root
    first_pairs(chunk, index_ref[0], raw_ref, root, once_ref, small_ref)


def second_pairs(index, once, last, vec, wide, small_ref, first=0):
    def top(x):
        return jnp.where(index == 0, x[2 * NB : 3 * NB], 0.0)

    grams = tn(beside(once, last), once)
    dots = tn(beside(vec, wide), once)
    put_pairs(
        small_ref,
        [
            beside(grams[:NB], grams[NB:]),
            beside(dots[:NB], dots[NB:]),
            beside(top(once), top(vec)),
            beside(top(wide), jnp.zeros((NB, NB), jnp.float32)),
        ],
        first,
    )


def second_once_kernel(
    chunk, index_ref, got_ref, raw_ref, panel_ref, pair_ref, root_ref, once_ref, small_ref
):
    root = inverse_root(unpack_symmetric(jnp.sum(got_ref[...], axis=0)))
    root_ref[...] = root
    once = nt(panel_ref[...], root)
    once_ref[...] = once
    last = last_raw(raw_ref, chunk)
    second_pairs(index_ref[0], once, last, pair_ref[:, :NB], pair_ref[:, NB:], small_ref)


def sum_kernel(got_ref, out_ref, chunk_ref):
    summed = jnp.sum(got_ref[...], axis=0)
    out_ref[...] = jnp.broadcast_to(summed[None], out_ref.shape)
    chunk_ref[...] = summed[: chunk_ref.shape[0]]


def sum_with_kernel(got_ref, raw_ref, out_ref, chunk_ref):
    summed = jnp.sum(got_ref[...], axis=0)
    block = jnp.concatenate([summed, raw_ref[...]], axis=0)
    out_ref[...] = jnp.broadcast_to(block[None], out_ref.shape)
    chunk_ref[...] = summed[: chunk_ref.shape[0]]


def inner_kernel(gathered_ref, once_ref, chunk_ref, out_ref):
    half = chunk_ref.shape[0]
    inner = tn(once_ref[...], unfold(gathered_ref[:, :half, :]))
    block = jnp.concatenate([pack_symmetric(inner), chunk_ref[...]], axis=0)
    out_ref[...] = jnp.broadcast_to(block[None], out_ref.shape)


def plain_inner_kernel(chunk, at, col_ref, gathered_ref, chunk_ref, out_ref):
    half = chunk_ref.shape[0]
    panel = below(pair_raw(gathered_ref, chunk, at)[:, :NB], col_ref[0], NB)
    inner = tn(panel, unfold(gathered_ref[:, :half, :]))
    block = jnp.concatenate([pack_symmetric(inner), chunk_ref[...]], axis=0)
    out_ref[...] = jnp.broadcast_to(block[None], out_ref.shape)


PICK, COEF, PICK_T, COEF_T, LOWER, FACTOR, INNER, WIDE = range(8)


def factor_small(near, gram, top, next_top, image_top, small_ref):
    root = near_root(gram) if near else inverse_root(gram)
    lower, upper, inverse, signs = signed_lu(-nt(top, root))
    sub = lax.broadcasted_iota(jnp.int32, (NB, NB), 0)
    lane = lax.broadcasted_iota(jnp.int32, (NB, NB), 1)
    triangle = lane >= sub
    upper_inverse = jnp.where(triangle, nn(inverse, lower), 0.0)
    lower_inverse = nn(upper, inverse)
    factor = jnp.where(triangle, nt(upper * signs, lower_inverse), 0.0)
    pick = nn(jnp.where(sub == lane, signs, 0.0), upper_inverse)
    coef = tn(root, upper_inverse)
    crossed = tn(pick, nn(image_top, coef))
    pick_t = nn(pick, factor)
    coef_t = nn(coef, factor)
    small_ref[PICK] = pick
    small_ref[COEF] = coef
    small_ref[PICK_T] = pick_t
    small_ref[COEF_T] = coef_t
    small_ref[LOWER] = lower
    small_ref[FACTOR] = factor
    small_ref[INNER] = tn(pick, nn(next_top, pick)) - crossed - crossed.T
    small_ref[WIDE] = nn(next_top, pick_t) - nn(image_top, coef_t)
    sizes = jnp.sum(jnp.where(sub == lane, gram, 0.0), axis=0, keepdims=True)
    fine = jnp.sum(root * root * sizes) < 1.5 * NB
    return pick, coef, pick_t, coef_t, fine


def vectors_of(once, index, start, pick, coef):
    vec = -nn(once, coef)
    top = vec[start : start + NB] + jnp.where(index == 0, pick, 0.0)
    return jnp.concatenate([vec[:start], top, vec[start + NB :]], axis=0)


def half_core(coef, factor, known, got):
    inner = known + tn(coef, nn(got, coef))
    return 0.5 * tn(factor, nn(inner, factor))


def first_factor(near, chunk, half, at, col, gathered_ref, once_c, outs):
    small_ref, state_ref, fine_ref = outs
    gram, image_top, top, next_top, _, _ = get_pairs(gathered_ref, half, 3)
    pick, coef, pick_t, coef_t, fine = factor_small(
        near, gram, top, next_top, image_top, small_ref
    )
    fine_ref[0] = jnp.where(fine, 1, 0)
    following = pair_raw(gathered_ref, chunk, at)[:, NB:]
    image = unfold(gathered_ref[:, :half, :])
    vec = vectors_of(once_c, col, NB, pick, coef)
    state_ref[...] = beside(vec, nn(following, pick_t) - nn(image, coef_t))


def first_factor_kernel(chunk, half, at, col_ref, gathered_ref, once_c_ref, *outs):
    first_factor(True, chunk, half, at, col_ref[0], gathered_ref, once_c_ref[...], outs)


def plain_factor_kernel(chunk, half, at, col_ref, gathered_ref, *outs):
    panel = below(pair_raw(gathered_ref, chunk, at)[:, :NB], col_ref[0], NB)
    first_factor(False, chunk, half, at, col_ref[0], gathered_ref, panel, outs)


def second_panel(following, pair, tops, index):
    return below(following - nt(pair, tops), index, 2 * NB)


def first_cols(
    chunk, at, index, got_ref, small_ref, state_ref, raw_ref, pair_ref, panel_ref, tops_ref
):
    got = unpack_symmetric(jnp.sum(got_ref[:, :PACKED, :], axis=0))
    half = half_core(small_ref[COEF], small_ref[FACTOR], small_ref[INNER], got)
    lower = small_ref[LOWER]
    wide_top = small_ref[WIDE] - nn(lower, half)
    tops_ref[0] = half
    tops_ref[1] = wide_top
    vec = state_ref[:, :NB]
    wide = state_ref[:, NB:] - nn(vec, half)
    pair = beside(wide, vec)
    pair_ref[...] = pair
    following = pair_raw(raw_ref, chunk, at)[:, NB:]
    panel = second_panel(following, pair, beside(lower, wide_top), index)
    spare = jnp.zeros((panel.shape[0] - NB, NB), jnp.float32)
    panel_ref[...] = beside(panel, jnp.concatenate([small_ref[FACTOR], spare], axis=0))
    return panel, vec, wide


def first_cols_kernel(
    chunk, at, col_ref, got_ref, small_ref, state_ref, raw_ref,
    pair_ref, panel_ref, tops_ref, out_ref,
):
    panel, _, _ = first_cols(
        chunk, at, col_ref[0], got_ref, small_ref, state_ref, raw_ref,
        pair_ref, panel_ref, tops_ref,
    )
    packed = pack_symmetric(tn(panel, panel))
    out_ref[...] = jnp.broadcast_to(packed[None], out_ref.shape)


def plain_cols_kernel(
    chunk, at, col_ref, got_ref, small_ref, state_ref, raw_ref, matrix_ref,
    pair_ref, panel_ref, tops_ref, out_ref,
):
    panel, vec, wide = first_cols(
        chunk, at, col_ref[0], got_ref, small_ref, state_ref, raw_ref,
        pair_ref, panel_ref, tops_ref,
    )
    half = chunk // 2
    out_ref[:, :half, :] = fold(nn(matrix_ref[...], panel), chunk)
    last = last_raw(raw_ref, chunk, at)
    second_pairs(col_ref[0], panel, last, vec, wide, out_ref, half)


def first_rows_kernel(
    chunk, row_ref, got_ref, small_ref, once_ref, raw_ref, tops_ref, pair_ref, panel_ref
):
    image = unfold(got_ref[:, PACKED:, :])
    following = pair_raw(raw_ref, chunk)[:, NB:]
    vec = vectors_of(once_ref[...], row_ref[0], NB, small_ref[PICK], small_ref[COEF])
    wide = nn(following, small_ref[PICK_T]) - nn(image, small_ref[COEF_T]) - nn(vec, tops_ref[0])
    pair = beside(vec, wide)
    pair_ref[...] = pair
    tops = beside(tops_ref[1], small_ref[LOWER])
    panel_ref[...] = second_panel(following, pair, tops, row_ref[0])


def second_small(near, half, gathered_ref, old_ref, panel_ref, small_ref, factors_ref):
    gram, image_top, vec_dot, wide_dot, top, vec_top, wide_top, _ = get_pairs(
        gathered_ref, half, 4
    )
    last_top = get_pairs(old_ref, half, 3)[4]
    image_top = image_top - nn(vec_top, wide_dot) - nn(wide_top, vec_dot)
    crossed = nt(vec_top, wide_top)
    next_top = last_top - crossed - crossed.T
    pick, coef, pick_t, coef_t, fine = factor_small(
        near, gram, top, next_top, image_top, small_ref
    )
    crossed = tn(nn(vec_dot, coef), nn(wide_dot, coef))
    small_ref[INNER] -= crossed + crossed.T
    factors_ref[0] = panel_ref[:NB, NB:]
    factors_ref[1] = small_ref[FACTOR]
    vec_dots = nn(wide_dot, coef_t) - tn(wide_top, pick_t)
    wide_dots = nn(vec_dot, coef_t) - tn(vec_top, pick_t)
    return pick, coef, pick_t, coef_t, vec_dots, wide_dots, fine


def second_factor_kernel(
    chunk, half, at, row_ref, col_ref, gathered_ref, old_ref, raw_r_ref,
    panel_c_ref, once_c_ref, once_r_ref, pair_c_ref, pair_r_ref,
    right_ref, state_ref, vectors_ref, factors_ref, small_ref,
):
    pick, coef, pick_t, coef_t, vec_dots, wide_dots, _ = second_small(
        True, half, gathered_ref, old_ref, panel_c_ref, small_ref, factors_ref
    )
    new = vectors_of(once_r_ref[...], row_ref[0], 2 * NB, pick, coef)
    vec = pair_r_ref[:, :NB]
    vectors_ref[0] = vec.T
    vectors_ref[1] = new.T
    part = nn(last_raw(raw_r_ref, chunk), pick_t)
    part += nn(vec, vec_dots) + nn(pair_r_ref[:, NB:], wide_dots)
    state_ref[...] = with_smalls(beside(new, part), small_ref)
    new = vectors_of(once_c_ref[...], col_ref[0], 2 * NB, pick, coef)
    part = nn(last_raw(old_ref, chunk, at), pick_t) - nn(unfold(gathered_ref[:, :half, :]), coef_t)
    part += nn(pair_c_ref[:, NB:], vec_dots) + nn(pair_c_ref[:, :NB], wide_dots)
    right_ref[...] = beside(part, new)


def plain_second_kernel(
    chunk, half, at, row_ref, col_ref, gathered_ref, old_ref, raw_r_ref,
    panel_c_ref, panel_r_ref, pair_c_ref, pair_r_ref,
    state_ref, left_ref, vectors_ref, factors_ref, fine_ref, small_ref,
):
    pick, coef, pick_t, coef_t, vec_dots, wide_dots, fine = second_small(
        False, half, gathered_ref, old_ref, panel_c_ref, small_ref, factors_ref
    )
    fine_ref[0] = jnp.where(fine, 1, 0)
    new = vectors_of(panel_r_ref[...], row_ref[0], 2 * NB, pick, coef)
    vec = pair_r_ref[:, :NB]
    vectors_ref[0] = vec.T
    vectors_ref[1] = new.T
    part = nn(last_raw(raw_r_ref, chunk), pick_t) - nn(unfold(gathered_ref[:, :half, :]), coef_t)
    part += nn(vec, vec_dots) + nn(pair_r_ref[:, NB:], wide_dots)
    left_ref[...] = beside(part, new)
    new = vectors_of(panel_c_ref[:, :NB], col_ref[0], 2 * NB, pick, coef)
    part = nn(last_raw(old_ref, chunk, at), pick_t)
    part += nn(pair_c_ref[:, NB:], vec_dots) + nn(pair_c_ref[:, :NB], wide_dots)
    state_ref[...] = with_smalls(beside(new, part), small_ref)


def with_smalls(state, small_ref):
    upper = beside(small_ref[COEF], small_ref[FACTOR])
    lower = beside(small_ref[INNER], small_ref[COEF_T])
    return jnp.concatenate([state, upper, lower], axis=0)


def last_kernel(got_ref, state_ref, out_ref):
    tall = out_ref.shape[0]
    coef, factor = state_ref[tall : tall + NB, :NB], state_ref[tall : tall + NB, NB:]
    inner, coef_t = state_ref[tall + NB :, :NB], state_ref[tall + NB :, NB:]
    got = unpack_symmetric(jnp.sum(got_ref[:, :PACKED, :], axis=0))
    half = half_core(coef, factor, inner, got)
    new = state_ref[:tall, :NB]
    image = unfold(got_ref[:, PACKED:, :])
    wide = state_ref[:tall, NB:] - nn(image, coef_t) - nn(new, half + half.T)
    out_ref[...] = beside(new, wide)


def call(kernel, name, outs, *args, statics=(), scalars=0, flag=False, small=False):
    in_smem = pl.BlockSpec(memory_space=pltpu.SMEM)
    in_vmem = pl.BlockSpec(memory_space=pltpu.VMEM)
    out_shape = [jax.ShapeDtypeStruct(shape, jnp.float32) for shape in outs]
    out_specs = [in_vmem] * len(outs)
    if flag:
        out_shape.append(jax.ShapeDtypeStruct((1,), jnp.int32))
        out_specs.append(in_smem)
    result = pl.pallas_call(
        functools.partial(kernel, *statics),
        out_shape=out_shape,
        in_specs=[in_smem if k < scalars else in_vmem for k in range(len(args))],
        out_specs=out_specs,
        compiler_params=pltpu.CompilerParams(vmem_limit_bytes=16 << 20),
        scratch_shapes=[pltpu.VMEM((8, NB, NB), jnp.float32)] if small else [],
        cost_estimate=pl.CostEstimate(flops=1 << 24, bytes_accessed=1 << 22, transcendentals=0),
        name=name,
    )(*args)
    return result[0] if len(result) == 1 else result


def swap(x, axis):
    return lax.all_to_all(x, axis, 0, 0)


def solution(mesh):
    nr = mesh.shape["row"]
    nc = mesh.shape["col"]

    def local(matrix):
        rows_here, cols_here = matrix.shape
        chunk = rows_here // nc
        half = chunk // 2
        my_row = lax.axis_index("row").astype(jnp.int32).reshape(1)
        my_col = lax.axis_index("col").astype(jnp.int32).reshape(1)
        col_place = (lax.axis_index("col") * cols_here + jnp.arange(cols_here))[:, None]
        to_rows = []
        for r in range(nr):
            for c in range(nc):
                first = r * rows_here + c * chunk
                source = (first % cols_here // chunk) * nc + first // cols_here
                to_rows.append((source, r * nc + c))
        to_cols = [(b, a) for a, b in to_rows]
        square = (NB, NB)
        tall_r = (rows_here, NB)
        tall_c = (cols_here, NB)
        pair_shape_c = (cols_here, 2 * NB)
        pair_shape_r = (rows_here, 2 * NB)
        raw_rows = chunk + half

        def few(peers):
            return -(-4 * (NB // peers) // 8) * 8

        def image_round(mine, axis, targets, extra=(), beside=()):
            got, *beside = lax.optimization_barrier((swap(mine, axis), *beside))
            rows = got.shape[1] + sum(x.shape[0] for x in extra)
            blocks, image_chunk = call(
                sum_with_kernel if extra else sum_kernel, "sum_blocks",
                [(got.shape[0], rows, 2 * NB), (half, 2 * NB)], got, *extra,
            )
            return swap(blocks, axis), lax.ppermute(image_chunk, ("row", "col"), targets), *beside

        def image_blocks(once_r, smalls):
            return jnp.concatenate([fold(tn(matrix, once_r), chunk), smalls], axis=1)

        at = half + few(nr)

        block_r = (nc, PACKED + half, 2 * NB)
        block_c = (nr, PACKED + half, 2 * NB)

        def plain():
            raw = pl.pallas_call(
                functools.partial(plain_start_kernel, chunk),
                grid=(1,),
                in_specs=[pl.BlockSpec((rows_here, 4 * NB), lambda _: (0, 0))],
                out_specs=pl.BlockSpec((nc, raw_rows, 2 * NB), lambda _: (0, 0, 0)),
                out_shape=jax.ShapeDtypeStruct((nc, raw_rows, 2 * NB), jnp.float32),
                name="plain_start",
            )(matrix)
            raw_chunk = swap(raw, "col")[0]
            raw_chunk_c = lax.ppermute(raw_chunk, ("row", "col"), to_cols)
            raw_r = swap(jnp.broadcast_to(raw_chunk[None], raw.shape), "col")
            first_r, smalls = call(
                plain_first_kernel, "plain_first", [tall_r, (nr, few(nr), 2 * NB)],
                my_row, raw_r, statics=(chunk,), scalars=1,
            )
            gathered, image_chunk = image_round(
                image_blocks(first_r, smalls), "row", to_rows, (raw_chunk_c,)
            )
            inners = call(
                plain_inner_kernel, "plain_inner", [block_r],
                my_col, gathered, image_chunk, statics=(chunk, at), scalars=1,
            )
            got = swap(inners, "col")
            small_one, state_c, fine_one = call(
                plain_factor_kernel, "plain_factor", [(8,) + square, pair_shape_c],
                my_col, gathered, statics=(chunk, half, at), scalars=1, flag=True,
            )
            pair_c, panel_c, tops, blocks = call(
                plain_cols_kernel, "plain_cols",
                [pair_shape_c, pair_shape_c, (2,) + square, (nc, half + few(nc), 2 * NB)],
                my_col, got, small_one, state_c, gathered, matrix, statics=(chunk, at), scalars=1,
            )
            pair_r, panel_r = call(
                first_rows_kernel, "first_rows", [pair_shape_r, tall_r],
                my_row, got, small_one, first_r, raw_r, tops, statics=(chunk,), scalars=1,
            )
            current = matrix - nt(pair_r, pair_c)
            old = gathered
            gathered, image_chunk, current, pair_r, panel_r = image_round(
                blocks, "col", to_cols, beside=(current, pair_r, panel_r)
            )
            inners = call(
                inner_kernel, "inner", [block_c], gathered, panel_r, image_chunk
            )
            got = swap(inners, "row")
            state_c, left, vectors, factors, fine_two = call(
                plain_second_kernel, "plain_second",
                [
                    (cols_here + 2 * NB, 2 * NB), pair_shape_r, (2, NB, rows_here), (2,) + square
                ],
                my_row, my_col, gathered, old, raw_r, panel_c, panel_r,
                pair_c, pair_r, statics=(chunk, half, at), scalars=2, flag=True,
                small=True,
            )
            right = call(
                last_kernel, "last", [pair_shape_c], got, state_c
            )
            return (current, left, right, vectors, factors), (fine_one + fine_two)[0] == 2

        def careful():
            raw, grams = call(
                start_kernel, "start", [(nc, raw_rows, 2 * NB), (nr, PACKED, 2 * NB)],
                my_row, matrix[:, : 4 * NB], statics=(chunk,), scalars=1,
            )
            raw_chunk = swap(raw, "col")[0]
            raw_chunk_c = lax.ppermute(raw_chunk, ("row", "col"), to_cols)
            raw_r = call(
                relay_kernel, "relay", [(nc, raw_rows + PACKED, 2 * NB)], raw_chunk, swap(grams, "row")
            )
            raw_r = swap(raw_r, "col")

            root, once_r, smalls = call(
                first_once_kernel, "first_once", [square, tall_r, (nr, few(nr), 2 * NB)],
                my_row, raw_r, statics=(chunk,), scalars=1,
            )

            gathered, image_chunk_r = image_round(
                image_blocks(once_r, smalls), "row", to_rows, (raw_chunk_c,)
            )
            first_c = gathered[:, at : at + chunk, :NB].reshape(tall_c)
            once_c = nt(jnp.where(col_place >= NB, first_c, 0.0), root)
            inners = call(inner_kernel, "inner", [block_r], gathered, once_c, image_chunk_r)
            got = swap(inners, "col")
            small_one, state_c, _ = call(
                first_factor_kernel, "first_factor", [(8,) + square, pair_shape_c],
                my_col, gathered, once_c, statics=(chunk, half, at), scalars=1, flag=True,
            )
            pair_c, panel_c, tops, grams = call(
                first_cols_kernel, "first_cols",
                [pair_shape_c, pair_shape_c, (2,) + square, (nc, PACKED, 2 * NB)],
                my_col, got, small_one, state_c, gathered, statics=(chunk, at), scalars=1,
            )
            grams = swap(grams, "col")
            pair_r, panel_r = call(
                first_rows_kernel, "first_rows", [pair_shape_r, tall_r],
                my_row, got, small_one, once_r, raw_r, tops, statics=(chunk,), scalars=1,
            )

            root, once_r, smalls = call(
                second_once_kernel, "second_once", [square, tall_r, (nr, few(nr), 2 * NB)],
                my_row, grams, raw_r, panel_r, pair_r, statics=(chunk,), scalars=1,
            )
            old = gathered
            gathered, image_chunk_r = image_round(image_blocks(once_r, smalls), "row", to_rows)
            once_c = nt(panel_c[:, :NB], root)
            current = matrix - nt(pair_r, pair_c)
            inners = call(inner_kernel, "inner", [block_r], gathered, once_c, image_chunk_r)
            got = swap(inners, "col")
            right, state_r, vectors, factors = call(
                second_factor_kernel, "second_factor",
                [
                    pair_shape_c, (rows_here + 2 * NB, 2 * NB), (2, NB, rows_here), (2,) + square
                ],
                my_row, my_col, gathered, old, raw_r, panel_c, once_c, once_r, pair_c, pair_r,
                statics=(chunk, half, at), scalars=2, small=True,
            )
            left = call(last_kernel, "last", [pair_shape_r], got, state_r)
            return current, left, right, vectors, factors

        ready, fine = plain()
        current, left, right, vectors, factors = lax.cond(
            fine, lambda *given: given, lambda *_: careful(), *ready
        )
        return current - nt(left, right), vectors.transpose(0, 2, 1), factors

    return jax.shard_map(
        local,
        mesh=mesh,
        in_specs=(P("row", "col"),),
        out_specs=(P("row", "col"), P(None, "row", None), P()),
        check_vma=False,
    )
```

```python
import functools

import jax
import jax.numpy as jnp
from jax import lax
from jax.experimental import pallas as pl
from jax.experimental.pallas import tpu as pltpu
from jax.sharding import PartitionSpec as P

NB = 64
precise = lax.Precision.HIGHEST


def nn(a, b):
    return lax.dot_general(
        a, b, (((1,), (0,)), ((), ())), precision=precise, preferred_element_type=jnp.float32
    )


def tn(a, b):
    return lax.dot_general(
        a, b, (((0,), (0,)), ((), ())), precision=precise, preferred_element_type=jnp.float32
    )


def nt(a, b):
    return lax.dot_general(
        a, b, (((1,), (1,)), ((), ())), precision=precise, preferred_element_type=jnp.float32
    )


def places():
    sub = lax.broadcasted_iota(jnp.int32, (NB, 2 * NB), 0)
    lane = lax.broadcasted_iota(jnp.int32, (NB, 2 * NB), 1)
    return sub, lane


def inverse_root(gram):
    sub, lane = places()
    eye = (sub + NB == lane).astype(jnp.float32)
    work = jnp.concatenate([gram, jnp.zeros_like(gram)], axis=1) + eye
    scales = jnp.zeros((NB, 2 * NB), jnp.float32)
    for step in range(0, NB, 2):
        first = work[step : step + 1]
        second = work[step + 1 : step + 2]
        left = jnp.broadcast_to(work[:, step : step + 1], work.shape)
        right = jnp.broadcast_to(work[:, step + 1 : step + 2], work.shape)
        a, b = left[step : step + 1], right[step : step + 1]
        c, d = left[step + 1 : step + 2], right[step + 1 : step + 2]
        inverse = 1.0 / a
        det = a * d - b * c
        last = a * (1.0 / det)
        second = second - (c * inverse) * first
        scales = jnp.where(sub == step, a, jnp.where(sub == step + 1, det * inverse, scales))
        second_scaled = second * last
        first_scaled = first * inverse - (b * inverse) * second_scaled
        change = left * first_scaled + right * second_scaled
        work = jnp.where(sub > step + 1, work - change, jnp.where(sub == step + 1, second, work))
    return (work * lax.rsqrt(scales))[:, NB:]


def signed_lu(negated_top):
    sub, lane = places()
    eye = (sub + NB == lane).astype(jnp.float32)
    work = jnp.concatenate([negated_top, jnp.zeros_like(negated_top)], axis=1) + eye
    lower = jnp.zeros((NB, 2 * NB), jnp.float32)
    upper = jnp.zeros((NB, 2 * NB), jnp.float32)
    signs = jnp.zeros((1, 2 * NB), jnp.float32)
    lane_row = lax.broadcasted_iota(jnp.int32, (1, 2 * NB), 1)
    for step in range(0, NB, 2):
        left = jnp.broadcast_to(work[:, step : step + 1], work.shape)
        right = jnp.broadcast_to(work[:, step + 1 : step + 2], work.shape)
        raw, b = left[step : step + 1], right[step : step + 1]
        c, d = left[step + 1 : step + 2], right[step + 1 : step + 2]
        flip = jnp.where(raw > 0, 1.0, -1.0)
        a = raw + flip
        raw_det = a * d - b * c
        flip_last = jnp.where(raw_det * flip > 0, 1.0, -1.0)
        det = raw_det + flip_last * a
        inverse = 1.0 / a
        last = a * (1.0 / det)
        signs = jnp.where(lane_row == step, flip, jnp.where(lane_row == step + 1, flip_last, signs))
        first = jnp.where(lane_row == step, a, work[step : step + 1])
        second = work[step + 1 : step + 2] - (c * inverse) * first
        second = jnp.where(lane_row == step + 1, det * inverse, second)
        upper = jnp.where(
            (sub == step) & (lane >= step), first,
            jnp.where((sub == step + 1) & (lane > step), second, upper),
        )
        second_scaled = second * last
        second_scaled = jnp.where(lane_row == step, 0.0, second_scaled)
        ratio = b * inverse
        first_scaled = first * inverse - ratio * second_scaled
        below_first = jnp.where(sub > step, left * inverse, jnp.where(sub == step, 1.0, 0.0))
        below_last = (right - left * ratio) * last
        below_last = jnp.where(sub > step + 1, below_last, jnp.where(sub == step + 1, 1.0, 0.0))
        lower = jnp.where(lane == step, below_first, jnp.where(lane == step + 1, below_last, lower))
        change = left * first_scaled + right * second_scaled
        work = jnp.where(
            sub == step, first_scaled, jnp.where(sub == step + 1, second_scaled, work - change)
        )
    return lower[:, :NB], upper[:, :NB], work[:, NB:], signs[:, :NB]


def near_root(gram):
    sub = lax.broadcasted_iota(jnp.int32, (NB, NB), 0)
    lane = lax.broadcasted_iota(jnp.int32, (NB, NB), 1)
    eye = (sub == lane).astype(jnp.float32)
    off = gram - eye
    first_order = eye - jnp.where(sub > lane, off, jnp.where(sub == lane, 0.5 * off, 0.0))
    close = jnp.sum(off * off) < 2e-8
    return lax.cond(close, lambda: first_order, lambda: inverse_root(gram))


def fold(x, chunk):
    x = x.reshape(-1, chunk, NB)
    return jnp.concatenate([x[:, : chunk // 2], x[:, chunk // 2 :]], axis=2)


def unfold(x):
    return jnp.concatenate([x[:, :, :NB], x[:, :, NB:]], axis=1).reshape(-1, NB)


def pack_symmetric(g):
    h = NB // 2
    rows = []
    for quadrant in (g[:h, :h], g[:h, h:], g[h:, h:]):
        rows.append(jnp.concatenate([quadrant[k : k + 8] for k in range(0, h, 8)], axis=1))
    return jnp.concatenate(rows, axis=0)


def unpack_symmetric(x):
    h = NB // 2
    first, cross, last = [
        jnp.concatenate([x[q : q + 8, k : k + h] for k in range(0, 4 * h, h)], axis=0)
        for q in (0, 8, 16)
    ]
    upper = jnp.concatenate([first, cross], axis=1)
    return jnp.concatenate([upper, jnp.concatenate([cross.T, last], axis=1)], axis=0)


PACKED = 24


def put_pairs(out_ref, pairs, first=0):
    peers, rows = out_ref.shape[:2]
    per = NB // peers
    for q, pair in enumerate(pairs):
        for t in range(per):
            out_ref[:, first + q * per + t, :] = pair[t * peers : (t + 1) * peers]
    for k in range(first + len(pairs) * per, rows):
        out_ref[:, k, :] = jnp.zeros((peers, 2 * NB), jnp.float32)


def get_pairs(ref, first, count):
    per = NB // ref.shape[0]
    pairs = []
    for q in range(count):
        slots = [ref[:, first + q * per + t, :] for t in range(per)]
        pair = jnp.concatenate(slots, axis=0)
        pairs += [pair[:, :NB], pair[:, NB:]]
    return pairs


def beside(*parts):
    return jnp.concatenate(parts, axis=1)


def below(x, index, start):
    place = lax.broadcasted_iota(jnp.int32, x.shape, 0)
    return jnp.where((place >= start) | (index > 0), x, 0.0)


def plain_start_kernel(chunk, matrix_ref, raw_ref):
    raw_ref[:, :chunk, :] = matrix_ref[:, : 2 * NB].reshape(-1, chunk, 2 * NB)
    raw_ref[:, chunk:, :] = fold(matrix_ref[:, 2 * NB : 3 * NB], chunk)


def start_kernel(chunk, index_ref, matrix_ref, raw_ref, out_ref):
    plain_start_kernel(chunk, matrix_ref, raw_ref)
    panel = below(matrix_ref[:, :NB], index_ref[0], NB)
    packed = pack_symmetric(tn(panel, panel))
    out_ref[...] = jnp.broadcast_to(packed[None], out_ref.shape)


def relay_kernel(raw_ref, got_ref, out_ref):
    block = jnp.concatenate([raw_ref[...], jnp.sum(got_ref[...], axis=0)], axis=0)
    out_ref[...] = jnp.broadcast_to(block[None], out_ref.shape)


def pair_raw(raw_ref, chunk, at=0):
    return raw_ref[:, at : at + chunk, :].reshape(-1, 2 * NB)


def last_raw(raw_ref, chunk, at=0):
    return unfold(raw_ref[:, at + chunk : at + chunk + chunk // 2, :])


def first_pairs(chunk, index, raw_ref, root, once_ref, small_ref):
    pair = pair_raw(raw_ref, chunk)
    following = pair[:, NB:]
    once = below(pair[:, :NB], index, NB)
    if root is not None:
        once = nt(once, root)
    once_ref[...] = once
    last = last_raw(raw_ref, chunk)
    gram = tn(once, once)
    image_top = tn(following, once)

    def top(x, k):
        return jnp.where(index == 0, x[k * NB : (k + 1) * NB], 0.0)

    put_pairs(
        small_ref,
        [
            beside(gram, image_top),
            beside(top(once, 1), top(following, 1)),
            beside(top(last, 2), jnp.zeros((NB, NB), jnp.float32)),
        ],
    )


def plain_first_kernel(chunk, index_ref, raw_ref, panel_ref, small_ref):
    first_pairs(chunk, index_ref[0], raw_ref, None, panel_ref, small_ref)


def first_once_kernel(chunk, index_ref, raw_ref, root_ref, once_ref, small_ref):
    root = inverse_root(unpack_symmetric(raw_ref[0, chunk + chunk // 2 :, :]))
    root_ref[...] = root
    first_pairs(chunk, index_ref[0], raw_ref, root, once_ref, small_ref)


def second_pairs(index, once, last, vec, wide, small_ref, first=0):
    def top(x):
        return jnp.where(index == 0, x[2 * NB : 3 * NB], 0.0)

    grams = tn(beside(once, last), once)
    dots = tn(beside(vec, wide), once)
    put_pairs(
        small_ref,
        [
            beside(grams[:NB], grams[NB:]),
            beside(dots[:NB], dots[NB:]),
            beside(top(once), top(vec)),
            beside(top(wide), jnp.zeros((NB, NB), jnp.float32)),
        ],
        first,
    )


def second_once_kernel(
    chunk, index_ref, got_ref, raw_ref, panel_ref, pair_ref, root_ref, once_ref, small_ref
):
    root = inverse_root(unpack_symmetric(jnp.sum(got_ref[...], axis=0)))
    root_ref[...] = root
    once = nt(panel_ref[...], root)
    once_ref[...] = once
    last = last_raw(raw_ref, chunk)
    second_pairs(index_ref[0], once, last, pair_ref[:, :NB], pair_ref[:, NB:], small_ref)


def sum_kernel(got_ref, out_ref, chunk_ref):
    summed = jnp.sum(got_ref[...], axis=0)
    out_ref[...] = jnp.broadcast_to(summed[None], out_ref.shape)
    chunk_ref[...] = summed[: chunk_ref.shape[0]]


def sum_with_kernel(got_ref, raw_ref, out_ref, chunk_ref):
    summed = jnp.sum(got_ref[...], axis=0)
    block = jnp.concatenate([summed, raw_ref[...]], axis=0)
    out_ref[...] = jnp.broadcast_to(block[None], out_ref.shape)
    chunk_ref[...] = summed[: chunk_ref.shape[0]]


def inner_kernel(gathered_ref, once_ref, chunk_ref, out_ref):
    half = chunk_ref.shape[0]
    inner = tn(once_ref[...], unfold(gathered_ref[:, :half, :]))
    block = jnp.concatenate([pack_symmetric(inner), chunk_ref[...]], axis=0)
    out_ref[...] = jnp.broadcast_to(block[None], out_ref.shape)


def plain_inner_kernel(chunk, at, col_ref, gathered_ref, chunk_ref, out_ref):
    half = chunk_ref.shape[0]
    panel = below(pair_raw(gathered_ref, chunk, at)[:, :NB], col_ref[0], NB)
    inner = tn(panel, unfold(gathered_ref[:, :half, :]))
    block = jnp.concatenate([pack_symmetric(inner), chunk_ref[...]], axis=0)
    out_ref[...] = jnp.broadcast_to(block[None], out_ref.shape)


PICK, COEF, PICK_T, COEF_T, LOWER, FACTOR, INNER, WIDE = range(8)


def factor_small(near, gram, top, next_top, image_top, small_ref):
    root = near_root(gram) if near else inverse_root(gram)
    lower, upper, inverse, signs = signed_lu(-nt(top, root))
    sub = lax.broadcasted_iota(jnp.int32, (NB, NB), 0)
    lane = lax.broadcasted_iota(jnp.int32, (NB, NB), 1)
    triangle = lane >= sub
    upper_inverse = jnp.where(triangle, nn(inverse, lower), 0.0)
    lower_inverse = nn(upper, inverse)
    factor = jnp.where(triangle, nt(upper * signs, lower_inverse), 0.0)
    pick = nn(jnp.where(sub == lane, signs, 0.0), upper_inverse)
    coef = tn(root, upper_inverse)
    crossed = tn(pick, nn(image_top, coef))
    pick_t = nn(pick, factor)
    coef_t = nn(coef, factor)
    small_ref[PICK] = pick
    small_ref[COEF] = coef
    small_ref[PICK_T] = pick_t
    small_ref[COEF_T] = coef_t
    small_ref[LOWER] = lower
    small_ref[FACTOR] = factor
    small_ref[INNER] = tn(pick, nn(next_top, pick)) - crossed - crossed.T
    small_ref[WIDE] = nn(next_top, pick_t) - nn(image_top, coef_t)
    sizes = jnp.sum(jnp.where(sub == lane, gram, 0.0), axis=0, keepdims=True)
    fine = jnp.sum(root * root * sizes) < 1.5 * NB
    return pick, coef, pick_t, coef_t, fine


def vectors_of(once, index, start, pick, coef):
    vec = -nn(once, coef)
    top = vec[start : start + NB] + jnp.where(index == 0, pick, 0.0)
    return jnp.concatenate([vec[:start], top, vec[start + NB :]], axis=0)


def half_core(coef, factor, known, got):
    inner = known + tn(coef, nn(got, coef))
    return 0.5 * tn(factor, nn(inner, factor))


def first_factor(near, chunk, half, at, col, gathered_ref, once_c, outs):
    small_ref, state_ref, fine_ref = outs
    gram, image_top, top, next_top, _, _ = get_pairs(gathered_ref, half, 3)
    pick, coef, pick_t, coef_t, fine = factor_small(
        near, gram, top, next_top, image_top, small_ref
    )
    fine_ref[0] = jnp.where(fine, 1, 0)
    following = pair_raw(gathered_ref, chunk, at)[:, NB:]
    image = unfold(gathered_ref[:, :half, :])
    vec = vectors_of(once_c, col, NB, pick, coef)
    state_ref[...] = beside(vec, nn(following, pick_t) - nn(image, coef_t))


def first_factor_kernel(chunk, half, at, col_ref, gathered_ref, once_c_ref, *outs):
    first_factor(True, chunk, half, at, col_ref[0], gathered_ref, once_c_ref[...], outs)


def plain_factor_kernel(chunk, half, at, col_ref, gathered_ref, *outs):
    panel = below(pair_raw(gathered_ref, chunk, at)[:, :NB], col_ref[0], NB)
    first_factor(False, chunk, half, at, col_ref[0], gathered_ref, panel, outs)


def second_panel(following, pair, tops, index):
    return below(following - nt(pair, tops), index, 2 * NB)


def first_cols(
    chunk, at, index, got_ref, small_ref, state_ref, raw_ref, pair_ref, panel_ref, tops_ref
):
    got = unpack_symmetric(jnp.sum(got_ref[:, :PACKED, :], axis=0))
    half = half_core(small_ref[COEF], small_ref[FACTOR], small_ref[INNER], got)
    lower = small_ref[LOWER]
    wide_top = small_ref[WIDE] - nn(lower, half)
    tops_ref[0] = half
    tops_ref[1] = wide_top
    vec = state_ref[:, :NB]
    wide = state_ref[:, NB:] - nn(vec, half)
    pair = beside(wide, vec)
    pair_ref[...] = pair
    following = pair_raw(raw_ref, chunk, at)[:, NB:]
    panel = second_panel(following, pair, beside(lower, wide_top), index)
    spare = jnp.zeros((panel.shape[0] - NB, NB), jnp.float32)
    panel_ref[...] = beside(panel, jnp.concatenate([small_ref[FACTOR], spare], axis=0))
    return panel, vec, wide


def first_cols_kernel(
    chunk, at, col_ref, got_ref, small_ref, state_ref, raw_ref,
    pair_ref, panel_ref, tops_ref, out_ref,
):
    panel, _, _ = first_cols(
        chunk, at, col_ref[0], got_ref, small_ref, state_ref, raw_ref,
        pair_ref, panel_ref, tops_ref,
    )
    packed = pack_symmetric(tn(panel, panel))
    out_ref[...] = jnp.broadcast_to(packed[None], out_ref.shape)


def plain_cols_kernel(
    chunk, at, col_ref, got_ref, small_ref, state_ref, raw_ref, matrix_ref,
    pair_ref, panel_ref, tops_ref, out_ref,
):
    panel, vec, wide = first_cols(
        chunk, at, col_ref[0], got_ref, small_ref, state_ref, raw_ref,
        pair_ref, panel_ref, tops_ref,
    )
    half = chunk // 2
    out_ref[:, :half, :] = fold(nn(matrix_ref[...], panel), chunk)
    last = last_raw(raw_ref, chunk, at)
    second_pairs(col_ref[0], panel, last, vec, wide, out_ref, half)


def first_rows_kernel(
    chunk, row_ref, got_ref, small_ref, once_ref, raw_ref, tops_ref, pair_ref, panel_ref
):
    image = unfold(got_ref[:, PACKED:, :])
    following = pair_raw(raw_ref, chunk)[:, NB:]
    vec = vectors_of(once_ref[...], row_ref[0], NB, small_ref[PICK], small_ref[COEF])
    wide = nn(following, small_ref[PICK_T]) - nn(image, small_ref[COEF_T]) - nn(vec, tops_ref[0])
    pair = beside(vec, wide)
    pair_ref[...] = pair
    tops = beside(tops_ref[1], small_ref[LOWER])
    panel_ref[...] = second_panel(following, pair, tops, row_ref[0])


def second_small(near, half, gathered_ref, old_ref, panel_ref, small_ref, factors_ref):
    gram, image_top, vec_dot, wide_dot, top, vec_top, wide_top, _ = get_pairs(
        gathered_ref, half, 4
    )
    last_top = get_pairs(old_ref, half, 3)[4]
    image_top = image_top - nn(vec_top, wide_dot) - nn(wide_top, vec_dot)
    crossed = nt(vec_top, wide_top)
    next_top = last_top - crossed - crossed.T
    pick, coef, pick_t, coef_t, fine = factor_small(
        near, gram, top, next_top, image_top, small_ref
    )
    crossed = tn(nn(vec_dot, coef), nn(wide_dot, coef))
    small_ref[INNER] -= crossed + crossed.T
    factors_ref[0] = panel_ref[:NB, NB:]
    factors_ref[1] = small_ref[FACTOR]
    vec_dots = nn(wide_dot, coef_t) - tn(wide_top, pick_t)
    wide_dots = nn(vec_dot, coef_t) - tn(vec_top, pick_t)
    return pick, coef, pick_t, coef_t, vec_dots, wide_dots, fine


def second_factor_kernel(
    chunk, half, at, row_ref, col_ref, gathered_ref, old_ref, raw_r_ref,
    panel_c_ref, once_c_ref, once_r_ref, pair_c_ref, pair_r_ref,
    right_ref, state_ref, vectors_ref, factors_ref, small_ref,
):
    pick, coef, pick_t, coef_t, vec_dots, wide_dots, _ = second_small(
        True, half, gathered_ref, old_ref, panel_c_ref, small_ref, factors_ref
    )
    new = vectors_of(once_r_ref[...], row_ref[0], 2 * NB, pick, coef)
    vec = pair_r_ref[:, :NB]
    vectors_ref[0] = vec.T
    vectors_ref[1] = new.T
    part = nn(last_raw(raw_r_ref, chunk), pick_t)
    part += nn(vec, vec_dots) + nn(pair_r_ref[:, NB:], wide_dots)
    state_ref[...] = with_smalls(beside(new, part), small_ref)
    new = vectors_of(once_c_ref[...], col_ref[0], 2 * NB, pick, coef)
    part = nn(last_raw(old_ref, chunk, at), pick_t) - nn(unfold(gathered_ref[:, :half, :]), coef_t)
    part += nn(pair_c_ref[:, NB:], vec_dots) + nn(pair_c_ref[:, :NB], wide_dots)
    right_ref[...] = beside(part, new)


def plain_second_kernel(
    chunk, half, at, row_ref, col_ref, gathered_ref, old_ref, raw_r_ref,
    panel_c_ref, panel_r_ref, pair_c_ref, pair_r_ref,
    state_ref, left_ref, vectors_ref, factors_ref, fine_ref, small_ref,
):
    pick, coef, pick_t, coef_t, vec_dots, wide_dots, fine = second_small(
        False, half, gathered_ref, old_ref, panel_c_ref, small_ref, factors_ref
    )
    fine_ref[0] = jnp.where(fine, 1, 0)
    new = vectors_of(panel_r_ref[...], row_ref[0], 2 * NB, pick, coef)
    vec = pair_r_ref[:, :NB]
    vectors_ref[0] = vec.T
    vectors_ref[1] = new.T
    part = nn(last_raw(raw_r_ref, chunk), pick_t) - nn(unfold(gathered_ref[:, :half, :]), coef_t)
    part += nn(vec, vec_dots) + nn(pair_r_ref[:, NB:], wide_dots)
    left_ref[...] = beside(part, new)
    new = vectors_of(panel_c_ref[:, :NB], col_ref[0], 2 * NB, pick, coef)
    part = nn(last_raw(old_ref, chunk, at), pick_t)
    part += nn(pair_c_ref[:, NB:], vec_dots) + nn(pair_c_ref[:, :NB], wide_dots)
    state_ref[...] = with_smalls(beside(new, part), small_ref)


def with_smalls(state, small_ref):
    upper = beside(small_ref[COEF], small_ref[FACTOR])
    lower = beside(small_ref[INNER], small_ref[COEF_T])
    return jnp.concatenate([state, upper, lower], axis=0)


def last_kernel(got_ref, state_ref, out_ref):
    tall = out_ref.shape[0]
    coef, factor = state_ref[tall : tall + NB, :NB], state_ref[tall : tall + NB, NB:]
    inner, coef_t = state_ref[tall + NB :, :NB], state_ref[tall + NB :, NB:]
    got = unpack_symmetric(jnp.sum(got_ref[:, :PACKED, :], axis=0))
    half = half_core(coef, factor, inner, got)
    new = state_ref[:tall, :NB]
    image = unfold(got_ref[:, PACKED:, :])
    wide = state_ref[:tall, NB:] - nn(image, coef_t) - nn(new, half + half.T)
    out_ref[...] = beside(new, wide)


def call(kernel, name, outs, *args, statics=(), scalars=0, flag=False, small=False):
    in_smem = pl.BlockSpec(memory_space=pltpu.SMEM)
    in_vmem = pl.BlockSpec(memory_space=pltpu.VMEM)
    out_shape = [jax.ShapeDtypeStruct(shape, jnp.float32) for shape in outs]
    out_specs = [in_vmem] * len(outs)
    if flag:
        out_shape.append(jax.ShapeDtypeStruct((1,), jnp.int32))
        out_specs.append(in_smem)
    result = pl.pallas_call(
        functools.partial(kernel, *statics),
        out_shape=out_shape,
        in_specs=[in_smem if k < scalars else in_vmem for k in range(len(args))],
        out_specs=out_specs,
        compiler_params=pltpu.CompilerParams(vmem_limit_bytes=16 << 20),
        scratch_shapes=[pltpu.VMEM((8, NB, NB), jnp.float32)] if small else [],
        cost_estimate=pl.CostEstimate(flops=1 << 24, bytes_accessed=1 << 22, transcendentals=0),
        name=name,
    )(*args)
    return result[0] if len(result) == 1 else result


def swap(x, axis):
    return lax.all_to_all(x, axis, 0, 0)


def solution(mesh):
    nr = mesh.shape["row"]
    nc = mesh.shape["col"]

    def local(matrix):
        rows_here, cols_here = matrix.shape
        chunk = rows_here // nc
        half = chunk // 2
        my_row = lax.axis_index("row").astype(jnp.int32).reshape(1)
        my_col = lax.axis_index("col").astype(jnp.int32).reshape(1)
        col_place = (lax.axis_index("col") * cols_here + jnp.arange(cols_here))[:, None]
        to_rows = []
        for r in range(nr):
            for c in range(nc):
                first = r * rows_here + c * chunk
                source = (first % cols_here // chunk) * nc + first // cols_here
                to_rows.append((source, r * nc + c))
        to_cols = [(b, a) for a, b in to_rows]
        square = (NB, NB)
        tall_r = (rows_here, NB)
        tall_c = (cols_here, NB)
        pair_shape_c = (cols_here, 2 * NB)
        pair_shape_r = (rows_here, 2 * NB)
        raw_rows = chunk + half

        def few(peers):
            return -(-4 * (NB // peers) // 8) * 8

        def image_round(mine, axis, targets, extra=(), beside=()):
            got, *beside = lax.optimization_barrier((swap(mine, axis), *beside))
            rows = got.shape[1] + sum(x.shape[0] for x in extra)
            blocks, image_chunk = call(
                sum_with_kernel if extra else sum_kernel, "sum_blocks",
                [(got.shape[0], rows, 2 * NB), (half, 2 * NB)], got, *extra,
            )
            return swap(blocks, axis), lax.ppermute(image_chunk, ("row", "col"), targets), *beside

        def image_blocks(once_r, smalls):
            return jnp.concatenate([fold(tn(matrix, once_r), chunk), smalls], axis=1)

        at = half + few(nr)

        block_r = (nc, PACKED + half, 2 * NB)
        block_c = (nr, PACKED + half, 2 * NB)

        def plain():
            raw = pl.pallas_call(
                functools.partial(plain_start_kernel, chunk),
                grid=(1,),
                in_specs=[pl.BlockSpec((rows_here, 4 * NB), lambda _: (0, 0))],
                out_specs=pl.BlockSpec((nc, raw_rows, 2 * NB), lambda _: (0, 0, 0)),
                out_shape=jax.ShapeDtypeStruct((nc, raw_rows, 2 * NB), jnp.float32),
                name="plain_start",
            )(matrix)
            raw_chunk = swap(raw, "col")[0]
            raw_chunk_c = lax.ppermute(raw_chunk, ("row", "col"), to_cols)
            raw_r = swap(jnp.broadcast_to(raw_chunk[None], raw.shape), "col")
            first_r, smalls = call(
                plain_first_kernel, "plain_first", [tall_r, (nr, few(nr), 2 * NB)],
                my_row, raw_r, statics=(chunk,), scalars=1,
            )
            gathered, image_chunk = image_round(
                image_blocks(first_r, smalls), "row", to_rows, (raw_chunk_c,)
            )
            inners = call(
                plain_inner_kernel, "plain_inner", [block_r],
                my_col, gathered, image_chunk, statics=(chunk, at), scalars=1,
            )
            got = swap(inners, "col")
            small_one, state_c, fine_one = call(
                plain_factor_kernel, "plain_factor", [(8,) + square, pair_shape_c],
                my_col, gathered, statics=(chunk, half, at), scalars=1, flag=True,
            )
            pair_c, panel_c, tops, blocks = call(
                plain_cols_kernel, "plain_cols",
                [pair_shape_c, pair_shape_c, (2,) + square, (nc, half + few(nc), 2 * NB)],
                my_col, got, small_one, state_c, gathered, matrix, statics=(chunk, at), scalars=1,
            )
            pair_r, panel_r = call(
                first_rows_kernel, "first_rows", [pair_shape_r, tall_r],
                my_row, got, small_one, first_r, raw_r, tops, statics=(chunk,), scalars=1,
            )
            current = matrix - nt(pair_r, pair_c)
            old = gathered
            gathered, image_chunk, current, pair_r, panel_r = image_round(
                blocks, "col", to_cols, beside=(current, pair_r, panel_r)
            )
            inners = call(
                inner_kernel, "inner", [block_c], gathered, panel_r, image_chunk
            )
            got = swap(inners, "row")
            state_c, left, vectors, factors, fine_two = call(
                plain_second_kernel, "plain_second",
                [
                    (cols_here + 2 * NB, 2 * NB), pair_shape_r, (2, NB, rows_here), (2,) + square
                ],
                my_row, my_col, gathered, old, raw_r, panel_c, panel_r,
                pair_c, pair_r, statics=(chunk, half, at), scalars=2, flag=True,
                small=True,
            )
            right = call(
                last_kernel, "last", [pair_shape_c], got, state_c
            )
            return (current, left, right, vectors, factors), (fine_one + fine_two)[0] == 2

        def careful():
            raw, grams = call(
                start_kernel, "start", [(nc, raw_rows, 2 * NB), (nr, PACKED, 2 * NB)],
                my_row, matrix[:, : 4 * NB], statics=(chunk,), scalars=1,
            )
            raw_chunk = swap(raw, "col")[0]
            raw_chunk_c = lax.ppermute(raw_chunk, ("row", "col"), to_cols)
            raw_r = call(
                relay_kernel, "relay", [(nc, raw_rows + PACKED, 2 * NB)], raw_chunk, swap(grams, "row")
            )
            raw_r = swap(raw_r, "col")

            root, once_r, smalls = call(
                first_once_kernel, "first_once", [square, tall_r, (nr, few(nr), 2 * NB)],
                my_row, raw_r, statics=(chunk,), scalars=1,
            )

            gathered, image_chunk_r = image_round(
                image_blocks(once_r, smalls), "row", to_rows, (raw_chunk_c,)
            )
            first_c = gathered[:, at : at + chunk, :NB].reshape(tall_c)
            once_c = nt(jnp.where(col_place >= NB, first_c, 0.0), root)
            inners = call(inner_kernel, "inner", [block_r], gathered, once_c, image_chunk_r)
            got = swap(inners, "col")
            small_one, state_c, _ = call(
                first_factor_kernel, "first_factor", [(8,) + square, pair_shape_c],
                my_col, gathered, once_c, statics=(chunk, half, at), scalars=1, flag=True,
            )
            pair_c, panel_c, tops, grams = call(
                first_cols_kernel, "first_cols",
                [pair_shape_c, pair_shape_c, (2,) + square, (nc, PACKED, 2 * NB)],
                my_col, got, small_one, state_c, gathered, statics=(chunk, at), scalars=1,
            )
            grams = swap(grams, "col")
            pair_r, panel_r = call(
                first_rows_kernel, "first_rows", [pair_shape_r, tall_r],
                my_row, got, small_one, once_r, raw_r, tops, statics=(chunk,), scalars=1,
            )

            root, once_r, smalls = call(
                second_once_kernel, "second_once", [square, tall_r, (nr, few(nr), 2 * NB)],
                my_row, grams, raw_r, panel_r, pair_r, statics=(chunk,), scalars=1,
            )
            old = gathered
            gathered, image_chunk_r = image_round(image_blocks(once_r, smalls), "row", to_rows)
            once_c = nt(panel_c[:, :NB], root)
            current = matrix - nt(pair_r, pair_c)
            inners = call(inner_kernel, "inner", [block_r], gathered, once_c, image_chunk_r)
            got = swap(inners, "col")
            right, state_r, vectors, factors = call(
                second_factor_kernel, "second_factor",
                [
                    pair_shape_c, (rows_here + 2 * NB, 2 * NB), (2, NB, rows_here), (2,) + square
                ],
                my_row, my_col, gathered, old, raw_r, panel_c, once_c, once_r, pair_c, pair_r,
                statics=(chunk, half, at), scalars=2, small=True,
            )
            left = call(last_kernel, "last", [pair_shape_r], got, state_r)
            return current, left, right, vectors, factors

        ready, fine = plain()
        current, left, right, vectors, factors = lax.cond(
            fine, lambda *given: given, lambda *_: careful(), *ready
        )
        change = lax.dot_general(
            left, right, (((1,), (1,)), ((), ())),
            precision=lax.Precision.HIGH, preferred_element_type=jnp.float32,
        )
        return current - change, vectors.transpose(0, 2, 1), factors

    return jax.shard_map(
        local,
        mesh=mesh,
        in_specs=(P("row", "col"),),
        out_specs=(P("row", "col"), P(None, "row", None), P()),
        check_vma=False,
    )
```
